256 devices in a mesh: stream: 8 (over x_lo, y), wall: 32 (over x_hi, z, core).
Axes of the slice: x: 4 (x_hi: 2, x_lo: 2; x = x_hi * 2 + x_lo), y: 4, z: 8, core: 2. Of those that a mesh axis runs over, the one named last changes fastest.
Arguments:
- right_side: float32 [2048, 24576], P('stream', 'wall'), may hold values from -6 to 6
- diagonal: float32 [2048, 24576], P('stream', 'wall'), may hold values from 0.05 to 1
- coarse_inverse: float32 [4096, 4096], P('wall', 'stream'), may hold values from -1 to 2
- owner_slot: int32 [256], replicated, may hold values from 0 to 255, each once
Outputs:
- pressure_update: float32 [2048, 24576], P('stream', 'wall')
- residual_field: float32 [2048, 24576], P('stream', 'wall')
The draws below stay inside these ranges and needn't reach their ends.
All inputs are finite; a program needn't handle non-finite values.
Results may differ from the reference program's by a relative error of at most 0.0003.
Values sent between devices are 32-bit elements; how exact they have to be, the bound alone decides.
A program may use at most 64 MiB of HBM per device.

```python
import math
import jax
import jax.numpy as jnp
from jax import lax

CX = 256
CY = 768
MARGIN = 4
DEG = 4
MODES_X = 4
MODES_Y = 4
NX = 2048
NY = 24576
SUBDOMAINS = 256
NC = 4096
N_STREAM = 8
N_WALL = 32


def draw_right_side(key, part):
    key = jax.random.fold_in(key, 11)
    values = jnp.clip(jax.random.normal(key, (NX, NY), jnp.float32), -6.0, 6.0)
    return values


def draw_coarse_inverse(key, part):
    key = jax.random.fold_in(key, 23)
    first_key, second_key = jax.random.split(key)
    leading = jax.random.uniform(first_key, (NC,), jnp.float32, 1.0, 2.0)
    spread_part = jnp.clip(jax.random.normal(second_key, (NC, NC), jnp.float32), -4.0, 4.0)
    spread_part = spread_part * (0.5 / jnp.sqrt(jnp.float32(NC)))
    positions = jnp.arange(NC, dtype=jnp.int32)
    return jnp.where(positions[:, None] == positions[None, :], leading[:, None], spread_part)


def block_levels(own_key, shape, cuts, low, high):
    def one(dim, shards_of):
        steps = jax.random.uniform(jax.random.fold_in(jax.random.fold_in(own_key, 6), dim), (shards_of,), jnp.float32, low / len(cuts), high / len(cuts))
        return jnp.repeat(jnp.exp(steps), shape[dim] // shards_of).reshape((-1,) + (1,) * (len(shape) - dim - 1))

    loudness = one(*cuts[0])
    for cut in cuts[1:]:
        loudness = loudness * one(*cut)
    return loudness


def setup_inputs(seed: int = 0) -> dict:
    arg_keys = jax.random.split(jax.random.key(seed), 5)
    right_side = draw_right_side(jax.random.fold_in(arg_keys[4], 71), 0)
    diagonal = jnp.clip(jnp.exp(math.log(1.0) - 2.9957323 * jax.random.uniform(arg_keys[1], (NX, NY), jnp.float32) ** block_levels(arg_keys[1], (NX, NY), ((0, 8), (1, 32)), -0.2, 0.2)), 0.05, 1.0)
    coarse_inverse = draw_coarse_inverse(jax.random.fold_in(arg_keys[4], 71), 0)
    owner_slot = jax.random.permutation(arg_keys[3], SUBDOMAINS).astype(jnp.int32)
    return {"right_side": right_side, "diagonal": diagonal, "coarse_inverse": coarse_inverse, "owner_slot": owner_slot}


lower_end = 0.05
upper_end = 5.0
centre_weight = 8.0 / 3.0
side_weight = 1.0 / 3.0
precise = lax.Precision.HIGHEST

def stencil(padded, shift):
    centre = padded[1:-1, 1:-1]
    beside_all = padded[:-2, :-2] + padded[:-2, 1:-1] + padded[:-2, 2:] + padded[1:-1, :-2]
    beside_all = beside_all + padded[1:-1, 2:] + padded[2:, :-2] + padded[2:, 1:-1] + padded[2:, 2:]
    return (centre_weight + shift) * centre - side_weight * beside_all

def chebyshev(source, shift, inside):
    middle = (upper_end + lower_end) / 2.0
    spread = (upper_end - lower_end) / 2.0
    quotient = middle / spread
    factor = 1.0 / quotient
    update = inside * source / middle
    estimate = update
    for sweep in range(DEG):
        defect = source - stencil(jnp.pad(estimate, 1), shift)
        factor_next = 1.0 / (2.0 * quotient - factor)
        update = inside * (factor_next * factor * update + 2.0 * factor_next / spread * defect)
        estimate = estimate + update
        factor = factor_next
    return estimate

def cosine_table(length, modes):
    position = jnp.arange(length, dtype=jnp.float32) + 0.5
    frequency = jnp.arange(modes, dtype=jnp.float32)
    return jnp.cos(jnp.pi * position[:, None] * frequency[None, :] / length)

def restrict(region, stream_table, wall_table):
    partial_product = jnp.dot(region, wall_table, precision=precise)
    scale = 1.0 / math.sqrt(stream_table.shape[0] * wall_table.shape[0])
    return jnp.dot(stream_table.T, partial_product, precision=precise) * scale

def prolong(coefficients, stream_table, wall_table):
    return jnp.dot(jnp.dot(stream_table, coefficients, precision=precise), wall_table.T, precision=precise)

def precondition(source, shift, coarse_inverse, owner_slot):
    subdomains = N_STREAM * N_WALL
    mode_count = MODES_X * MODES_Y
    wrapped = jnp.concatenate([source[-MARGIN:], source, source[:MARGIN]], 0)
    padded = jnp.pad(wrapped, ((0, 0), (MARGIN, MARGIN)))
    shift_wrapped = jnp.concatenate([shift[-MARGIN:], shift, shift[:MARGIN]], 0)
    shift_padded = jnp.pad(shift_wrapped, ((0, 0), (MARGIN, MARGIN)))
    stream_table = cosine_table(CX, MODES_X)
    wall_table = cosine_table(CY, MODES_Y)

    def local(subdomain):
        stream_at = subdomain // N_WALL
        wall_at = subdomain % N_WALL
        start = (stream_at * CX, wall_at * CY)
        size = (CX + 2 * MARGIN, CY + 2 * MARGIN)
        source_wide = lax.dynamic_slice(padded, start, size)
        shift_wide = lax.dynamic_slice(shift_padded, start, size)
        columns = wall_at * CY - MARGIN + jnp.arange(CY + 2 * MARGIN, dtype=jnp.int32)
        inside = ((columns >= 0) & (columns < CY * N_WALL)).astype(jnp.float32)[None, :]
        solved = chebyshev(source_wide, shift_wide, inside)
        owned = solved[MARGIN:MARGIN + CX, MARGIN:MARGIN + CY]
        coefficients = restrict(source_wide[MARGIN:MARGIN + CX, MARGIN:MARGIN + CY], stream_table, wall_table)
        return (owned, coefficients.reshape(mode_count))
    owned_all, coefficients_all = lax.map(local, jnp.arange(subdomains, dtype=jnp.int32))
    ordered = jnp.zeros((subdomains, mode_count), jnp.float32).at[owner_slot].set(coefficients_all)
    values = jnp.dot(coarse_inverse, ordered.reshape(subdomains * mode_count), precision=precise)
    values = values.reshape(subdomains, mode_count)[owner_slot]

    def lift(couple):
        owned, coarse_part = couple
        return owned + prolong(coarse_part.reshape(MODES_X, MODES_Y), stream_table, wall_table)
    summed = lax.map(lift, (owned_all, values))
    summed = summed.reshape(N_STREAM, N_WALL, CX, CY).transpose(0, 2, 1, 3)
    return summed.reshape(CX * N_STREAM, CY * N_WALL)

def global_apply(source, shift):
    wrapped = jnp.concatenate([source[-1:], source, source[:1]], 0)
    return stencil(jnp.pad(wrapped, ((0, 0), (1, 1))), shift)

def reference(right_side, diagonal, coarse_inverse, owner_slot):
    initial = precondition(right_side, diagonal, coarse_inverse, owner_slot)
    residual_field = right_side - global_apply(initial, diagonal)
    second = precondition(residual_field, diagonal, coarse_inverse, owner_slot)
    return (initial + second, residual_field)
```

```python
import math

import jax
import jax.numpy as jnp
import numpy as np
from jax import lax
from jax.experimental import pallas as pl
from jax.experimental.pallas import tpu as pltpu
from jax.sharding import PartitionSpec as P

MESH = pl.DeviceIdType.MESH
NS, NW = 8, 32
DEVICES = NS * NW
CX, CY = 256, 768
DEG = 4
ROWS, COLS = CX + 16, CY + 128
STRIPS = ROWS // 8
MIDDLE = (5.0 + 0.05) / 2.0
SPREAD = (5.0 - 0.05) / 2.0
SCALE = 1.0 / math.sqrt(CX * CY)
F32, BF16 = jnp.float32, jnp.bfloat16


def sweep_factors():
    quotient = MIDDLE / SPREAD
    factor = 1.0 / quotient
    pairs = []
    for _ in range(DEG):
        following = 1.0 / (2.0 * quotient - factor)
        pairs.append((following * factor, 2.0 * following / SPREAD))
        factor = following
    return pairs


def halves(table):
    high = table.astype(BF16)
    return high, (table - high.astype(np.float32)).astype(BF16)


def tables():
    phi = np.cos(np.pi * (np.arange(CX) + 0.5)[None, :] * np.arange(4)[:, None] / CX)
    psi = np.cos(np.pi * (np.arange(CY) + 0.5)[None, :] * np.arange(4)[:, None] / CY)
    phi_lanes = np.repeat(phi[1:].reshape(3 * CX, 1), 128, axis=1).astype(np.float32)
    psi_rows = np.concatenate([psi, psi]).astype(np.float32)
    stream = np.zeros((ROWS, 32), np.float32)
    stream[0:8, 0:4] = phi[:, CX - 8 :].T
    stream[8 : 8 + CX, 8:12] = phi.T
    stream[8 + CX :, 16:20] = phi[:, :8].T
    high, low = halves(stream)
    stream_k = np.concatenate([high, high, low, np.zeros_like(high)], axis=1)
    own_k = stream_k[8 : 8 + CX]
    wall = np.zeros((64, COLS), np.float32)
    for m in range(4):
        wall[4 * m : 4 * m + 4, COLS - 64 :] = psi[:, CY - 64 :]
        wall[16 + 4 * m : 20 + 4 * m, :CY] = psi
        wall[32 + 4 * m : 36 + 4 * m, CY : CY + 64] = psi[:, :64]
    high, low = halves(wall)
    wall_k = np.concatenate([high, high, low, np.zeros_like(high)], axis=0)
    return phi_lanes, psi_rows, stream_k, own_k, wall_k


def iota(shape, dim):
    return lax.broadcasted_iota(jnp.int32, shape, dim)


def split(value):
    high = value.astype(BF16).astype(F32)
    return high, value - high


def lane_totals(value):
    high, low = split(value)
    both = jnp.concatenate([high, low], axis=1).astype(BF16)
    return jnp.dot(both, jnp.ones((256, 128), BF16), preferred_element_type=F32)


def strip(i):
    return pl.ds(pl.multiple_of(i * 8, 8), 8)


def kernel(
    rhs_hbm, diag_hbm, inv_hbm, slot_hbm, slots_hbm, phi_hbm, psi_hbm, sk_hbm, so_hbm, wk_hbm,
    out_hbm, resid_hbm,
    ext, gm, d3, x, u, first, res, py, inv, phi, psi, sk, so, wk, slots,
    colsend, colrecv, corners, hcolsend, hcolrecv, hcorners, hrows,
    rows, bufs, ypk, slot,
    load_sem, msend, mrecv, asend, arecv, store_sem,
):
    s = lax.axis_index("stream")
    w = lax.axis_index("wall")
    me = s * NW + w
    ya, xl = s % 4, s // 4
    xh, za, core = w // 16, (w // 2) % 8, w % 2
    xa = xh * 2 + xl
    up, down = (s + NS - 1) % NS, (s + 1) % NS
    left, right = (w + NW - 1) % NW, (w + 1) % NW

    def around(k, n):
        return n // 2 + (k % 2) * ((k + 1) // 2) - (1 - k % 2) * (k // 2)

    def everyone(act):
        ys = [(ya + d) % 4 for d in (2, 3, 1, 0)]

        def some(k, count):
            z = (za + around(k // 4, 8)) % 8
            xx = (xa + around(k % 4, 4)) % 4
            base_s = (xx % 2) * 4
            base_w = (xx // 2) * 16 + z * 2
            for j in range(count):
                act((base_s + ys[j // 2], base_w + ((1 - core) if j % 2 == 0 else core)))

        def body(k, carry):
            some(k, 8)
            return carry

        lax.fori_loop(0, 31, body, 0)
        some(jnp.int32(31), 7)

    barrier = pltpu.get_barrier_semaphore()
    everyone(lambda to: pl.semaphore_signal(barrier, inc=1, device_id=to, device_id_type=MESH))

    own = ext.at[:, pl.ds(8, CX), pl.ds(0, CY)]
    loads = [
        pltpu.make_async_copy(src, dst, load_sem.at[i])
        for i, (src, dst) in enumerate(
            [
                (rhs_hbm, own.at[0]),
                (phi_hbm, phi),
                (psi_hbm, psi),
                (diag_hbm, own.at[1]),
                (slot_hbm, slot),
                (slots_hbm, slots),
                (inv_hbm, inv),
                (sk_hbm, sk),
                (so_hbm, so),
                (wk_hbm, wk),
            ]
        )
    ]
    for load in loads:
        load.start()

    lane = iota((8, 128), 1)
    sub = iota((8, 128), 0)
    lane16 = iota((16, 128), 1)

    def restrict(ref):
        def body(i, sums):
            f = ref[strip(i + 1), 0:CY]
            new = [sums[0] + f]
            for m in range(3):
                t = phi[pl.ds(pl.multiple_of(m * CX + i * 8, 8), 8), :]
                new.append(sums[m + 1] + f * jnp.concatenate([t] * 6, axis=1))
            return tuple(new)

        zero = jnp.zeros((8, CY), F32)
        sums = lax.fori_loop(0, CX // 8, body, (zero,) * 4)
        parts = []
        for m in range(4):
            for n in range(4):
                value = sums[m] if n == 0 else sums[m] * psi[n : n + 1, :]
                total = value[:, 0:128]
                for t in range(1, 6):
                    total = total + value[:, 128 * t : 128 * t + 128]
                parts.append(total)
        totals = lane_totals(jnp.concatenate(parts, axis=0))
        keep = iota((128, 128), 0) // 8 == iota((128, 128), 1) % 16
        return jnp.sum(jnp.where(keep, totals, 0.0), axis=0, keepdims=True) * SCALE

    def pack(ref):
        to_left = jnp.zeros((16, 128), F32)
        to_right = jnp.zeros((16, 128), F32)
        for k in range(16):
            a = jnp.where(lane16 < 8, ref[8 + 16 * k : 24 + 16 * k, 0:128], 0.0)
            b = jnp.where(lane16 >= 120, ref[8 + 16 * k : 24 + 16 * k, CY - 128 : CY], 0.0)
            to_left = to_left + (pltpu.roll(a, 8 * k, 1) if k else a)
            shift = (8 * k + 8) % 128
            to_right = to_right + (pltpu.roll(b, shift, 1) if shift else b)
        return to_left, to_right

    def unpack(from_right, from_left, k):
        a = pltpu.roll(from_right, 128 - 8 * k, 1) if k else from_right
        shift = (120 - 8 * k) % 128
        b = pltpu.roll(from_left, shift, 1) if shift else from_left
        return jnp.where(lane16 < 8, a, jnp.where(lane16 >= 120, b, 0.0))

    def corner(from_right, from_left):
        return jnp.where(lane < 8, from_right, jnp.where(lane >= 120, from_left, 0.0))

    def to_neighbours(which, pairs):
        targets = [(up, w), (down, w), (s, left), (s, right), (up, left), (up, right), (down, left), (down, right)]
        return [
            pltpu.make_async_remote_copy(
                src_ref=src, dst_ref=dst, send_sem=msend.at[which, i], recv_sem=mrecv.at[which, i],
                device_id=to, device_id_type=MESH,
            )
            for i, ((src, dst), to) in enumerate(zip(pairs, targets, strict=True))
        ]

    def send_row(which):
        def act(to):
            pltpu.make_async_remote_copy(
                src_ref=rows.at[which, pl.ds(0, 1)], dst_ref=bufs.at[which, pl.ds(me, 1)],
                send_sem=asend.at[which], recv_sem=arecv.at[which], device_id=to, device_id_type=MESH,
            ).start()

        everyone(act)
        pltpu.make_async_copy(
            rows.at[which, pl.ds(0, 1)], bufs.at[which, pl.ds(me, 1)], arecv.at[which]
        ).start()

    def wait_rows(which):
        pltpu.make_async_copy(bufs.at[which], bufs.at[which], arecv.at[which]).wait()

    def wait_sent(which):
        part = bufs.at[which, pl.ds(0, DEVICES - 1)]
        pltpu.make_async_copy(part, part, asend.at[which]).wait()

    def partial_values(c):
        at = iota((32, DEVICES), 0) + 32 * s
        pick = jnp.where(slots[...] == at, 1.0, 0.0)
        high, low = split(c)
        pick2 = jnp.concatenate([pick, pick], axis=1).astype(BF16)
        both = jnp.concatenate([high, low], axis=0).astype(BF16)
        ordered = jnp.dot(pick2, both, preferred_element_type=F32)
        keep = iota((32, 128), 1) // 16 == iota((32, 128), 0) % 8
        ordered = jnp.where(keep, ordered, 0.0)
        total = jnp.zeros((128, 128), F32)
        for q in range(4):
            row = jnp.sum(ordered[8 * q : 8 * q + 8], axis=0, keepdims=True)
            total = total + inv[:, 128 * q : 128 * q + 128] * row
        sums = lane_totals(total)
        return jnp.sum(jnp.where(iota((128, 128), 0) == iota((128, 128), 1), sums, 0.0), axis=0, keepdims=True)

    def add_partials(which):
        total = bufs[2 * which + 1, 0:32]
        for a in range(1, NS):
            total = total + bufs[2 * which + 1, 32 * a : 32 * a + 32]
        ypk[which] = total

    def coefficients(which, a, b, place):
        mine = slot[a * NW + b]
        row = ypk[which, pl.ds(lax.shift_right_logical(mine, 3), 1), :]
        shift = lax.bitwise_and(16 * place + 128 - 16 * lax.bitwise_and(mine, 7), 127)
        rolled = pltpu.roll(jnp.broadcast_to(row, (8, 128)), shift, 1)
        return jnp.where(lane // 16 == place, rolled, 0.0)

    def prolonged(groups, stream_table, wall_table):
        own_row = (lane % 16) // 4 == sub
        stacked = jnp.concatenate(
            [jnp.where(own_row, g, 0.0) for g in groups] + [jnp.zeros((8, 128), F32)], axis=0
        )
        high, low = split(stacked)
        operand = jnp.concatenate([high + pltpu.roll(low, 64, 1), high], axis=1).astype(BF16)
        mixed = jnp.dot(operand, wall_table, preferred_element_type=F32)
        high, low = split(mixed)
        operand = jnp.concatenate([high, low, high, jnp.zeros_like(high)], axis=0).astype(BF16)
        return jnp.dot(stream_table[...], operand, preferred_element_type=F32)

    tail_lane = iota((8, 128), 1)

    def tail_valid(depth):
        inner = jnp.logical_and(tail_lane < depth, w < NW - 1)
        outer = jnp.logical_and(tail_lane >= 128 - depth, w > 0)
        return jnp.logical_or(inner, outer)

    def masked(value, valid):
        return jnp.concatenate([value[:, 0:CY], jnp.where(valid, value[:, CY:], 0.0)], axis=1)

    wide_sub = iota((8, COLS), 0)

    def hsum(v):
        return v + pltpu.roll(v, 1, 1) + pltpu.roll(v, COLS - 1, 1)

    def vsum(before, here, after):
        above = pltpu.roll(jnp.where(wide_sub == 7, before, here), 1, 0)
        below = pltpu.roll(jnp.where(wide_sub == 0, after, here), 7, 0)
        return here + above + below

    def chebyshev(g):
        valid = tail_valid(4)

        def begin(i, carry):
            value = g[strip(i), :] * (1.0 / MIDDLE)
            x[strip(i), :] = value
            u[strip(i), :] = value
            return carry

        lax.fori_loop(0, STRIPS, begin, 0)
        for a, b in sweep_factors():

            def update(i, total):
                here = x[strip(i), :]
                e = g[strip(i), :] - d3[strip(i), :] * here + total * (1.0 / 3.0)
                return here, masked(a * u[strip(i), :] + b * e, valid)

            h0 = hsum(x[0:8, :])
            h1 = hsum(x[8:16, :])
            here, step = update(0, vsum(jnp.zeros_like(h0), h0, h1))
            step = jnp.where(wide_sub >= 4, step, 0.0)
            u[0:8, :] = step
            x[0:8, :] = here + step

            def body(i, carry):
                before, now = carry
                after = hsum(x[strip(i + 1), :])
                here, step = update(i, vsum(before, now, after))
                u[strip(i), :] = step
                x[strip(i), :] = here + step
                return now, after

            before, now = lax.fori_loop(1, STRIPS - 1, body, (h0, h1))
            here, step = update(STRIPS - 1, vsum(before, now, jnp.zeros_like(now)))
            step = jnp.where(wide_sub < 4, step, 0.0)
            u[ROWS - 8 : ROWS, :] = step
            x[ROWS - 8 : ROWS, :] = here + step

    loads[0].wait()
    loads[1].wait()
    loads[2].wait()
    rows[0] = jnp.broadcast_to(restrict(ext.at[0]), (8, 128))
    loads[3].wait()
    for f in range(2):
        a, b = pack(ext.at[f])
        colsend[0, 16 * f : 16 * f + 16] = a
        colsend[1, 16 * f : 16 * f + 16] = b

    pl.semaphore_wait(barrier, DEVICES - 1)
    top, bottom = pl.ds(8, 8), pl.ds(CX, 8)
    west, east, body_lanes = pl.ds(0, 128), pl.ds(CY - 128, 128), pl.ds(0, CY)
    margins = to_neighbours(
        0,
        [
            (ext.at[:, top, body_lanes], ext.at[:, pl.ds(ROWS - 8, 8), body_lanes]),
            (ext.at[:, bottom, body_lanes], ext.at[:, pl.ds(0, 8), body_lanes]),
            (colsend.at[0], colrecv.at[0]),
            (colsend.at[1], colrecv.at[1]),
            (ext.at[:, top, west], corners.at[3]),
            (ext.at[:, top, east], corners.at[2]),
            (ext.at[:, bottom, west], corners.at[1]),
            (ext.at[:, bottom, east], corners.at[0]),
        ],
    )
    for copy in margins:
        copy.start()
    send_row(0)
    for copy in margins:
        copy.wait_recv()

    valid4 = tail_valid(4)
    for f in range(2):
        from_right = colrecv[0, 16 * f : 16 * f + 16]
        from_left = colrecv[1, 16 * f : 16 * f + 16]
        for k in range(16):
            ext[f, 8 + 16 * k : 24 + 16 * k, CY:COLS] = unpack(from_right, from_left, k)
        ext[f, 0:8, CY:COLS] = corner(corners[1, f], corners[0, f])
        ext[f, ROWS - 8 : ROWS, CY:COLS] = corner(corners[3, f], corners[2, f])

    def prepare(i, carry):
        gm[strip(i), :] = masked(ext[0, strip(i), :], valid4)
        d3[strip(i), :] = ext[1, strip(i), :] + 3.0
        return carry

    lax.fori_loop(0, STRIPS, prepare, 0)
    gm[0:8, :] = jnp.where(wide_sub >= 4, gm[0:8, :], 0.0)
    gm[ROWS - 8 : ROWS, :] = jnp.where(wide_sub < 4, gm[ROWS - 8 : ROWS, :], 0.0)
    chebyshev(gm)

    a, b = pack(x)
    hcolsend[0] = a
    hcolsend[1] = b
    halos = to_neighbours(
        1,
        [
            (x.at[top, body_lanes], hrows.at[1]),
            (x.at[bottom, body_lanes], hrows.at[0]),
            (hcolsend.at[0], hcolrecv.at[0]),
            (hcolsend.at[1], hcolrecv.at[1]),
            (x.at[top, west], hcorners.at[3]),
            (x.at[top, east], hcorners.at[2]),
            (x.at[bottom, west], hcorners.at[1]),
            (x.at[bottom, east], hcorners.at[0]),
        ],
    )
    for copy in halos:
        copy.start()

    for load in loads[4:]:
        load.wait()
    wait_rows(0)
    rows[1] = jnp.broadcast_to(partial_values(bufs[0]), (8, 128))
    send_row(1)

    for copy in halos:
        copy.wait_recv()
    valid8 = tail_valid(8)

    def place(i, carry):
        first[strip(i), 0:CY] = x[strip(i), 0:CY]
        return carry

    lax.fori_loop(1, STRIPS - 1, place, 0)
    first[0:8, 0:CY] = hrows[0]
    first[ROWS - 8 : ROWS, 0:CY] = hrows[1]
    for k in range(16):
        edge = unpack(hcolrecv[0], hcolrecv[1], k)
        first[8 + 16 * k : 16 + 16 * k, CY:COLS] = jnp.where(valid8, edge[0:8], 0.0)
        first[16 + 16 * k : 24 + 16 * k, CY:COLS] = jnp.where(valid8, edge[8:16], 0.0)
    first[0:8, CY:COLS] = jnp.where(valid8, corner(hcorners[1], hcorners[0]), 0.0)
    first[ROWS - 8 : ROWS, CY:COLS] = jnp.where(valid8, corner(hcorners[3], hcorners[2]), 0.0)

    wait_rows(1)
    add_partials(0)
    groups = []
    for a in (up, s, down):
        group = coefficients(0, a, w, 1)
        group = group + jnp.where(w > 0, coefficients(0, a, left, 0), 0.0)
        group = group + jnp.where(w < NW - 1, coefficients(0, a, right, 2), 0.0)
        groups.append(group)
    py[...] = prolonged(groups, sk, wk[...])

    def total_at(i):
        value = first[strip(i), :] + py[strip(i), :]
        first[strip(i), :] = value
        return hsum(value)

    def residual(i, total):
        value = gm[strip(i), :] - d3[strip(i), :] * first[strip(i), :] + total * (1.0 / 3.0)
        return masked(value, valid4)

    h0 = total_at(0)
    h1 = total_at(1)
    res[0:8, :] = jnp.where(wide_sub >= 4, residual(0, vsum(jnp.zeros_like(h0), h0, h1)), 0.0)

    def residual_body(i, carry):
        before, now = carry
        after = total_at(i + 1)
        res[strip(i), :] = residual(i, vsum(before, now, after))
        return now, after

    before, now = lax.fori_loop(1, STRIPS - 1, residual_body, (h0, h1))
    res[ROWS - 8 : ROWS, :] = jnp.where(
        wide_sub < 4, residual(STRIPS - 1, vsum(before, now, jnp.zeros_like(now))), 0.0
    )

    rows[2] = jnp.broadcast_to(restrict(res), (8, 128))
    send_row(2)
    resid_copy = pltpu.make_async_copy(res.at[pl.ds(8, CX), pl.ds(0, CY)], resid_hbm, store_sem.at[0])
    resid_copy.start()
    for copy in halos:
        copy.wait_send()
    chebyshev(res)
    wait_rows(2)
    rows[3] = jnp.broadcast_to(partial_values(bufs[2]), (8, 128))
    send_row(3)

    def add_local(i, carry):
        first[strip(i), 0:CY] = first[strip(i), 0:CY] + x[strip(i), 0:CY]
        return carry

    lax.fori_loop(1, STRIPS - 1, add_local, 0)
    wait_rows(3)
    add_partials(1)
    none = jnp.zeros((8, 128), F32)
    py[0:CX, 0:CY] = prolonged([none, coefficients(1, s, w, 1), none], so, wk[:, 0:CY])

    def add_coarse(i, carry):
        first[strip(i + 1), 0:CY] = first[strip(i + 1), 0:CY] + py[strip(i), 0:CY]
        return carry

    lax.fori_loop(0, CX // 8, add_coarse, 0)
    out_copy = pltpu.make_async_copy(first.at[pl.ds(8, CX), pl.ds(0, CY)], out_hbm, store_sem.at[1])
    out_copy.start()
    for which in range(4):
        wait_sent(which)
    for copy in margins:
        copy.wait_send()
    resid_copy.wait()
    out_copy.wait()


def local(right_side, diagonal, coarse_inverse, owner_slot):
    phi_lanes, psi_rows, stream_k, own_k, wall_k = tables()
    field = jax.ShapeDtypeStruct((CX, CY), F32)
    anywhere = pl.BlockSpec(memory_space=pl.ANY)
    vmem = pltpu.VMEM
    dma = pltpu.SemaphoreType.DMA
    work = vmem((ROWS, COLS), F32)
    return pl.pallas_call(
        kernel,
        out_shape=(field, field),
        in_specs=[anywhere] * 10,
        out_specs=(anywhere, anywhere),
        scratch_shapes=[
            vmem((2, ROWS, COLS), F32), work, work, work, work, work, work, work,
            vmem((128, 512), F32), vmem((3 * CX, 128), F32), vmem((8, CY), F32),
            vmem((ROWS, 128), BF16), vmem((CX, 128), BF16), vmem((256, COLS), BF16), vmem((1, DEVICES), jnp.int32),
            vmem((2, 32, 128), F32), vmem((2, 32, 128), F32), vmem((4, 2, 8, 128), F32),
            vmem((2, 16, 128), F32), vmem((2, 16, 128), F32), vmem((4, 8, 128), F32), vmem((2, 8, CY), F32),
            vmem((4, 8, 128), F32), vmem((4, DEVICES, 128), F32), vmem((2, 32, 128), F32),
            pltpu.SMEM((DEVICES,), jnp.int32),
            dma((10,)), dma((2, 8)), dma((2, 8)), dma((4,)), dma((4,)), dma((2,)),
        ],
        compiler_params=pltpu.CompilerParams(
            collective_id=0, has_side_effects=True, vmem_limit_bytes=32 * 1024 * 1024
        ),
        cost_estimate=pl.CostEstimate(flops=100_000_000, bytes_accessed=4_000_000, transcendentals=0),
    )(
        right_side, diagonal, coarse_inverse, owner_slot, owner_slot.reshape(1, DEVICES),
        phi_lanes, psi_rows, stream_k, own_k, wall_k,
    )


def solution(mesh):
    placed = (P("stream", "wall"), P("stream", "wall"), P("wall", "stream"), P())
    return jax.shard_map(
        local,
        mesh=mesh,
        in_specs=placed,
        out_specs=(P("stream", "wall"), P("stream", "wall")),
        check_vma=False,
    )
```

```python
import math

import jax
import jax.numpy as jnp
import numpy as np
from jax import lax
from jax.experimental import pallas as pl
from jax.experimental.pallas import tpu as pltpu
from jax.sharding import PartitionSpec as P

MESH = pl.DeviceIdType.MESH
NS, NW = 8, 32
DEVICES = NS * NW
CX, CY = 256, 768
DEG = 4
ROWS, COLS = CX + 16, CY + 128
STRIPS = ROWS // 8
MIDDLE = (5.0 + 0.05) / 2.0
SPREAD = (5.0 - 0.05) / 2.0
SCALE = 1.0 / math.sqrt(CX * CY)
F32, BF16 = jnp.float32, jnp.bfloat16


def sweep_factors():
    quotient = MIDDLE / SPREAD
    factor = 1.0 / quotient
    pairs = []
    for _ in range(DEG):
        following = 1.0 / (2.0 * quotient - factor)
        pairs.append((following * factor, 2.0 * following / SPREAD))
        factor = following
    return pairs


def halves(table):
    high = table.astype(BF16)
    return high, (table - high.astype(np.float32)).astype(BF16)


def tables():
    phi = np.cos(np.pi * (np.arange(CX) + 0.5)[None, :] * np.arange(4)[:, None] / CX)
    psi = np.cos(np.pi * (np.arange(CY) + 0.5)[None, :] * np.arange(4)[:, None] / CY)
    phi_lanes = np.repeat(phi[1:].reshape(3 * CX, 1), 128, axis=1).astype(np.float32)
    psi_rows = np.concatenate([psi, psi]).astype(np.float32)
    stream = np.zeros((ROWS, 32), np.float32)
    stream[0:8, 0:4] = phi[:, CX - 8 :].T
    stream[8 : 8 + CX, 8:12] = phi.T
    stream[8 + CX :, 16:20] = phi[:, :8].T
    high, low = halves(stream)
    stream_k = np.concatenate([high, high, low, np.zeros_like(high)], axis=1)
    own_k = stream_k[8 : 8 + CX]
    wall = np.zeros((64, COLS), np.float32)
    for m in range(4):
        wall[4 * m : 4 * m + 4, COLS - 64 :] = psi[:, CY - 64 :]
        wall[16 + 4 * m : 20 + 4 * m, :CY] = psi
        wall[32 + 4 * m : 36 + 4 * m, CY : CY + 64] = psi[:, :64]
    high, low = halves(wall)
    wall_k = np.concatenate([high, high, low, np.zeros_like(high)], axis=0)
    return phi_lanes, psi_rows, stream_k, own_k, wall_k


def iota(shape, dim):
    return lax.broadcasted_iota(jnp.int32, shape, dim)


def split(value):
    high = value.astype(BF16).astype(F32)
    return high, value - high


def lane_totals(value):
    high, low = split(value)
    both = jnp.concatenate([high, low], axis=1).astype(BF16)
    return jnp.dot(both, jnp.ones((256, 128), BF16), preferred_element_type=F32)


def prolonged(groups, stream_table, wall_table):
    stacked = jnp.concatenate(groups + [jnp.zeros((8, 128), F32)], axis=0)
    high, low = split(stacked)
    operand = jnp.concatenate([high + pltpu.roll(low, 64, 1), high], axis=1).astype(BF16)
    mixed = jnp.dot(operand, wall_table, preferred_element_type=F32)
    high, low = split(mixed)
    operand = jnp.concatenate([high, low, high, jnp.zeros_like(high)], axis=0).astype(BF16)
    return jnp.dot(stream_table, operand, preferred_element_type=F32)


def strip(i):
    return pl.ds(pl.multiple_of(i * 8, 8), 8)


def kernel(
    rhs_hbm, diag_hbm, inv_hbm, slot_hbm, slots_hbm, phi_hbm, psi_hbm, sk_hbm, wk_hbm,
    base_hbm, resid_hbm, mine_out,
    ext, gm, d9, x, x2, u, first, res, py, inv, phi, psi, sk, wk, slots,
    colsend, colrecv, corners, hcolsend, hcolrecv, hcorners, hrows,
    rows, bufs, ypk, slot,
    load_sem, msend, mrecv, asend, arecv, store_sem,
):
    s = lax.axis_index("stream")
    w = lax.axis_index("wall")
    me = s * NW + w
    ya, xl = s % 4, s // 4
    xh, za, core = w // 16, (w // 2) % 8, w % 2
    xa = xh * 2 + xl
    up, down = (s + NS - 1) % NS, (s + 1) % NS
    left, right = (w + NW - 1) % NW, (w + 1) % NW

    def around(k, n):
        return n // 2 + (k % 2) * ((k + 1) // 2) - (1 - k % 2) * (k // 2)

    def everyone(act):
        ys = [(ya + d) % 4 for d in (2, 3, 1, 0)]

        def some(k, count):
            z = (za + around(k // 4, 8)) % 8
            xx = (xa + around(k % 4, 4)) % 4
            base_s = (xx % 2) * 4
            base_w = (xx // 2) * 16 + z * 2
            for j in range(count):
                act((base_s + ys[j // 2], base_w + ((1 - core) if j % 2 == 0 else core)))

        def body(k, carry):
            some(k, 8)
            return carry

        lax.fori_loop(0, 31, body, 0)
        some(jnp.int32(31), 7)

    barrier = pltpu.get_barrier_semaphore()
    everyone(lambda to: pl.semaphore_signal(barrier, inc=1, device_id=to, device_id_type=MESH))

    own = ext.at[:, pl.ds(8, CX), pl.ds(0, CY)]
    loads = [
        pltpu.make_async_copy(src, dst, load_sem.at[i])
        for i, (src, dst) in enumerate(
            [
                (rhs_hbm, own.at[0]),
                (phi_hbm, phi),
                (psi_hbm, psi),
                (diag_hbm, own.at[1]),
                (slot_hbm, slot),
                (slots_hbm, slots),
                (inv_hbm, inv),
                (sk_hbm, sk),
                (wk_hbm, wk),
            ]
        )
    ]
    for load in loads:
        load.start()

    lane = iota((8, 128), 1)
    sub = iota((8, 128), 0)
    lane16 = iota((16, 128), 1)

    def restrict(ref):
        def body(i, sums):
            f = ref[strip(i + 1), 0:CY]
            new = [sums[0] + f]
            for m in range(3):
                t = phi[pl.ds(pl.multiple_of(m * CX + i * 8, 8), 8), :]
                new.append(sums[m + 1] + f * jnp.concatenate([t] * 6, axis=1))
            return tuple(new)

        zero = jnp.zeros((8, CY), F32)
        sums = lax.fori_loop(0, CX // 8, body, (zero,) * 4)
        parts = []
        for m in range(4):
            for n in range(4):
                value = sums[m] if n == 0 else sums[m] * psi[n : n + 1, :]
                total = value[:, 0:128]
                for t in range(1, 6):
                    total = total + value[:, 128 * t : 128 * t + 128]
                parts.append(total)
        totals = lane_totals(jnp.concatenate(parts, axis=0))
        keep = iota((128, 128), 0) // 8 == iota((128, 128), 1) % 16
        return jnp.sum(jnp.where(keep, totals, 0.0), axis=0, keepdims=True) * SCALE

    def pack(ref):
        to_left = jnp.zeros((16, 128), F32)
        to_right = jnp.zeros((16, 128), F32)
        for k in range(16):
            a = jnp.where(lane16 < 8, ref[8 + 16 * k : 24 + 16 * k, 0:128], 0.0)
            b = jnp.where(lane16 >= 120, ref[8 + 16 * k : 24 + 16 * k, CY - 128 : CY], 0.0)
            to_left = to_left + (pltpu.roll(a, 8 * k, 1) if k else a)
            shift = (8 * k + 8) % 128
            to_right = to_right + (pltpu.roll(b, shift, 1) if shift else b)
        return to_left, to_right

    def unpack(from_right, from_left, k):
        a = pltpu.roll(from_right, 128 - 8 * k, 1) if k else from_right
        shift = (120 - 8 * k) % 128
        b = pltpu.roll(from_left, shift, 1) if shift else from_left
        return jnp.where(lane16 < 8, a, jnp.where(lane16 >= 120, b, 0.0))

    def corner(from_right, from_left):
        return jnp.where(lane < 8, from_right, jnp.where(lane >= 120, from_left, 0.0))

    def to_neighbours(which, pairs):
        targets = [(up, w), (down, w), (s, left), (s, right), (up, left), (up, right), (down, left), (down, right)]
        return [
            pltpu.make_async_remote_copy(
                src_ref=src, dst_ref=dst, send_sem=msend.at[which, i], recv_sem=mrecv.at[which, i],
                device_id=to, device_id_type=MESH,
            )
            for i, ((src, dst), to) in enumerate(zip(pairs, targets, strict=True))
        ]

    def send_row(which):
        def act(to):
            pltpu.make_async_remote_copy(
                src_ref=rows.at[which, pl.ds(0, 1)], dst_ref=bufs.at[which, pl.ds(me, 1)],
                send_sem=asend.at[which], recv_sem=arecv.at[which], device_id=to, device_id_type=MESH,
            ).start()

        everyone(act)
        pltpu.make_async_copy(
            rows.at[which, pl.ds(0, 1)], bufs.at[which, pl.ds(me, 1)], arecv.at[which]
        ).start()

    def wait_rows(which):
        pltpu.make_async_copy(bufs.at[which], bufs.at[which], arecv.at[which]).wait()

    def wait_sent(which):
        part = bufs.at[which, pl.ds(0, DEVICES - 1)]
        pltpu.make_async_copy(part, part, asend.at[which]).wait()

    def partial_values(c):
        at = iota((32, DEVICES), 0) + 32 * s
        pick = jnp.where(slots[...] == at, 1.0, 0.0)
        high, low = split(c)
        pick2 = jnp.concatenate([pick, pick], axis=1).astype(BF16)
        both = jnp.concatenate([high, low], axis=0).astype(BF16)
        ordered = jnp.dot(pick2, both, preferred_element_type=F32)
        keep = iota((32, 128), 1) // 16 == iota((32, 128), 0) % 8
        ordered = jnp.where(keep, ordered, 0.0)
        total = jnp.zeros((128, 128), F32)
        for q in range(4):
            row = jnp.sum(ordered[8 * q : 8 * q + 8], axis=0, keepdims=True)
            total = total + inv[:, 128 * q : 128 * q + 128] * row
        sums = lane_totals(total)
        return jnp.sum(jnp.where(iota((128, 128), 0) == iota((128, 128), 1), sums, 0.0), axis=0, keepdims=True)

    def add_partials(which):
        total = bufs[2 * which + 1, 0:32]
        for a in range(1, NS):
            total = total + bufs[2 * which + 1, 32 * a : 32 * a + 32]
        ypk[which] = total

    def coefficients(which, a, b, place):
        mine = slot[a * NW + b]
        row = ypk[which, pl.ds(lax.shift_right_logical(mine, 3), 1), :]
        shift = lax.bitwise_and(16 * place + 128 - 16 * lax.bitwise_and(mine, 7), 127)
        rolled = pltpu.roll(jnp.broadcast_to(row, (8, 128)), shift, 1)
        return jnp.where(lane // 16 == place, rolled, 0.0)

    tail_lane = iota((8, 128), 1)

    def tail_valid(depth):
        inner = jnp.logical_and(tail_lane < depth, w < NW - 1)
        outer = jnp.logical_and(tail_lane >= 128 - depth, w > 0)
        return jnp.logical_or(inner, outer)

    def masked(value, valid):
        return jnp.concatenate([value[:, 0:CY], jnp.where(valid, value[:, CY:], 0.0)], axis=1)

    wide_sub = iota((8, COLS), 0)

    def hsum(v):
        return v + pltpu.roll(v, 1, 1) + pltpu.roll(v, COLS - 1, 1)

    def vsum(before, here, after):
        above = pltpu.roll(jnp.where(wide_sub == 7, before, here), 1, 0)
        below = pltpu.roll(jnp.where(wide_sub == 0, after, here), 7, 0)
        return here + above + below

    def rows_at(i):
        return slice(8 * i, 8 * i + 8)

    def stencil_strips(load, use):
        zero = jnp.zeros((8, COLS), F32)
        value = load(0)
        before, now = zero, hsum(value)
        for i in range(STRIPS):
            following = load(i + 1) if i + 1 < STRIPS else None
            after = zero if following is None else hsum(following)
            use(i, value, vsum(before, now, after))
            before, now, value = now, after, following

    def inside(i, value, valid):
        value = masked(value, valid)
        if i == 0:
            return jnp.where(wide_sub >= 4, value, 0.0)
        if i == STRIPS - 1:
            return jnp.where(wide_sub < 4, value, 0.0)
        return value

    def chebyshev(g):
        valid = tail_valid(4)
        old, new = x, x2
        for k, (a, b) in enumerate(sweep_factors()):

            def load(i, k=k, old=old):
                return g[rows_at(i), :] * (1.0 / (3.0 * MIDDLE)) if k == 0 else old[rows_at(i), :]

            def use(i, value, total, k=k, a=a, b=b, new=new):
                e = g[rows_at(i), :] - d9[rows_at(i), :] * value + total
                step = a * (value if k == 0 else u[rows_at(i), :]) + (b / 3.0) * e
                step = inside(i, step, valid)
                if k < DEG - 1:
                    u[rows_at(i), :] = step
                new[rows_at(i), :] = value + step

            stencil_strips(load, use)
            old, new = new, old

    loads[0].wait()
    loads[1].wait()
    loads[2].wait()
    rows[0] = jnp.broadcast_to(restrict(ext.at[0]), (8, 128))
    loads[3].wait()
    for f in range(2):
        a, b = pack(ext.at[f])
        colsend[0, 16 * f : 16 * f + 16] = a
        colsend[1, 16 * f : 16 * f + 16] = b

    pl.semaphore_wait(barrier, DEVICES - 1)
    top, bottom = pl.ds(8, 8), pl.ds(CX, 8)
    west, east, body_lanes = pl.ds(0, 128), pl.ds(CY - 128, 128), pl.ds(0, CY)
    margins = to_neighbours(
        0,
        [
            (ext.at[:, top, body_lanes], ext.at[:, pl.ds(ROWS - 8, 8), body_lanes]),
            (ext.at[:, bottom, body_lanes], ext.at[:, pl.ds(0, 8), body_lanes]),
            (colsend.at[0], colrecv.at[0]),
            (colsend.at[1], colrecv.at[1]),
            (ext.at[:, top, west], corners.at[3]),
            (ext.at[:, top, east], corners.at[2]),
            (ext.at[:, bottom, west], corners.at[1]),
            (ext.at[:, bottom, east], corners.at[0]),
        ],
    )
    for copy in margins:
        copy.start()
    send_row(0)
    for copy in margins:
        copy.wait_recv()

    valid4 = tail_valid(4)
    for f in range(2):
        from_right = colrecv[0, 16 * f : 16 * f + 16]
        from_left = colrecv[1, 16 * f : 16 * f + 16]
        for k in range(16):
            ext[f, 8 + 16 * k : 24 + 16 * k, CY:COLS] = unpack(from_right, from_left, k)
        ext[f, 0:8, CY:COLS] = corner(corners[1, f], corners[0, f])
        ext[f, ROWS - 8 : ROWS, CY:COLS] = corner(corners[3, f], corners[2, f])

    def prepare(i, carry):
        gm[strip(i), :] = masked(ext[0, strip(i), :], valid4)
        d9[strip(i), :] = ext[1, strip(i), :] * 3.0 + 9.0
        return carry

    lax.fori_loop(0, STRIPS, prepare, 0, unroll=True)
    gm[0:8, :] = jnp.where(wide_sub >= 4, gm[0:8, :], 0.0)
    gm[ROWS - 8 : ROWS, :] = jnp.where(wide_sub < 4, gm[ROWS - 8 : ROWS, :], 0.0)
    chebyshev(gm)

    a, b = pack(x)
    hcolsend[0] = a
    hcolsend[1] = b
    halos = to_neighbours(
        1,
        [
            (x.at[top, body_lanes], hrows.at[1]),
            (x.at[bottom, body_lanes], hrows.at[0]),
            (hcolsend.at[0], hcolrecv.at[0]),
            (hcolsend.at[1], hcolrecv.at[1]),
            (x.at[top, west], hcorners.at[3]),
            (x.at[top, east], hcorners.at[2]),
            (x.at[bottom, west], hcorners.at[1]),
            (x.at[bottom, east], hcorners.at[0]),
        ],
    )
    for copy in halos:
        copy.start()

    for load in loads[4:]:
        load.wait()
    wait_rows(0)
    rows[1] = jnp.broadcast_to(partial_values(bufs[0]), (8, 128))
    send_row(1)

    for copy in halos:
        copy.wait_recv()
    valid8 = tail_valid(8)

    def place(i, carry):
        first[strip(i), 0:CY] = x[strip(i), 0:CY]
        return carry

    lax.fori_loop(1, STRIPS - 1, place, 0, unroll=True)
    first[0:8, 0:CY] = hrows[0]
    first[ROWS - 8 : ROWS, 0:CY] = hrows[1]
    for k in range(16):
        edge = unpack(hcolrecv[0], hcolrecv[1], k)
        first[8 + 16 * k : 16 + 16 * k, CY:COLS] = jnp.where(valid8, edge[0:8], 0.0)
        first[16 + 16 * k : 24 + 16 * k, CY:COLS] = jnp.where(valid8, edge[8:16], 0.0)
    first[0:8, CY:COLS] = jnp.where(valid8, corner(hcorners[1], hcorners[0]), 0.0)
    first[ROWS - 8 : ROWS, CY:COLS] = jnp.where(valid8, corner(hcorners[3], hcorners[2]), 0.0)

    wait_rows(1)
    add_partials(0)
    groups = []
    for a in (up, s, down):
        group = coefficients(0, a, w, 1)
        group = group + jnp.where(w > 0, coefficients(0, a, left, 0), 0.0)
        group = group + jnp.where(w < NW - 1, coefficients(0, a, right, 2), 0.0)
        groups.append(jnp.where((lane % 16) // 4 == sub, group, 0.0))
    py[...] = prolonged(groups, sk[...], wk[...])

    def first_at(i):
        value = first[rows_at(i), :] + py[rows_at(i), :] * (1.0 / 3.0)
        first[rows_at(i), :] = value
        return value

    def residual(i, value, total):
        res[rows_at(i), :] = inside(i, gm[rows_at(i), :] - d9[rows_at(i), :] * value + total, valid4)

    stencil_strips(first_at, residual)

    rows[2] = jnp.broadcast_to(restrict(res), (8, 128))
    send_row(2)
    resid_copy = pltpu.make_async_copy(res.at[pl.ds(8, CX), pl.ds(0, CY)], resid_hbm, store_sem.at[0])
    resid_copy.start()
    for copy in halos:
        copy.wait_send()
    chebyshev(res)
    wait_rows(2)
    rows[3] = jnp.broadcast_to(partial_values(bufs[2]), (8, 128))
    send_row(3)

    def add_local(i, carry):
        first[strip(i), 0:CY] = (first[strip(i), 0:CY] + x[strip(i), 0:CY]) * 3.0
        return carry

    lax.fori_loop(1, STRIPS - 1, add_local, 0, unroll=True)
    base_copy = pltpu.make_async_copy(first.at[pl.ds(8, CX), pl.ds(0, CY)], base_hbm, store_sem.at[1])
    base_copy.start()
    wait_rows(3)
    add_partials(1)
    own_row = (lane % 16) // 4 == sub
    mine_out[...] = jnp.where(own_row, coefficients(1, s, w, 1), 0.0)
    for which in range(4):
        wait_sent(which)
    for copy in margins:
        copy.wait_send()
    resid_copy.wait()
    base_copy.wait()


PIECES = 4


def finish(
    base_hbm, resid_hbm, mine_hbm, stream_hbm, wall_hbm, out_hbm, resid_out,
    base, resid, mine, stream_table, wall_table, small_sem, load_sem, store_sem,
):
    small = [
        pltpu.make_async_copy(src, dst, small_sem.at[i])
        for i, (src, dst) in enumerate([(mine_hbm, mine), (wall_hbm, wall_table), (stream_hbm, stream_table)])
    ]
    for copy in small:
        copy.start()
    parts = [pl.ds(i * (CX // PIECES), CX // PIECES) for i in range(PIECES)]
    loads, stores = [], []
    for k, (src, here, dst) in enumerate(((resid_hbm, resid, resid_out), (base_hbm, base, out_hbm))):
        loads.append([pltpu.make_async_copy(src.at[p], here.at[p], load_sem.at[k, i]) for i, p in enumerate(parts)])
        stores.append([pltpu.make_async_copy(here.at[p], dst.at[p], store_sem.at[k, i]) for i, p in enumerate(parts)])
    for copy in loads[0] + loads[1]:
        copy.start()
    for copy in small:
        copy.wait()
    none = jnp.zeros((8, 128), F32)
    coarse = prolonged([none, mine[...], none], stream_table[...], wall_table[...])
    for i in range(PIECES):
        loads[0][i].wait()
        stores[0][i].start()
    for i in range(PIECES):
        rows = slice(i * (CX // PIECES), (i + 1) * (CX // PIECES))
        loads[1][i].wait()
        base[rows, :] = base[rows, :] + coarse[rows, :]
        stores[1][i].start()
    for copy in stores[0] + stores[1]:
        copy.wait()


def local(right_side, diagonal, coarse_inverse, owner_slot):
    phi_lanes, psi_rows, stream_k, own_k, wall_k = tables()
    field = jax.ShapeDtypeStruct((CX, CY), F32)
    anywhere = pl.BlockSpec(memory_space=pl.ANY)
    in_vmem = pl.BlockSpec(memory_space=pltpu.VMEM)
    vmem = pltpu.VMEM
    dma = pltpu.SemaphoreType.DMA
    work = vmem((ROWS, COLS), F32)
    base, resid, mine = pl.pallas_call(
        kernel,
        out_shape=(field, field, jax.ShapeDtypeStruct((8, 128), F32)),
        in_specs=[anywhere] * 9,
        out_specs=(anywhere, anywhere, in_vmem),
        scratch_shapes=[
            vmem((2, ROWS, COLS), F32), work, work, work, work, work, work, work, work,
            vmem((128, 512), F32), vmem((3 * CX, 128), F32), vmem((8, CY), F32),
            vmem((ROWS, 128), BF16), vmem((256, COLS), BF16), vmem((1, DEVICES), jnp.int32),
            vmem((2, 32, 128), F32), vmem((2, 32, 128), F32), vmem((4, 2, 8, 128), F32),
            vmem((2, 16, 128), F32), vmem((2, 16, 128), F32), vmem((4, 8, 128), F32), vmem((2, 8, CY), F32),
            vmem((4, 8, 128), F32), vmem((4, DEVICES, 128), F32), vmem((2, 32, 128), F32),
            pltpu.SMEM((DEVICES,), jnp.int32),
            dma((10,)), dma((2, 8)), dma((2, 8)), dma((4,)), dma((4,)), dma((2,)),
        ],
        compiler_params=pltpu.CompilerParams(
            collective_id=0, has_side_effects=True, vmem_limit_bytes=60 * 1024 * 1024
        ),
        cost_estimate=pl.CostEstimate(flops=100_000_000, bytes_accessed=4_000_000, transcendentals=0),
    )(
        right_side, diagonal, coarse_inverse, owner_slot, owner_slot.reshape(1, DEVICES),
        phi_lanes, psi_rows, stream_k, wall_k,
    )
    return pl.pallas_call(
        finish,
        out_shape=(field, field),
        in_specs=[anywhere] * 5,
        out_specs=(anywhere, anywhere),
        scratch_shapes=[
            vmem((CX, CY), F32), vmem((CX, CY), F32), vmem((8, 128), F32), vmem((CX, 128), BF16), vmem((256, CY), BF16),
            dma((3,)), dma((2, PIECES)), dma((2, PIECES)),
        ],
        compiler_params=pltpu.CompilerParams(vmem_limit_bytes=60 * 1024 * 1024),
        cost_estimate=pl.CostEstimate(flops=50_000_000, bytes_accessed=3_000_000, transcendentals=0),
    )(base, resid, mine, own_k, np.ascontiguousarray(wall_k[:, :CY]))


def solution(mesh):
    placed = (P("stream", "wall"), P("stream", "wall"), P("wall", "stream"), P())
    return jax.shard_map(
        local,
        mesh=mesh,
        in_specs=placed,
        out_specs=(P("stream", "wall"), P("stream", "wall")),
        check_vma=False,
    )
```

```python
import math

import jax
import jax.numpy as jnp
import numpy as np
from jax import lax
from jax.experimental import pallas as pl
from jax.experimental.pallas import tpu as pltpu
from jax.sharding import PartitionSpec as P

MESH = pl.DeviceIdType.MESH
NS, NW = 8, 32
DEVICES = NS * NW
CX, CY = 256, 768
DEG = 4
ROWS, COLS = CX + 16, CY + 128
STRIPS = ROWS // 8
MIDDLE = (5.0 + 0.05) / 2.0
SPREAD = (5.0 - 0.05) / 2.0
SCALE = 1.0 / math.sqrt(CX * CY)
F32, BF16 = jnp.float32, jnp.bfloat16


def sweep_factors():
    quotient = MIDDLE / SPREAD
    factor = 1.0 / quotient
    pairs = []
    for _ in range(DEG):
        following = 1.0 / (2.0 * quotient - factor)
        pairs.append((following * factor, 2.0 * following / SPREAD))
        factor = following
    return pairs


def halves(table):
    high = table.astype(BF16)
    return high, (table - high.astype(np.float32)).astype(BF16)


def tables():
    phi = np.cos(np.pi * (np.arange(CX) + 0.5)[None, :] * np.arange(7)[:, None] / CX)
    psi = np.cos(np.pi * (np.arange(CY) + 0.5)[None, :] * np.arange(7)[:, None] / CY)
    phi_lanes = np.repeat(phi[1:].reshape(6 * CX, 1), 128, axis=1).astype(np.float32)
    psi_rows = np.concatenate([psi, psi[:1]]).astype(np.float32)
    stream = np.zeros((ROWS, 32), np.float32)
    stream[0:8, 0:4] = phi[:4, CX - 8 :].T
    stream[8 : 8 + CX, 8:12] = phi[:4].T
    stream[8 + CX :, 16:20] = phi[:4, :8].T
    high, low = halves(stream)
    stream_k = np.concatenate([high, high, low, np.zeros_like(high)], axis=1)
    own_k = stream_k[8 : 8 + CX]
    wall = np.zeros((64, COLS), np.float32)
    for m in range(4):
        wall[4 * m : 4 * m + 4, COLS - 64 :] = psi[:4, CY - 64 :]
        wall[16 + 4 * m : 20 + 4 * m, :CY] = psi[:4]
        wall[32 + 4 * m : 36 + 4 * m, CY : CY + 64] = psi[:4, :64]
    high, low = halves(wall)
    wall_k = np.concatenate([high, high, low, np.zeros_like(high)], axis=0)
    return phi_lanes, psi_rows, stream_k, own_k, wall_k


EDGES = 20


def coarse_tables():
    phi = np.cos(np.pi * (np.arange(CX) + 0.5)[None, :] * np.arange(4)[:, None] / CX)
    psi = np.cos(np.pi * (np.arange(CY) + 0.5)[None, :] * np.arange(4)[:, None] / CY)
    lam = 1.0 + 2.0 * np.cos(np.pi * np.arange(4) / CX)
    mu = 1.0 + 2.0 * np.cos(np.pi * np.arange(4) / CY)
    p0, p1, q0, q1 = phi[:, 0], phi[:, -1], psi[:, 0], psi[:, -1]
    nx, ny = (phi**2).sum(1), (psi**2).sum(1)
    near = {(a, b): np.zeros((EDGES, 4, 4)) for a in (-1, 0, 1) for b in (-1, 0, 1)}
    from_modes = np.zeros((4, 4, EDGES))
    corner = {(0, 0): 16, (0, 1): 17, (1, 0): 18, (1, 1): 19}
    ps, qs = (p0, p1), (q0, q1)
    for n in range(4):
        for side in (0, 1):
            row = 4 * side + n
            near[0, 0][row, :, n] -= mu[n] * ps[side]
            near[1 if side == 0 else -1, 0][row, :, n] += mu[n] * ps[1 - side]
            from_modes[:, n, row] += ps[side] * ny[n]
    for m in range(4):
        for side in (0, 1):
            row = 8 + 4 * side + m
            near[0, 0][row, m, :] -= lam[m] * qs[side]
            near[0, 1 if side == 0 else -1][row, m, :] += lam[m] * qs[1 - side]
            from_modes[m, :, row] += qs[side] * nx[m]
    for (i, j), row in corner.items():
        a, b = (1 if i == 0 else -1), (1 if j == 0 else -1)
        near[0, 0][row] += np.outer(ps[i], qs[j])
        near[a, 0][row] -= np.outer(ps[1 - i], qs[j])
        near[0, b][row] -= np.outer(ps[i], qs[1 - j])
        near[a, b][row] += np.outer(ps[1 - i], qs[1 - j])
        from_modes[:, :, row] += np.outer(ps[i], qs[j])
    near = {key: value.reshape(EDGES, 16) * (SCALE / 3.0) for key, value in near.items()}
    from_modes = from_modes.reshape(16, EDGES)
    smooth = np.outer(lam, mu).reshape(16) / 3.0
    norm = np.outer(nx, ny).reshape(16)
    mix = np.zeros((3, 128, 16))
    mix[0, 0:16] = np.eye(16)
    for side, b in enumerate((0, -1, 1)):
        for place, a in enumerate((0, -1, 1)):
            start = 16 + 36 * place
            values = from_modes @ near[a, b]
            if a == 0 and b == 0:
                values = values - np.diag(SCALE * (3.0 - smooth) * norm)
            mix[side, start : start + 20] = near[a, b]
            for k in range(16):
                mix[side, start + 20 + k] = values[(36 + k) % 16]
    wide = np.concatenate([np.tile(mix[i], (1, 8)) for i in range(3)], axis=1).astype(np.float32)
    high, low = halves(wide)
    mix_k = np.concatenate([high, high, low], axis=0)
    weights = np.zeros((52, 128), np.float32)
    for k in range(16):
        weights[k, k] = 3.0 * SCALE * smooth[k]
        weights[16 + k, k] = -SCALE
    for e in range(EDGES):
        weights[32 + e, 16 + e] = 3.0
    spread = np.zeros((128, 256), np.float32)
    for k in range(16):
        for j in range(16):
            m, n, mm, nn = k // 4, k % 4, j // 4, j % 4
            for p in (m + mm, abs(m - mm)):
                for q in (n + nn, abs(n - nn)):
                    spread[7 * p + q, 16 * k + j] += 0.25
    return mix_k, np.repeat(weights, 8, axis=0), np.concatenate([spread, spread]).astype(BF16)


def iota(shape, dim):
    return lax.broadcasted_iota(jnp.int32, shape, dim)


def split(value):
    high = value.astype(BF16).astype(F32)
    return high, value - high


def lane_totals(value):
    high, low = split(value)
    both = jnp.concatenate([high, low], axis=1).astype(BF16)
    return jnp.dot(both, jnp.ones((256, 128), BF16), preferred_element_type=F32)


def prolonged(groups, stream_table, wall_table):
    stacked = jnp.concatenate(groups + [jnp.zeros((8, 128), F32)], axis=0)
    high, low = split(stacked)
    operand = jnp.concatenate([high + pltpu.roll(low, 64, 1), high], axis=1).astype(BF16)
    mixed = jnp.dot(operand, wall_table, preferred_element_type=F32)
    high, low = split(mixed)
    operand = jnp.concatenate([high, low, high, jnp.zeros_like(high)], axis=0).astype(BF16)
    return jnp.dot(stream_table, operand, preferred_element_type=F32)


def tile16(value):
    alike = jnp.where(iota((256, 128), 0) % 16 == iota((256, 128), 1) % 16, 1.0, 0.0).astype(BF16)
    high, low = split(value)
    both = jnp.concatenate([high, low], axis=1).astype(BF16)
    return jnp.dot(both, alike, preferred_element_type=F32)


def strip(i):
    return pl.ds(pl.multiple_of(i * 8, 8), 8)


def kernel(
    rhs_hbm, diag_hbm, inv_hbm, slot_hbm, slots_hbm, phi_hbm, psi_hbm, sk_hbm, wk_hbm, mix_hbm, weights_hbm, spread_hbm,
    base_hbm, resid_hbm, mine_out,
    ext, gm, d9, x, x2, u, first, res, py, inv, phi, psi, sk, wk, mix, weights, spread, slots,
    colsend, colrecv, corners, hcolsend, hcolrecv, hcorners, hrows,
    row0, st, packed, cw, dbuf, row1, buf1, row2, buf2, ypk, onehot, block, diag_modes, slot,
    load_sem, msend, mrecv, asend, arecv, store_sem,
):
    s = lax.axis_index("stream")
    w = lax.axis_index("wall")
    me = s * NW + w
    ya, xl = s % 4, s // 4
    xh, za, core = w // 16, (w // 2) % 8, w % 2
    xa = xh * 2 + xl
    up, down = (s + NS - 1) % NS, (s + 1) % NS
    left, right = (w + NW - 1) % NW, (w + 1) % NW

    def around(k, n):
        return n // 2 + (k % 2) * ((k + 1) // 2) - (1 - k % 2) * (k // 2)

    def everyone(act):
        ys = [(ya + d) % 4 for d in (2, 3, 1, 0)]

        def some(k, count):
            z = (za + around(k // 4, 8)) % 8
            xx = (xa + around(k % 4, 4)) % 4
            base_s = (xx % 2) * 4
            base_w = (xx // 2) * 16 + z * 2
            for j in range(count):
                act((base_s + ys[j // 2], base_w + ((1 - core) if j % 2 == 0 else core)))

        def body(k, carry):
            some(k, 8)
            return carry

        lax.fori_loop(0, 31, body, 0)
        some(jnp.int32(31), 7)

    def stream_mates(act):
        for d in (2, 3, 1, 0):
            for flip in (1, 0):
                if d or flip:
                    act(((xl if flip == 0 else 1 - xl) * 4 + (ya + d) % 4, w))

    def wall_mates(act):
        for d in (4, 5, 3, 6, 2, 7, 1, 0):
            for flip in (1, 0):
                for other in (1, 0):
                    if d or flip or other:
                        x_part = (xh if flip == 0 else 1 - xh) * 16
                        act((s, x_part + ((za + d) % 8) * 2 + (core if other == 0 else 1 - core)))

    barrier = pltpu.get_barrier_semaphore()

    def greet(to):
        pl.semaphore_signal(barrier, inc=1, device_id=to, device_id_type=MESH)

    wall_mates(greet)
    stream_mates(greet)
    diagonals = [(up, left), (up, right), (down, left), (down, right)]
    for to in diagonals:
        greet(to)

    own = ext.at[:, pl.ds(8, CX), pl.ds(0, CY)]
    loads = [
        pltpu.make_async_copy(src, dst, load_sem.at[i])
        for i, (src, dst) in enumerate(
            [
                (rhs_hbm, own.at[0]),
                (phi_hbm, phi),
                (psi_hbm, psi),
                (diag_hbm, own.at[1]),
                (slot_hbm, slot),
                (slots_hbm, slots),
                (inv_hbm, inv),
                (sk_hbm, sk),
                (wk_hbm, wk),
                (mix_hbm, mix),
                (weights_hbm, weights),
                (spread_hbm, spread),
            ]
        )
    ]
    for load in loads:
        load.start()

    lane = iota((8, 128), 1)
    sub = iota((8, 128), 0)
    lane16 = iota((16, 128), 1)

    def mode_sums(load, count):
        def body(i, sums):
            f = load(i)
            new = [sums[0] + f]
            for m in range(count - 1):
                t = phi[pl.ds(pl.multiple_of(m * CX + i * 8, 8), 8), :]
                new.append(sums[m + 1] + f * jnp.concatenate([t] * 6, axis=1))
            return tuple(new)

        return lax.fori_loop(0, CX // 8, body, (jnp.zeros((8, CY), F32),) * count)

    def fold(value):
        total = value[:, 0:128]
        for t in range(1, 6):
            total = total + value[:, 128 * t : 128 * t + 128]
        return total

    def mode_parts(sums, count):
        return [fold(v if n == 0 else v * psi[n : n + 1, :]) for v in sums for n in range(count)]

    def gathered(parts, period):
        totals = lane_totals(jnp.concatenate(parts, axis=0))
        shape = totals.shape
        keep = iota(shape, 0) // 8 == iota(shape, 1) % period
        return jnp.sum(jnp.where(keep, totals, 0.0), axis=0, keepdims=True)

    def pack(ref):
        to_left = jnp.zeros((16, 128), F32)
        to_right = jnp.zeros((16, 128), F32)
        for k in range(16):
            a = jnp.where(lane16 < 8, ref[8 + 16 * k : 24 + 16 * k, 0:128], 0.0)
            b = jnp.where(lane16 >= 120, ref[8 + 16 * k : 24 + 16 * k, CY - 128 : CY], 0.0)
            to_left = to_left + (pltpu.roll(a, 8 * k, 1) if k else a)
            shift = (8 * k + 8) % 128
            to_right = to_right + (pltpu.roll(b, shift, 1) if shift else b)
        return to_left, to_right

    def unpack(from_right, from_left, k):
        a = pltpu.roll(from_right, 128 - 8 * k, 1) if k else from_right
        shift = (120 - 8 * k) % 128
        b = pltpu.roll(from_left, shift, 1) if shift else from_left
        return jnp.where(lane16 < 8, a, jnp.where(lane16 >= 120, b, 0.0))

    def corner(from_right, from_left):
        return jnp.where(lane < 8, from_right, jnp.where(lane >= 120, from_left, 0.0))

    def to_neighbours(which, pairs):
        targets = [(up, w), (down, w), (s, left), (s, right), (up, left), (up, right), (down, left), (down, right)]
        return [
            pltpu.make_async_remote_copy(
                src_ref=src, dst_ref=dst, send_sem=msend.at[which, i], recv_sem=mrecv.at[which, i],
                device_id=to, device_id_type=MESH,
            )
            for i, ((src, dst), to) in enumerate(zip(pairs, targets, strict=True))
        ]

    def sender(index, src, dst):
        def act(to):
            pltpu.make_async_remote_copy(
                src_ref=src, dst_ref=dst, send_sem=asend.at[index], recv_sem=arecv.at[index],
                device_id=to, device_id_type=MESH,
            ).start()

        return act

    def send(index, mates, src, dst):
        mates(sender(index, src, dst))
        pltpu.make_async_copy(src, dst, arecv.at[index]).start()

    def wait_all(index, buf):
        pltpu.make_async_copy(buf, buf, arecv.at[index]).wait()

    def wait_sent(index, part):
        pltpu.make_async_copy(part, part, asend.at[index]).wait()

    def partial_values(c, tiled):
        at = iota((32, DEVICES), 0) + 32 * s
        pick = jnp.where(slots[...] == at, 1.0, 0.0)
        high, low = split(c)
        pick2 = jnp.concatenate([pick, pick], axis=1).astype(BF16)
        both = jnp.concatenate([high, low], axis=0).astype(BF16)
        ordered = jnp.dot(pick2, both, preferred_element_type=F32)
        if not tiled:
            ordered = tile16(ordered)
        keep = iota((32, 128), 1) // 16 == iota((32, 128), 0) % 8
        ordered = jnp.where(keep, ordered, 0.0)
        total = jnp.zeros((128, 128), F32)
        for q in range(4):
            row = jnp.sum(ordered[8 * q : 8 * q + 8], axis=0, keepdims=True)
            total = total + inv[:, 128 * q : 128 * q + 128] * row
        sums = lane_totals(total)
        return jnp.sum(jnp.where(iota((128, 128), 0) == iota((128, 128), 1), sums, 0.0), axis=0, keepdims=True)

    def add_partials(which):
        buf = buf1.at[0] if which == 0 else buf2
        total = buf[0:32]
        for a in range(1, NS):
            total = total + buf[32 * a : 32 * a + 32]
        ypk[which] = total

    def coefficients(which, a, b, place):
        mine = slot[a * NW + b]
        row = ypk[which, pl.ds(lax.shift_right_logical(mine, 3), 1), :]
        shift = lax.bitwise_and(16 * place + 128 - 16 * lax.bitwise_and(mine, 7), 127)
        rolled = pltpu.roll(jnp.broadcast_to(row, (8, 128)), shift, 1)
        return jnp.where(lane // 16 == place, rolled, 0.0)

    tail_lane = iota((8, 128), 1)

    def tail_valid(depth):
        inner = jnp.logical_and(tail_lane < depth, w < NW - 1)
        outer = jnp.logical_and(tail_lane >= 128 - depth, w > 0)
        return jnp.logical_or(inner, outer)

    def masked(value, valid):
        return jnp.concatenate([value[:, 0:CY], jnp.where(valid, value[:, CY:], 0.0)], axis=1)

    wide_sub = iota((8, COLS), 0)

    def hsum(v):
        return v + pltpu.roll(v, 1, 1) + pltpu.roll(v, COLS - 1, 1)

    def vsum(before, here, after):
        above = pltpu.roll(jnp.where(wide_sub == 7, before, here), 1, 0)
        below = pltpu.roll(jnp.where(wide_sub == 0, after, here), 7, 0)
        return here + above + below

    def rows_at(i):
        return slice(8 * i, 8 * i + 8)

    def stencil_strips(load, use):
        zero = jnp.zeros((8, COLS), F32)
        value = load(0)
        before, now = zero, hsum(value)
        for i in range(STRIPS):
            following = load(i + 1) if i + 1 < STRIPS else None
            after = zero if following is None else hsum(following)
            use(i, value, vsum(before, now, after))
            before, now, value = now, after, following

    def inside(i, value, valid):
        value = masked(value, valid)
        if i == 0:
            return jnp.where(wide_sub >= 4, value, 0.0)
        if i == STRIPS - 1:
            return jnp.where(wide_sub < 4, value, 0.0)
        return value

    def chebyshev(g):
        valid = tail_valid(4)
        old, new = x, x2
        for k, (a, b) in enumerate(sweep_factors()):

            def load(i, k=k, old=old):
                return g[rows_at(i), :] * (1.0 / (3.0 * MIDDLE)) if k == 0 else old[rows_at(i), :]

            def use(i, value, total, k=k, a=a, b=b, new=new):
                e = g[rows_at(i), :] - d9[rows_at(i), :] * value + total
                step = a * (value if k == 0 else u[rows_at(i), :]) + (b / 3.0) * e
                step = inside(i, step, valid)
                if k < DEG - 1:
                    u[rows_at(i), :] = step
                new[rows_at(i), :] = value + step

            stencil_strips(load, use)
            old, new = new, old

    for load in loads[:3]:
        load.wait()
    sums = mode_sums(lambda i: ext[0, strip(i + 1), 0:CY], 4)
    first_residual = gathered(mode_parts(sums, 4), 16) * SCALE
    lane1 = iota((1, 128), 1)
    row0[0, 0:1] = jnp.where(lane1 // 16 == s, first_residual, 0.0)
    loads[3].wait()
    sums = mode_sums(lambda i: ext[1, strip(i + 1), 0:CY], 7)
    row0[0, 1:2] = gathered(mode_parts(sums, 7), 128)
    for f in range(2):
        a, b = pack(ext.at[f])
        colsend[0, 16 * f : 16 * f + 16] = a
        colsend[1, 16 * f : 16 * f + 16] = b

    pl.semaphore_wait(barrier, 7 + 31 + 4)
    top, bottom = pl.ds(8, 8), pl.ds(CX, 8)
    west, east, body_lanes = pl.ds(0, 128), pl.ds(CY - 128, 128), pl.ds(0, CY)
    margins = to_neighbours(
        0,
        [
            (ext.at[:, top, body_lanes], ext.at[:, pl.ds(ROWS - 8, 8), body_lanes]),
            (ext.at[:, bottom, body_lanes], ext.at[:, pl.ds(0, 8), body_lanes]),
            (colsend.at[0], colrecv.at[0]),
            (colsend.at[1], colrecv.at[1]),
            (ext.at[:, top, west], corners.at[3]),
            (ext.at[:, top, east], corners.at[2]),
            (ext.at[:, bottom, west], corners.at[1]),
            (ext.at[:, bottom, east], corners.at[0]),
        ],
    )
    send(0, stream_mates, row0, st.at[pl.ds(s, 1)])
    for copy in margins:
        copy.start()
    for load in loads[4:]:
        load.wait()
    at = iota((128, DEVICES), 0)
    group_of = lax.shift_right_logical(slots[...], 3)
    onehot[...] = jnp.where(jnp.logical_and(group_of == at % 32, at < 64), 1.0, 0.0).T
    block[...] = jnp.where(lax.bitwise_and(slots[...], 7) == at // 16, 1.0, 0.0).T
    wait_all(0, st)
    total = st[0, 0:1]
    for a in range(1, NS):
        total = total + st[a, 0:1]
    packed[...] = jnp.broadcast_to(total, (8, 128))
    send(1, wall_mates, packed.at[pl.ds(0, 1)], cw.at[pl.ds(w, 1)])
    send(2, wall_mates, st.at[:, pl.ds(1, 1), :], dbuf.at[:, pl.ds(w, 1), :])
    for copy in margins:
        copy.wait_recv()

    valid4 = tail_valid(4)
    for f in range(2):
        from_right = colrecv[0, 16 * f : 16 * f + 16]
        from_left = colrecv[1, 16 * f : 16 * f + 16]
        for k in range(16):
            ext[f, 8 + 16 * k : 24 + 16 * k, CY:COLS] = unpack(from_right, from_left, k)
        ext[f, 0:8, CY:COLS] = corner(corners[1, f], corners[0, f])
        ext[f, ROWS - 8 : ROWS, CY:COLS] = corner(corners[3, f], corners[2, f])

    def prepare(i, carry):
        gm[strip(i), :] = masked(ext[0, strip(i), :], valid4)
        d9[strip(i), :] = ext[1, strip(i), :] * 3.0 + 9.0
        return carry

    lax.fori_loop(0, STRIPS, prepare, 0, unroll=True)
    gm[0:8, :] = jnp.where(wide_sub >= 4, gm[0:8, :], 0.0)
    gm[ROWS - 8 : ROWS, :] = jnp.where(wide_sub < 4, gm[ROWS - 8 : ROWS, :], 0.0)
    chebyshev(gm)

    a, b = pack(x)
    hcolsend[0] = a
    hcolsend[1] = b
    halos = to_neighbours(
        1,
        [
            (x.at[top, body_lanes], hrows.at[1]),
            (x.at[bottom, body_lanes], hrows.at[0]),
            (hcolsend.at[0], hcolrecv.at[0]),
            (hcolsend.at[1], hcolrecv.at[1]),
            (x.at[top, west], hcorners.at[3]),
            (x.at[top, east], hcorners.at[2]),
            (x.at[bottom, west], hcorners.at[1]),
            (x.at[bottom, east], hcorners.at[0]),
        ],
    )
    for copy in halos:
        copy.start()

    u_sums = mode_sums(lambda i: x[strip(i + 1), 0:CY], 4)
    w_sums = mode_sums(lambda i: x[strip(i + 1), 0:CY] * d9[strip(i + 1), 0:CY], 4)
    parts = mode_parts(u_sums, 4) + mode_parts(w_sums, 4)
    for edge, here in ((x[8:16, 0:CY], sub == 0), (x[CX : CX + 8, 0:CY], sub == 7)):
        parts += [jnp.where(here, p, 0.0) for p in mode_parts([edge], 4)]
    parts += [jnp.where(lane == 0, v[:, 0:128], 0.0) for v in u_sums]
    parts += [jnp.where(lane == 127, v[:, CY - 128 : CY], 0.0) for v in u_sums]
    for edge, at_row in ((x[8:16, :], 0), (x[CX : CX + 8, :], 7)):
        for tile, at_lane in ((edge[:, 0:128], 0), (edge[:, CY - 128 : CY], 127)):
            parts.append(jnp.where(jnp.logical_and(sub == at_row, lane == at_lane), tile, 0.0))
    totals = lane_totals(jnp.concatenate(parts, axis=0)) * weights[...]
    moments = jnp.sum(totals, axis=0, keepdims=True)
    moments = moments + jnp.where(lane1 < 16, first_residual, 0.0)
    row1[1] = jnp.broadcast_to(moments, (8, 128))

    wait_all(1, cw)
    spread_rows = jnp.concatenate([cw[...]] * NS, axis=0)
    own_lanes = iota((DEVICES, 128), 1) // 16 == iota((DEVICES, 128), 0) // NW
    row1[0] = jnp.broadcast_to(partial_values(jnp.where(own_lanes, spread_rows, 0.0), False), (8, 128))
    send(3, everyone, row1.at[:, pl.ds(0, 1), :], buf1.at[:, pl.ds(me, 1), :])

    wait_all(2, dbuf)
    high, low = split(dbuf[...].reshape(DEVICES, 128))
    both = jnp.concatenate([high, low], axis=1).astype(BF16)
    diag_modes[...] = jnp.dot(both, spread[...], preferred_element_type=F32) * (-SCALE)

    for copy in halos:
        copy.wait_recv()
    valid8 = tail_valid(8)

    def place(i, carry):
        first[strip(i), 0:CY] = x[strip(i), 0:CY]
        return carry

    lax.fori_loop(1, STRIPS - 1, place, 0, unroll=True)
    first[0:8, 0:CY] = hrows[0]
    first[ROWS - 8 : ROWS, 0:CY] = hrows[1]
    for k in range(16):
        edge = unpack(hcolrecv[0], hcolrecv[1], k)
        first[8 + 16 * k : 16 + 16 * k, CY:COLS] = jnp.where(valid8, edge[0:8], 0.0)
        first[16 + 16 * k : 24 + 16 * k, CY:COLS] = jnp.where(valid8, edge[8:16], 0.0)
    first[0:8, CY:COLS] = jnp.where(valid8, corner(hcorners[1], hcorners[0]), 0.0)
    first[ROWS - 8 : ROWS, CY:COLS] = jnp.where(valid8, corner(hcorners[3], hcorners[2]), 0.0)

    wait_all(3, buf1)
    add_partials(0)

    high, low = split(ypk[0])
    both = jnp.concatenate([high, low, jnp.zeros((64, 128), F32)], axis=0).astype(BF16)
    values = jnp.dot(onehot[...].astype(BF16), both, preferred_element_type=F32) * block[...]
    values = tile16(values)
    known = buf1[1]
    lanes = iota((DEVICES, 128), 1)
    near = jnp.where(lanes < 36, known, jnp.where(lanes < 52, values, 0.0))
    near = jnp.where(lanes >= 16, near, 0.0)
    mixed = jnp.where(lanes < 16, known, near)
    mixed = mixed + pltpu.roll(jnp.concatenate([near[-NW:], near[:-NW]], axis=0), 36, 1)
    mixed = mixed + pltpu.roll(jnp.concatenate([near[NW:], near[:NW]], axis=0), 72, 1)
    high, low = split(mixed)
    both = jnp.concatenate([high, low, high], axis=1).astype(BF16)
    sides = jnp.dot(both, mix[...], preferred_element_type=F32)
    wall_row = iota((DEVICES, 128), 0) % NW
    second_residual = sides[:, 0:128]
    second_residual = second_residual + jnp.where(wall_row > 0, pltpu.roll(sides[:, 128:256], 1, 0), 0.0)
    second_residual = second_residual + jnp.where(
        wall_row < NW - 1, pltpu.roll(sides[:, 256:384], DEVICES - 1, 0), 0.0
    )
    products = [part for h in range(2) for part in split(values * diag_modes[:, 128 * h : 128 * h + 128])]
    both = jnp.concatenate(products, axis=1).astype(BF16)
    at = iota((512, 128), 0)
    summed = jnp.where(8 * (at // 256) + (at % 128) // 16 == iota((512, 128), 1) % 16, 1.0, 0.0)
    second_residual = second_residual + jnp.dot(both, summed.astype(BF16), preferred_element_type=F32)
    row2[...] = jnp.broadcast_to(partial_values(second_residual, True), (8, 128))
    send(4, everyone, row2.at[pl.ds(0, 1)], buf2.at[pl.ds(me, 1)])

    groups = []
    for a in (up, s, down):
        group = coefficients(0, a, w, 1)
        group = group + jnp.where(w > 0, coefficients(0, a, left, 0), 0.0)
        group = group + jnp.where(w < NW - 1, coefficients(0, a, right, 2), 0.0)
        groups.append(jnp.where((lane % 16) // 4 == sub, group, 0.0))
    py[...] = prolonged(groups, sk[...], wk[...])

    def first_at(i):
        value = first[rows_at(i), :] + py[rows_at(i), :] * (1.0 / 3.0)
        first[rows_at(i), :] = value
        return value

    def residual(i, value, total):
        res[rows_at(i), :] = inside(i, gm[rows_at(i), :] - d9[rows_at(i), :] * value + total, valid4)

    stencil_strips(first_at, residual)

    resid_copy = pltpu.make_async_copy(res.at[pl.ds(8, CX), pl.ds(0, CY)], resid_hbm, store_sem.at[0])
    resid_copy.start()
    for copy in halos:
        copy.wait_send()
    chebyshev(res)

    def add_local(i, carry):
        first[strip(i), 0:CY] = (first[strip(i), 0:CY] + x[strip(i), 0:CY]) * 3.0
        return carry

    lax.fori_loop(1, STRIPS - 1, add_local, 0, unroll=True)
    base_copy = pltpu.make_async_copy(first.at[pl.ds(8, CX), pl.ds(0, CY)], base_hbm, store_sem.at[1])
    base_copy.start()
    wait_all(4, buf2)
    add_partials(1)
    own_row = (lane % 16) // 4 == sub
    mine_out[...] = jnp.where(own_row, coefficients(1, s, w, 1), 0.0)
    wait_sent(0, st.at[pl.ds(0, 7)])
    wait_sent(1, cw.at[pl.ds(0, 31)])
    wait_sent(2, dbuf.at[:, pl.ds(0, 31), :])
    wait_sent(3, buf1.at[:, pl.ds(0, DEVICES - 1), :])
    wait_sent(4, buf2.at[pl.ds(0, DEVICES - 1)])
    for copy in margins:
        copy.wait_send()
    resid_copy.wait()
    base_copy.wait()


PIECES = 4


def finish(
    base_hbm, resid_hbm, mine_hbm, stream_hbm, wall_hbm, out_hbm, resid_out,
    base, resid, mine, stream_table, wall_table, small_sem, load_sem, store_sem,
):
    small = [
        pltpu.make_async_copy(src, dst, small_sem.at[i])
        for i, (src, dst) in enumerate([(mine_hbm, mine), (wall_hbm, wall_table), (stream_hbm, stream_table)])
    ]
    for copy in small:
        copy.start()
    parts = [pl.ds(i * (CX // PIECES), CX // PIECES) for i in range(PIECES)]
    loads, stores = [], []
    for k, (src, here, dst) in enumerate(((resid_hbm, resid, resid_out), (base_hbm, base, out_hbm))):
        loads.append([pltpu.make_async_copy(src.at[p], here.at[p], load_sem.at[k, i]) for i, p in enumerate(parts)])
        stores.append([pltpu.make_async_copy(here.at[p], dst.at[p], store_sem.at[k, i]) for i, p in enumerate(parts)])
    for copy in loads[0] + loads[1]:
        copy.start()
    for copy in small:
        copy.wait()
    none = jnp.zeros((8, 128), F32)
    coarse = prolonged([none, mine[...], none], stream_table[...], wall_table[...])
    for i in range(PIECES):
        loads[0][i].wait()
        stores[0][i].start()
    for i in range(PIECES):
        rows = slice(i * (CX // PIECES), (i + 1) * (CX // PIECES))
        loads[1][i].wait()
        base[rows, :] = base[rows, :] + coarse[rows, :]
        stores[1][i].start()
    for copy in stores[0] + stores[1]:
        copy.wait()


def local(right_side, diagonal, coarse_inverse, owner_slot):
    phi_lanes, psi_rows, stream_k, own_k, wall_k = tables()
    mix_k, moment_weights, spread_k = coarse_tables()
    field = jax.ShapeDtypeStruct((CX, CY), F32)
    anywhere = pl.BlockSpec(memory_space=pl.ANY)
    in_vmem = pl.BlockSpec(memory_space=pltpu.VMEM)
    vmem = pltpu.VMEM
    dma = pltpu.SemaphoreType.DMA
    work = vmem((ROWS, COLS), F32)
    base, resid, mine = pl.pallas_call(
        kernel,
        out_shape=(field, field, jax.ShapeDtypeStruct((8, 128), F32)),
        in_specs=[anywhere] * 12,
        out_specs=(anywhere, anywhere, in_vmem),
        scratch_shapes=[
            vmem((2, ROWS, COLS), F32), work, work, work, work, work, work, work, work,
            vmem((128, 512), F32), vmem((6 * CX, 128), F32), vmem((8, CY), F32),
            vmem((ROWS, 128), BF16), vmem((256, COLS), BF16),
            vmem((384, 384), BF16), vmem((416, 128), F32), vmem((256, 256), BF16), vmem((1, DEVICES), jnp.int32),
            vmem((2, 32, 128), F32), vmem((2, 32, 128), F32), vmem((4, 2, 8, 128), F32),
            vmem((2, 16, 128), F32), vmem((2, 16, 128), F32), vmem((4, 8, 128), F32), vmem((2, 8, CY), F32),
            vmem((1, 2, 128), F32), vmem((NS, 2, 128), F32), vmem((8, 128), F32), vmem((NW, 128), F32),
            vmem((NS, NW, 128), F32), vmem((2, 8, 128), F32), vmem((2, DEVICES, 128), F32),
            vmem((8, 128), F32), vmem((DEVICES, 128), F32), vmem((2, NW, 128), F32),
            vmem((DEVICES, 128), F32), vmem((DEVICES, 128), F32), vmem((DEVICES, 256), F32),
            pltpu.SMEM((DEVICES,), jnp.int32),
            dma((12,)), dma((2, 8)), dma((2, 8)), dma((5,)), dma((5,)), dma((2,)),
        ],
        compiler_params=pltpu.CompilerParams(
            collective_id=0, has_side_effects=True, vmem_limit_bytes=60 * 1024 * 1024
        ),
        cost_estimate=pl.CostEstimate(flops=100_000_000, bytes_accessed=4_000_000, transcendentals=0),
    )(
        right_side, diagonal, coarse_inverse, owner_slot, owner_slot.reshape(1, DEVICES),
        phi_lanes, psi_rows, stream_k, wall_k, mix_k, moment_weights, spread_k,
    )
    return pl.pallas_call(
        finish,
        out_shape=(field, field),
        in_specs=[anywhere] * 5,
        out_specs=(anywhere, anywhere),
        scratch_shapes=[
            vmem((CX, CY), F32), vmem((CX, CY), F32), vmem((8, 128), F32), vmem((CX, 128), BF16), vmem((256, CY), BF16),
            dma((3,)), dma((2, PIECES)), dma((2, PIECES)),
        ],
        compiler_params=pltpu.CompilerParams(vmem_limit_bytes=60 * 1024 * 1024),
        cost_estimate=pl.CostEstimate(flops=50_000_000, bytes_accessed=3_000_000, transcendentals=0),
    )(base, resid, mine, own_k, np.ascontiguousarray(wall_k[:, :CY]))


def solution(mesh):
    placed = (P("stream", "wall"), P("stream", "wall"), P("wall", "stream"), P())
    return jax.shard_map(
        local,
        mesh=mesh,
        in_specs=placed,
        out_specs=(P("stream", "wall"), P("stream", "wall")),
        check_vma=False,
    )
```

```python
import math

import jax
import jax.numpy as jnp
import numpy as np
from jax import lax
from jax.experimental import pallas as pl
from jax.experimental.pallas import tpu as pltpu
from jax.sharding import PartitionSpec as P

MESH = pl.DeviceIdType.MESH
NS, NW = 8, 32
DEVICES = NS * NW
CX, CY = 256, 768
DEG = 4
ROWS, COLS = CX + 16, CY + 128
STRIPS = ROWS // 8
MIDDLE = (5.0 + 0.05) / 2.0
SPREAD = (5.0 - 0.05) / 2.0
SCALE = 1.0 / math.sqrt(CX * CY)
F32, BF16 = jnp.float32, jnp.bfloat16


def sweep_factors():
    quotient = MIDDLE / SPREAD
    factor = 1.0 / quotient
    pairs = []
    for _ in range(DEG):
        following = 1.0 / (2.0 * quotient - factor)
        pairs.append((following * factor, 2.0 * following / SPREAD))
        factor = following
    return pairs


def halves(table):
    high = table.astype(BF16)
    return high, (table - high.astype(np.float32)).astype(BF16)


def tables():
    phi = np.cos(np.pi * (np.arange(CX) + 0.5)[None, :] * np.arange(7)[:, None] / CX)
    psi = np.cos(np.pi * (np.arange(CY) + 0.5)[None, :] * np.arange(7)[:, None] / CY)
    phi_lanes = np.repeat(phi[1:].reshape(6 * CX, 1), 128, axis=1).astype(np.float32)
    psi_rows = np.concatenate([psi, psi[:1]]).astype(np.float32)
    stream = np.zeros((ROWS, 32), np.float32)
    stream[0:8, 0:4] = phi[:4, CX - 8 :].T
    stream[8 : 8 + CX, 8:12] = phi[:4].T
    stream[8 + CX :, 16:20] = phi[:4, :8].T
    high, low = halves(stream)
    stream_k = np.concatenate([high, high, low, np.zeros_like(high)], axis=1)
    own_k = stream_k[8 : 8 + CX]
    wall = np.zeros((64, COLS), np.float32)
    for m in range(4):
        wall[4 * m : 4 * m + 4, COLS - 64 :] = psi[:4, CY - 64 :]
        wall[16 + 4 * m : 20 + 4 * m, :CY] = psi[:4]
        wall[32 + 4 * m : 36 + 4 * m, CY : CY + 64] = psi[:4, :64]
    high, low = halves(wall)
    wall_k = np.concatenate([high, high, low, np.zeros_like(high)], axis=0)
    return phi_lanes, psi_rows, stream_k, own_k, wall_k


EDGES = 20


def coarse_tables():
    phi = np.cos(np.pi * (np.arange(CX) + 0.5)[None, :] * np.arange(4)[:, None] / CX)
    psi = np.cos(np.pi * (np.arange(CY) + 0.5)[None, :] * np.arange(4)[:, None] / CY)
    lam = 1.0 + 2.0 * np.cos(np.pi * np.arange(4) / CX)
    mu = 1.0 + 2.0 * np.cos(np.pi * np.arange(4) / CY)
    p0, p1, q0, q1 = phi[:, 0], phi[:, -1], psi[:, 0], psi[:, -1]
    nx, ny = (phi**2).sum(1), (psi**2).sum(1)
    near = {(a, b): np.zeros((EDGES, 4, 4)) for a in (-1, 0, 1) for b in (-1, 0, 1)}
    from_modes = np.zeros((4, 4, EDGES))
    corner = {(0, 0): 16, (0, 1): 17, (1, 0): 18, (1, 1): 19}
    ps, qs = (p0, p1), (q0, q1)
    for n in range(4):
        for side in (0, 1):
            row = 4 * side + n
            near[0, 0][row, :, n] -= mu[n] * ps[side]
            near[1 if side == 0 else -1, 0][row, :, n] += mu[n] * ps[1 - side]
            from_modes[:, n, row] += ps[side] * ny[n]
    for m in range(4):
        for side in (0, 1):
            row = 8 + 4 * side + m
            near[0, 0][row, m, :] -= lam[m] * qs[side]
            near[0, 1 if side == 0 else -1][row, m, :] += lam[m] * qs[1 - side]
            from_modes[m, :, row] += qs[side] * nx[m]
    for (i, j), row in corner.items():
        a, b = (1 if i == 0 else -1), (1 if j == 0 else -1)
        near[0, 0][row] += np.outer(ps[i], qs[j])
        near[a, 0][row] -= np.outer(ps[1 - i], qs[j])
        near[0, b][row] -= np.outer(ps[i], qs[1 - j])
        near[a, b][row] += np.outer(ps[1 - i], qs[1 - j])
        from_modes[:, :, row] += np.outer(ps[i], qs[j])
    near = {key: value.reshape(EDGES, 16) * (SCALE / 3.0) for key, value in near.items()}
    from_modes = from_modes.reshape(16, EDGES)
    smooth = np.outer(lam, mu).reshape(16) / 3.0
    norm = np.outer(nx, ny).reshape(16)
    mix = np.zeros((3, 128, 16))
    mix[0, 0:16] = np.eye(16)
    for side, b in enumerate((0, -1, 1)):
        for place, a in enumerate((0, -1, 1)):
            start = 16 + 36 * place
            values = from_modes @ near[a, b]
            if a == 0 and b == 0:
                values = values - np.diag(SCALE * (3.0 - smooth) * norm)
            mix[side, start : start + 20] = near[a, b]
            for k in range(16):
                mix[side, start + 20 + k] = values[(36 + k) % 16]
    wide = np.concatenate([np.tile(mix[i], (1, 8)) for i in range(3)], axis=1).astype(np.float32)
    high, low = halves(wide)
    mix_k = np.concatenate([high, high, low], axis=0)
    weights = np.zeros((52, 128), np.float32)
    for k in range(16):
        weights[k, k] = 3.0 * SCALE * smooth[k]
        weights[16 + k, k] = -SCALE
    for e in range(EDGES):
        weights[32 + e, 16 + e] = 3.0
    spread = np.zeros((128, 256), np.float32)
    for k in range(16):
        for j in range(16):
            m, n, mm, nn = k // 4, k % 4, j // 4, j % 4
            for p in (m + mm, abs(m - mm)):
                for q in (n + nn, abs(n - nn)):
                    spread[7 * p + q, 16 * k + j] += 0.25
    return mix_k, np.repeat(weights, 8, axis=0), np.concatenate([spread, spread]).astype(BF16)


def iota(shape, dim):
    return lax.broadcasted_iota(jnp.int32, shape, dim)


def split(value):
    high = value.astype(BF16).astype(F32)
    return high, value - high


def lane_totals(value):
    high, low = split(value)
    both = jnp.concatenate([high, low], axis=1).astype(BF16)
    return jnp.dot(both, jnp.ones((256, 128), BF16), preferred_element_type=F32)


def prolonged(groups, stream_table, wall_table):
    stacked = jnp.concatenate(groups + [jnp.zeros((8, 128), F32)], axis=0)
    high, low = split(stacked)
    operand = jnp.concatenate([high + pltpu.roll(low, 64, 1), high], axis=1).astype(BF16)
    mixed = jnp.dot(operand, wall_table, preferred_element_type=F32)
    high, low = split(mixed)
    operand = jnp.concatenate([high, low, high, jnp.zeros_like(high)], axis=0).astype(BF16)
    return jnp.dot(stream_table, operand, preferred_element_type=F32)


def tile16(value):
    alike = jnp.where(iota((256, 128), 0) % 16 == iota((256, 128), 1) % 16, 1.0, 0.0).astype(BF16)
    high, low = split(value)
    both = jnp.concatenate([high, low], axis=1).astype(BF16)
    return jnp.dot(both, alike, preferred_element_type=F32)


def strip(i):
    return pl.ds(pl.multiple_of(i * 8, 8), 8)


def kernel(
    rhs_hbm, diag_hbm, inv_hbm, slot_hbm, slots_hbm, phi_hbm, psi_hbm, sk_hbm, wk_hbm, mix_hbm, weights_hbm, spread_hbm,
    base_hbm, resid_hbm, mine_out,
    ext, gm, d9, x, x2, u, first, res, py, inv, phi, psi, sk, wk, mix, weights, spread, slots,
    colsend, colrecv, corners, hcolsend, hcolrecv, hcorners, hrows,
    rows, st, drow, dst, qst, qpack, cw, dbuf, qbuf, yw0, yw1, onehot, block, diag_modes, slot,
    load_sem, msend, mrecv, asend, arecv, store_sem,
):
    s = lax.axis_index("stream")
    w = lax.axis_index("wall")
    me = s * NW + w
    ya, xl = s % 4, s // 4
    xh, za, core = w // 16, (w // 2) % 8, w % 2
    xa = xh * 2 + xl
    up, down = (s + NS - 1) % NS, (s + 1) % NS
    left, right = (w + NW - 1) % NW, (w + 1) % NW

    def stream_mates(act):
        for d in (2, 3, 1, 0):
            for flip in (1, 0):
                if d or flip:
                    act(((xl if flip == 0 else 1 - xl) * 4 + (ya + d) % 4, w))

    def wall_mates(act):
        for d in (4, 5, 3, 6, 2, 7, 1, 0):
            for flip in (1, 0):
                for other in (1, 0):
                    if d or flip or other:
                        x_part = (xh if flip == 0 else 1 - xh) * 16
                        act((s, x_part + ((za + d) % 8) * 2 + (core if other == 0 else 1 - core)))

    barrier = pltpu.get_barrier_semaphore()

    def greet(to):
        pl.semaphore_signal(barrier, inc=1, device_id=to, device_id_type=MESH)

    wall_mates(greet)
    stream_mates(greet)
    diagonals = [(up, left), (up, right), (down, left), (down, right)]
    for to in diagonals:
        greet(to)

    own = ext.at[:, pl.ds(8, CX), pl.ds(0, CY)]
    loads = [
        pltpu.make_async_copy(src, dst, load_sem.at[i])
        for i, (src, dst) in enumerate(
            [
                (rhs_hbm, own.at[0]),
                (phi_hbm, phi),
                (psi_hbm, psi),
                (diag_hbm, own.at[1]),
                (slot_hbm, slot),
                (slots_hbm, slots),
                (inv_hbm, inv),
                (sk_hbm, sk),
                (wk_hbm, wk),
                (mix_hbm, mix),
                (weights_hbm, weights),
                (spread_hbm, spread),
            ]
        )
    ]
    for load in loads:
        load.start()

    lane = iota((8, 128), 1)
    sub = iota((8, 128), 0)
    lane16 = iota((16, 128), 1)

    def mode_sums(load, count):
        def body(i, sums):
            f = load(i)
            new = [sums[0] + f]
            for m in range(count - 1):
                t = phi[pl.ds(pl.multiple_of(m * CX + i * 8, 8), 8), :]
                new.append(sums[m + 1] + f * jnp.concatenate([t] * 6, axis=1))
            return tuple(new)

        return lax.fori_loop(0, CX // 8, body, (jnp.zeros((8, CY), F32),) * count)

    def fold(value):
        total = value[:, 0:128]
        for t in range(1, 6):
            total = total + value[:, 128 * t : 128 * t + 128]
        return total

    def mode_parts(sums, count):
        return [fold(v if n == 0 else v * psi[n : n + 1, :]) for v in sums for n in range(count)]

    def gathered(parts, period):
        totals = lane_totals(jnp.concatenate(parts, axis=0))
        shape = totals.shape
        keep = iota(shape, 0) // 8 == iota(shape, 1) % period
        return jnp.sum(jnp.where(keep, totals, 0.0), axis=0, keepdims=True)

    def pack(ref):
        to_left = jnp.zeros((16, 128), F32)
        to_right = jnp.zeros((16, 128), F32)
        for k in range(16):
            a = jnp.where(lane16 < 8, ref[8 + 16 * k : 24 + 16 * k, 0:128], 0.0)
            b = jnp.where(lane16 >= 120, ref[8 + 16 * k : 24 + 16 * k, CY - 128 : CY], 0.0)
            to_left = to_left + (pltpu.roll(a, 8 * k, 1) if k else a)
            shift = (8 * k + 8) % 128
            to_right = to_right + (pltpu.roll(b, shift, 1) if shift else b)
        return to_left, to_right

    def unpack(from_right, from_left, k):
        a = pltpu.roll(from_right, 128 - 8 * k, 1) if k else from_right
        shift = (120 - 8 * k) % 128
        b = pltpu.roll(from_left, shift, 1) if shift else from_left
        return jnp.where(lane16 < 8, a, jnp.where(lane16 >= 120, b, 0.0))

    def corner(from_right, from_left):
        return jnp.where(lane < 8, from_right, jnp.where(lane >= 120, from_left, 0.0))

    def to_neighbours(which, pairs):
        targets = [(up, w), (down, w), (s, left), (s, right), (up, left), (up, right), (down, left), (down, right)]
        return [
            pltpu.make_async_remote_copy(
                src_ref=src, dst_ref=dst, send_sem=msend.at[which, i], recv_sem=mrecv.at[which, i],
                device_id=to, device_id_type=MESH,
            )
            for i, ((src, dst), to) in enumerate(zip(pairs, targets, strict=True))
        ]

    def sender(index, src, dst):
        def act(to):
            pltpu.make_async_remote_copy(
                src_ref=src, dst_ref=dst, send_sem=asend.at[index], recv_sem=arecv.at[index],
                device_id=to, device_id_type=MESH,
            ).start()

        return act

    def send(index, mates, src, dst):
        mates(sender(index, src, dst))
        pltpu.make_async_copy(src, dst, arecv.at[index]).start()

    def send_row(which):
        send(2 * which, stream_mates, rows.at[which, pl.ds(0, 1)], st.at[which, pl.ds(s, 1)])

    def forward_row(which, buf):
        wait_all(2 * which, st.at[which])
        total = jnp.sum(st[which], axis=0, keepdims=True)
        rows[3 + which] = jnp.broadcast_to(total, (8, 128))
        send(2 * which + 1, wall_mates, rows.at[3 + which, pl.ds(0, 1)], buf.at[pl.ds(w, 1)])

    def wait_all(index, buf):
        pltpu.make_async_copy(buf, buf, arecv.at[index]).wait()

    def wait_sent(index, part):
        pltpu.make_async_copy(part, part, asend.at[index]).wait()

    def partial_values(c, tiled):
        at = iota((32, DEVICES), 0) + 32 * s
        pick = jnp.where(slots[...] == at, 1.0, 0.0)
        high, low = split(c)
        pick2 = jnp.concatenate([pick, pick], axis=1).astype(BF16)
        both = jnp.concatenate([high, low], axis=0).astype(BF16)
        ordered = jnp.dot(pick2, both, preferred_element_type=F32)
        if not tiled:
            ordered = tile16(ordered)
        keep = iota((32, 128), 1) // 16 == iota((32, 128), 0) % 8
        ordered = jnp.where(keep, ordered, 0.0)
        total = jnp.zeros((128, 128), F32)
        for q in range(4):
            row = jnp.sum(ordered[8 * q : 8 * q + 8], axis=0, keepdims=True)
            total = total + inv[:, 128 * q : 128 * q + 128] * row
        sums = lane_totals(total)
        return jnp.sum(jnp.where(iota((128, 128), 0) == iota((128, 128), 1), sums, 0.0), axis=0, keepdims=True)

    def coefficients(which, a, b, place):
        mine = slot[a * NW + b]
        row = (yw1 if which else yw0)[pl.ds(lax.shift_right_logical(mine, 3), 1), :]
        shift = lax.bitwise_and(16 * place + 128 - 16 * lax.bitwise_and(mine, 7), 127)
        rolled = pltpu.roll(jnp.broadcast_to(row, (8, 128)), shift, 1)
        return jnp.where(lane // 16 == place, rolled, 0.0)

    tail_lane = iota((8, 128), 1)

    def tail_valid(depth):
        inner = jnp.logical_and(tail_lane < depth, w < NW - 1)
        outer = jnp.logical_and(tail_lane >= 128 - depth, w > 0)
        return jnp.logical_or(inner, outer)

    def masked(value, valid):
        return jnp.concatenate([value[:, 0:CY], jnp.where(valid, value[:, CY:], 0.0)], axis=1)

    wide_sub = iota((8, COLS), 0)

    def hsum(v):
        return v + pltpu.roll(v, 1, 1) + pltpu.roll(v, COLS - 1, 1)

    def vsum(before, here, after):
        above = pltpu.roll(jnp.where(wide_sub == 7, before, here), 1, 0)
        below = pltpu.roll(jnp.where(wide_sub == 0, after, here), 7, 0)
        return here + above + below

    def rows_at(i):
        return slice(8 * i, 8 * i + 8)

    def stencil_strips(load, use):
        zero = jnp.zeros((8, COLS), F32)
        value = load(0)
        before, now = zero, hsum(value)
        for i in range(STRIPS):
            following = load(i + 1) if i + 1 < STRIPS else None
            after = zero if following is None else hsum(following)
            use(i, value, vsum(before, now, after))
            before, now, value = now, after, following

    def inside(i, value, valid):
        value = masked(value, valid)
        if i == 0:
            return jnp.where(wide_sub >= 4, value, 0.0)
        if i == STRIPS - 1:
            return jnp.where(wide_sub < 4, value, 0.0)
        return value

    def chebyshev(g, between=None):
        valid = tail_valid(4)
        old, new = x, x2
        for k, (a, b) in enumerate(sweep_factors()):

            def load(i, k=k, old=old):
                return g[rows_at(i), :] * (1.0 / (3.0 * MIDDLE)) if k == 0 else old[rows_at(i), :]

            def use(i, value, total, k=k, a=a, b=b, new=new):
                e = g[rows_at(i), :] - d9[rows_at(i), :] * value + total
                step = a * (value if k == 0 else u[rows_at(i), :]) + (b / 3.0) * e
                step = inside(i, step, valid)
                if k < DEG - 1:
                    u[rows_at(i), :] = step
                new[rows_at(i), :] = value + step

            stencil_strips(load, use)
            old, new = new, old
            if k == 0 and between is not None:
                between()

    for load in loads[:3]:
        load.wait()
    sums = mode_sums(lambda i: ext[0, strip(i + 1), 0:CY], 4)
    first_residual = gathered(mode_parts(sums, 4), 16) * SCALE
    lane1 = iota((1, 128), 1)
    rows[0] = jnp.broadcast_to(jnp.where(lane1 // 16 == s, first_residual, 0.0), (8, 128))
    loads[3].wait()
    for f in range(2):
        a, b = pack(ext.at[f])
        colsend[0, 16 * f : 16 * f + 16] = a
        colsend[1, 16 * f : 16 * f + 16] = b

    pl.semaphore_wait(barrier, 7 + 31 + 4)
    top, bottom = pl.ds(8, 8), pl.ds(CX, 8)
    west, east, body_lanes = pl.ds(0, 128), pl.ds(CY - 128, 128), pl.ds(0, CY)
    margins = to_neighbours(
        0,
        [
            (ext.at[:, top, body_lanes], ext.at[:, pl.ds(ROWS - 8, 8), body_lanes]),
            (ext.at[:, bottom, body_lanes], ext.at[:, pl.ds(0, 8), body_lanes]),
            (colsend.at[0], colrecv.at[0]),
            (colsend.at[1], colrecv.at[1]),
            (ext.at[:, top, west], corners.at[3]),
            (ext.at[:, top, east], corners.at[2]),
            (ext.at[:, bottom, west], corners.at[1]),
            (ext.at[:, bottom, east], corners.at[0]),
        ],
    )
    send_row(0)
    for copy in margins:
        copy.start()
    sums = mode_sums(lambda i: ext[1, strip(i + 1), 0:CY], 7)
    drow[0] = gathered(mode_parts(sums, 7), 128)
    send(6, stream_mates, drow, dst.at[pl.ds(s, 1)])
    for load in loads[4:]:
        load.wait()
    at = iota((128, DEVICES), 0)
    group_of = lax.shift_right_logical(slots[...], 3)
    onehot[...] = jnp.where(jnp.logical_and(group_of == at % 32, at < 64), 1.0, 0.0).T
    block[...] = jnp.where(lax.bitwise_and(slots[...], 7) == at // 16, 1.0, 0.0).T
    forward_row(0, cw)
    wait_all(6, dst)
    send(7, wall_mates, dst, dbuf.at[:, pl.ds(w, 1), :])
    for copy in margins:
        copy.wait_recv()

    valid4 = tail_valid(4)
    for f in range(2):
        from_right = colrecv[0, 16 * f : 16 * f + 16]
        from_left = colrecv[1, 16 * f : 16 * f + 16]
        for k in range(16):
            ext[f, 8 + 16 * k : 24 + 16 * k, CY:COLS] = unpack(from_right, from_left, k)
        ext[f, 0:8, CY:COLS] = corner(corners[1, f], corners[0, f])
        ext[f, ROWS - 8 : ROWS, CY:COLS] = corner(corners[3, f], corners[2, f])

    def prepare(i, carry):
        gm[strip(i), :] = masked(ext[0, strip(i), :], valid4)
        d9[strip(i), :] = ext[1, strip(i), :] * 3.0 + 9.0
        return carry

    lax.fori_loop(0, STRIPS, prepare, 0, unroll=True)
    gm[0:8, :] = jnp.where(wide_sub >= 4, gm[0:8, :], 0.0)
    gm[ROWS - 8 : ROWS, :] = jnp.where(wide_sub < 4, gm[ROWS - 8 : ROWS, :], 0.0)
    chebyshev(gm)

    a, b = pack(x)
    hcolsend[0] = a
    hcolsend[1] = b
    halos = to_neighbours(
        1,
        [
            (x.at[top, body_lanes], hrows.at[1]),
            (x.at[bottom, body_lanes], hrows.at[0]),
            (hcolsend.at[0], hcolrecv.at[0]),
            (hcolsend.at[1], hcolrecv.at[1]),
            (x.at[top, west], hcorners.at[3]),
            (x.at[top, east], hcorners.at[2]),
            (x.at[bottom, west], hcorners.at[1]),
            (x.at[bottom, east], hcorners.at[0]),
        ],
    )
    for copy in halos:
        copy.start()

    u_sums = mode_sums(lambda i: x[strip(i + 1), 0:CY], 4)
    w_sums = mode_sums(lambda i: x[strip(i + 1), 0:CY] * d9[strip(i + 1), 0:CY], 4)
    parts = mode_parts(u_sums, 4) + mode_parts(w_sums, 4)
    for edge, here in ((x[8:16, 0:CY], sub == 0), (x[CX : CX + 8, 0:CY], sub == 7)):
        parts += [jnp.where(here, p, 0.0) for p in mode_parts([edge], 4)]
    parts += [jnp.where(lane == 0, v[:, 0:128], 0.0) for v in u_sums]
    parts += [jnp.where(lane == 127, v[:, CY - 128 : CY], 0.0) for v in u_sums]
    for edge, at_row in ((x[8:16, :], 0), (x[CX : CX + 8, :], 7)):
        for tile, at_lane in ((edge[:, 0:128], 0), (edge[:, CY - 128 : CY], 127)):
            parts.append(jnp.where(jnp.logical_and(sub == at_row, lane == at_lane), tile, 0.0))
    totals = lane_totals(jnp.concatenate(parts, axis=0)) * weights[...]
    moments = jnp.sum(totals, axis=0, keepdims=True)
    moments = moments + jnp.where(lane1 < 16, first_residual, 0.0)
    qpack[3] = moments
    send(8, stream_mates, qpack.at[pl.ds(3, 1)], qst.at[pl.ds(s, 1)])

    wait_all(1, cw)
    spread_rows = jnp.concatenate([cw[...]] * NS, axis=0)
    own_lanes = iota((DEVICES, 128), 1) // 16 == iota((DEVICES, 128), 0) // NW
    rows[1] = jnp.broadcast_to(partial_values(jnp.where(own_lanes, spread_rows, 0.0), False), (8, 128))
    send_row(1)

    wait_all(8, qst)
    for r in range(3):
        total = jnp.zeros((1, 128), F32)
        for a in range(3 * r, min(3 * r + 3, NS)):
            value = jnp.broadcast_to(jnp.where(lane1 < 36, qst[a], 0.0), (8, 128))
            total = total + (pltpu.roll(value, 40 * (a % 3), 1) if a % 3 else value)[0:1]
        qpack[r] = total
    send(9, wall_mates, qpack.at[pl.ds(0, 3)], qbuf.at[:, pl.ds(w, 1), :])

    wait_all(7, dbuf)
    high, low = split(dbuf[...].reshape(DEVICES, 128))
    both = jnp.concatenate([high, low], axis=1).astype(BF16)
    diag_modes[...] = jnp.dot(both, spread[...], preferred_element_type=F32) * (-SCALE)
    forward_row(1, yw0)

    for copy in halos:
        copy.wait_recv()
    valid8 = tail_valid(8)

    def place(i, carry):
        first[strip(i), 0:CY] = x[strip(i), 0:CY]
        return carry

    lax.fori_loop(1, STRIPS - 1, place, 0, unroll=True)
    first[0:8, 0:CY] = hrows[0]
    first[ROWS - 8 : ROWS, 0:CY] = hrows[1]
    for k in range(16):
        edge = unpack(hcolrecv[0], hcolrecv[1], k)
        first[8 + 16 * k : 16 + 16 * k, CY:COLS] = jnp.where(valid8, edge[0:8], 0.0)
        first[16 + 16 * k : 24 + 16 * k, CY:COLS] = jnp.where(valid8, edge[8:16], 0.0)
    first[0:8, CY:COLS] = jnp.where(valid8, corner(hcorners[1], hcorners[0]), 0.0)
    first[ROWS - 8 : ROWS, CY:COLS] = jnp.where(valid8, corner(hcorners[3], hcorners[2]), 0.0)

    wait_all(9, qbuf)
    known = []
    for a in range(NS):
        value = qbuf[a // 3]
        known.append(pltpu.roll(value, 128 - 40 * (a % 3), 1) if a % 3 else value)
    known = jnp.concatenate(known, axis=0)
    wait_all(3, yw0)

    high, low = split(yw0[...])
    both = jnp.concatenate([high, low, jnp.zeros((64, 128), F32)], axis=0).astype(BF16)
    values = jnp.dot(onehot[...].astype(BF16), both, preferred_element_type=F32) * block[...]
    values = tile16(values)
    lanes = iota((DEVICES, 128), 1)
    near = jnp.where(lanes < 36, known, jnp.where(lanes < 52, values, 0.0))
    near = jnp.where(lanes >= 16, near, 0.0)
    mixed = jnp.where(lanes < 16, known, near)
    mixed = mixed + pltpu.roll(jnp.concatenate([near[-NW:], near[:-NW]], axis=0), 36, 1)
    mixed = mixed + pltpu.roll(jnp.concatenate([near[NW:], near[:NW]], axis=0), 72, 1)
    high, low = split(mixed)
    both = jnp.concatenate([high, low, high], axis=1).astype(BF16)
    sides = jnp.dot(both, mix[...], preferred_element_type=F32)
    wall_row = iota((DEVICES, 128), 0) % NW
    second_residual = sides[:, 0:128]
    second_residual = second_residual + jnp.where(wall_row > 0, pltpu.roll(sides[:, 128:256], 1, 0), 0.0)
    second_residual = second_residual + jnp.where(
        wall_row < NW - 1, pltpu.roll(sides[:, 256:384], DEVICES - 1, 0), 0.0
    )
    products = [part for h in range(2) for part in split(values * diag_modes[:, 128 * h : 128 * h + 128])]
    both = jnp.concatenate(products, axis=1).astype(BF16)
    at = iota((512, 128), 0)
    summed = jnp.where(8 * (at // 256) + (at % 128) // 16 == iota((512, 128), 1) % 16, 1.0, 0.0)
    second_residual = second_residual + jnp.dot(both, summed.astype(BF16), preferred_element_type=F32)
    rows[2] = jnp.broadcast_to(partial_values(second_residual, True), (8, 128))
    send_row(2)

    groups = []
    for a in (up, s, down):
        group = coefficients(0, a, w, 1)
        group = group + jnp.where(w > 0, coefficients(0, a, left, 0), 0.0)
        group = group + jnp.where(w < NW - 1, coefficients(0, a, right, 2), 0.0)
        groups.append(jnp.where((lane % 16) // 4 == sub, group, 0.0))
    py[...] = prolonged(groups, sk[...], wk[...])

    def first_at(i):
        value = first[rows_at(i), :] + py[rows_at(i), :] * (1.0 / 3.0)
        first[rows_at(i), :] = value
        return value

    def residual(i, value, total):
        res[rows_at(i), :] = inside(i, gm[rows_at(i), :] - d9[rows_at(i), :] * value + total, valid4)

    stencil_strips(first_at, residual)

    resid_copy = pltpu.make_async_copy(res.at[pl.ds(8, CX), pl.ds(0, CY)], resid_hbm, store_sem.at[0])
    resid_copy.start()
    for copy in halos:
        copy.wait_send()
    chebyshev(res, lambda: forward_row(2, yw1))

    def add_local(i, carry):
        first[strip(i), 0:CY] = (first[strip(i), 0:CY] + x[strip(i), 0:CY]) * 3.0
        return carry

    lax.fori_loop(1, STRIPS - 1, add_local, 0, unroll=True)
    base_copy = pltpu.make_async_copy(first.at[pl.ds(8, CX), pl.ds(0, CY)], base_hbm, store_sem.at[1])
    base_copy.start()
    wait_all(5, yw1)
    own_row = (lane % 16) // 4 == sub
    mine_out[...] = jnp.where(own_row, coefficients(1, s, w, 1), 0.0)
    for which, buf in enumerate((cw, yw0, yw1)):
        wait_sent(2 * which, st.at[which, pl.ds(0, NS - 1)])
        wait_sent(2 * which + 1, buf.at[pl.ds(0, NW - 1)])
    wait_sent(6, dst.at[pl.ds(0, NS - 1)])
    wait_sent(7, dbuf.at[:, pl.ds(0, NW - 1), :])
    wait_sent(8, qst.at[pl.ds(0, NS - 1)])
    wait_sent(9, qbuf.at[:, pl.ds(0, NW - 1), :])
    for copy in margins:
        copy.wait_send()
    resid_copy.wait()
    base_copy.wait()


PIECES = 4


def finish(
    base_hbm, resid_hbm, mine_hbm, stream_hbm, wall_hbm, out_hbm, resid_out,
    base, resid, mine, stream_table, wall_table, small_sem, load_sem, store_sem,
):
    small = [
        pltpu.make_async_copy(src, dst, small_sem.at[i])
        for i, (src, dst) in enumerate([(mine_hbm, mine), (wall_hbm, wall_table), (stream_hbm, stream_table)])
    ]
    for copy in small:
        copy.start()
    parts = [pl.ds(i * (CX // PIECES), CX // PIECES) for i in range(PIECES)]
    loads, stores = [], []
    for k, (src, here, dst) in enumerate(((resid_hbm, resid, resid_out), (base_hbm, base, out_hbm))):
        loads.append([pltpu.make_async_copy(src.at[p], here.at[p], load_sem.at[k, i]) for i, p in enumerate(parts)])
        stores.append([pltpu.make_async_copy(here.at[p], dst.at[p], store_sem.at[k, i]) for i, p in enumerate(parts)])
    for copy in loads[0] + loads[1]:
        copy.start()
    for copy in small:
        copy.wait()
    none = jnp.zeros((8, 128), F32)
    coarse = prolonged([none, mine[...], none], stream_table[...], wall_table[...])
    for i in range(PIECES):
        loads[0][i].wait()
        stores[0][i].start()
    for i in range(PIECES):
        rows = slice(i * (CX // PIECES), (i + 1) * (CX // PIECES))
        loads[1][i].wait()
        base[rows, :] = base[rows, :] + coarse[rows, :]
        stores[1][i].start()
    for copy in stores[0] + stores[1]:
        copy.wait()


def local(right_side, diagonal, coarse_inverse, owner_slot):
    phi_lanes, psi_rows, stream_k, own_k, wall_k = tables()
    mix_k, moment_weights, spread_k = coarse_tables()
    field = jax.ShapeDtypeStruct((CX, CY), F32)
    anywhere = pl.BlockSpec(memory_space=pl.ANY)
    in_vmem = pl.BlockSpec(memory_space=pltpu.VMEM)
    vmem = pltpu.VMEM
    dma = pltpu.SemaphoreType.DMA
    work = vmem((ROWS, COLS), F32)
    base, resid, mine = pl.pallas_call(
        kernel,
        out_shape=(field, field, jax.ShapeDtypeStruct((8, 128), F32)),
        in_specs=[anywhere] * 12,
        out_specs=(anywhere, anywhere, in_vmem),
        scratch_shapes=[
            vmem((2, ROWS, COLS), F32), work, work, work, work, work, work, work, work,
            vmem((128, 512), F32), vmem((6 * CX, 128), F32), vmem((8, CY), F32),
            vmem((ROWS, 128), BF16), vmem((256, COLS), BF16),
            vmem((384, 384), BF16), vmem((416, 128), F32), vmem((256, 256), BF16), vmem((1, DEVICES), jnp.int32),
            vmem((2, 32, 128), F32), vmem((2, 32, 128), F32), vmem((4, 2, 8, 128), F32),
            vmem((2, 16, 128), F32), vmem((2, 16, 128), F32), vmem((4, 8, 128), F32), vmem((2, 8, CY), F32),
            vmem((6, 8, 128), F32), vmem((3, NS, 128), F32), vmem((1, 1, 128), F32), vmem((NS, 1, 128), F32),
            vmem((NS, 1, 128), F32), vmem((4, 1, 128), F32), vmem((NW, 128), F32), vmem((NS, NW, 128), F32),
            vmem((3, NW, 128), F32), vmem((NW, 128), F32), vmem((NW, 128), F32),
            vmem((DEVICES, 128), F32), vmem((DEVICES, 128), F32), vmem((DEVICES, 256), F32),
            pltpu.SMEM((DEVICES,), jnp.int32),
            dma((12,)), dma((2, 8)), dma((2, 8)), dma((10,)), dma((10,)), dma((2,)),
        ],
        compiler_params=pltpu.CompilerParams(
            collective_id=0, has_side_effects=True, vmem_limit_bytes=60 * 1024 * 1024
        ),
        cost_estimate=pl.CostEstimate(flops=100_000_000, bytes_accessed=4_000_000, transcendentals=0),
    )(
        right_side, diagonal, coarse_inverse, owner_slot, owner_slot.reshape(1, DEVICES),
        phi_lanes, psi_rows, stream_k, wall_k, mix_k, moment_weights, spread_k,
    )
    return pl.pallas_call(
        finish,
        out_shape=(field, field),
        in_specs=[anywhere] * 5,
        out_specs=(anywhere, anywhere),
        scratch_shapes=[
            vmem((CX, CY), F32), vmem((CX, CY), F32), vmem((8, 128), F32), vmem((CX, 128), BF16), vmem((256, CY), BF16),
            dma((3,)), dma((2, PIECES)), dma((2, PIECES)),
        ],
        compiler_params=pltpu.CompilerParams(vmem_limit_bytes=60 * 1024 * 1024),
        cost_estimate=pl.CostEstimate(flops=50_000_000, bytes_accessed=3_000_000, transcendentals=0),
    )(base, resid, mine, own_k, np.ascontiguousarray(wall_k[:, :CY]))


def solution(mesh):
    placed = (P("stream", "wall"), P("stream", "wall"), P("wall", "stream"), P())
    return jax.shard_map(
        local,
        mesh=mesh,
        in_specs=placed,
        out_specs=(P("stream", "wall"), P("stream", "wall")),
        check_vma=False,
    )
```

```python
import math

import jax
import jax.numpy as jnp
import numpy as np
from jax import lax
from jax.experimental import pallas as pl
from jax.experimental.pallas import tpu as pltpu
from jax.sharding import PartitionSpec as P

MESH = pl.DeviceIdType.MESH
NS, NW = 8, 32
DEVICES = NS * NW
CX, CY = 256, 768
DEG = 4
ROWS, COLS = CX + 16, CY + 128
STRIPS = ROWS // 8
MIDDLE = (5.0 + 0.05) / 2.0
SPREAD = (5.0 - 0.05) / 2.0
SCALE = 1.0 / math.sqrt(CX * CY)
F32, BF16 = jnp.float32, jnp.bfloat16


def sweep_factors():
    quotient = MIDDLE / SPREAD
    factor = 1.0 / quotient
    pairs = []
    for _ in range(DEG):
        following = 1.0 / (2.0 * quotient - factor)
        pairs.append((following * factor, 2.0 * following / SPREAD))
        factor = following
    return pairs


def halves(table):
    high = table.astype(BF16)
    return high, (table - high.astype(np.float32)).astype(BF16)


def tables():
    phi = np.cos(np.pi * (np.arange(CX) + 0.5)[None, :] * np.arange(7)[:, None] / CX)
    psi = np.cos(np.pi * (np.arange(CY) + 0.5)[None, :] * np.arange(7)[:, None] / CY)
    phi_lanes = np.repeat(phi[1:].reshape(6 * CX, 1), 128, axis=1).astype(np.float32)
    psi_rows = np.concatenate([psi, psi[:1]]).astype(np.float32)
    stream = np.zeros((ROWS, 32), np.float32)
    stream[0:8, 0:4] = phi[:4, CX - 8 :].T
    stream[8 : 8 + CX, 8:12] = phi[:4].T
    stream[8 + CX :, 16:20] = phi[:4, :8].T
    high, low = halves(stream)
    stream_k = np.concatenate([high, high, low, np.zeros_like(high)], axis=1)
    own_k = stream_k[8 : 8 + CX]
    wall = np.zeros((64, COLS), np.float32)
    for m in range(4):
        wall[4 * m : 4 * m + 4, COLS - 64 :] = psi[:4, CY - 64 :]
        wall[16 + 4 * m : 20 + 4 * m, :CY] = psi[:4]
        wall[32 + 4 * m : 36 + 4 * m, CY : CY + 64] = psi[:4, :64]
    high, low = halves(wall)
    wall_k = np.concatenate([high, high, low, np.zeros_like(high)], axis=0)
    return phi_lanes, psi_rows, stream_k, own_k, wall_k


EDGES = 20


def coarse_tables():
    phi = np.cos(np.pi * (np.arange(CX) + 0.5)[None, :] * np.arange(4)[:, None] / CX)
    psi = np.cos(np.pi * (np.arange(CY) + 0.5)[None, :] * np.arange(4)[:, None] / CY)
    lam = 1.0 + 2.0 * np.cos(np.pi * np.arange(4) / CX)
    mu = 1.0 + 2.0 * np.cos(np.pi * np.arange(4) / CY)
    p0, p1, q0, q1 = phi[:, 0], phi[:, -1], psi[:, 0], psi[:, -1]
    nx, ny = (phi**2).sum(1), (psi**2).sum(1)
    near = {(a, b): np.zeros((EDGES, 4, 4)) for a in (-1, 0, 1) for b in (-1, 0, 1)}
    from_modes = np.zeros((4, 4, EDGES))
    corner = {(0, 0): 16, (0, 1): 17, (1, 0): 18, (1, 1): 19}
    ps, qs = (p0, p1), (q0, q1)
    for n in range(4):
        for side in (0, 1):
            row = 4 * side + n
            near[0, 0][row, :, n] -= mu[n] * ps[side]
            near[1 if side == 0 else -1, 0][row, :, n] += mu[n] * ps[1 - side]
            from_modes[:, n, row] += ps[side] * ny[n]
    for m in range(4):
        for side in (0, 1):
            row = 8 + 4 * side + m
            near[0, 0][row, m, :] -= lam[m] * qs[side]
            near[0, 1 if side == 0 else -1][row, m, :] += lam[m] * qs[1 - side]
            from_modes[m, :, row] += qs[side] * nx[m]
    for (i, j), row in corner.items():
        a, b = (1 if i == 0 else -1), (1 if j == 0 else -1)
        near[0, 0][row] += np.outer(ps[i], qs[j])
        near[a, 0][row] -= np.outer(ps[1 - i], qs[j])
        near[0, b][row] -= np.outer(ps[i], qs[1 - j])
        near[a, b][row] += np.outer(ps[1 - i], qs[1 - j])
        from_modes[:, :, row] += np.outer(ps[i], qs[j])
    near = {key: value.reshape(EDGES, 16) * (SCALE / 3.0) for key, value in near.items()}
    from_modes = from_modes.reshape(16, EDGES)
    smooth = np.outer(lam, mu).reshape(16) / 3.0
    norm = np.outer(nx, ny).reshape(16)
    mix = np.zeros((3, 128, 16))
    mix[0, 0:16] = np.eye(16)
    for side, b in enumerate((0, -1, 1)):
        for place, a in enumerate((0, -1, 1)):
            start = 16 + 36 * place
            values = from_modes @ near[a, b]
            if a == 0 and b == 0:
                values = values - np.diag(SCALE * (3.0 - smooth) * norm)
            mix[side, start : start + 20] = near[a, b]
            for k in range(16):
                mix[side, start + 20 + k] = values[(36 + k) % 16]
    wide = np.concatenate([np.tile(mix[i], (1, 8)) for i in range(3)], axis=1).astype(np.float32)
    high, low = halves(wide)
    mix_k = np.concatenate([high, high, low], axis=0)
    weights = np.zeros((52, 128), np.float32)
    for k in range(16):
        weights[k, k] = 3.0 * SCALE * smooth[k]
        weights[16 + k, k] = -SCALE
    for e in range(EDGES):
        weights[32 + e, 16 + e] = 3.0
    spread = np.zeros((128, 256), np.float32)
    for k in range(16):
        for j in range(16):
            m, n, mm, nn = k // 4, k % 4, j // 4, j % 4
            for p in (m + mm, abs(m - mm)):
                for q in (n + nn, abs(n - nn)):
                    spread[7 * p + q, 16 * k + j] += 0.25
    return mix_k, np.repeat(weights, 8, axis=0), np.concatenate([spread, spread]).astype(BF16)


def iota(shape, dim):
    return lax.broadcasted_iota(jnp.int32, shape, dim)


def split(value):
    high = value.astype(BF16).astype(F32)
    return high, value - high


def lane_totals(value):
    high, low = split(value)
    both = jnp.concatenate([high, low], axis=1).astype(BF16)
    return jnp.dot(both, jnp.ones((256, 128), BF16), preferred_element_type=F32)


def prolonged(groups, stream_table, wall_table):
    stacked = jnp.concatenate(groups + [jnp.zeros((8, 128), F32)], axis=0)
    high, low = split(stacked)
    operand = jnp.concatenate([high + pltpu.roll(low, 64, 1), high], axis=1).astype(BF16)
    mixed = jnp.dot(operand, wall_table, preferred_element_type=F32)
    high, low = split(mixed)
    operand = jnp.concatenate([high, low, high, jnp.zeros_like(high)], axis=0).astype(BF16)
    return jnp.dot(stream_table, operand, preferred_element_type=F32)


def tile16(value):
    alike = jnp.where(iota((256, 128), 0) % 16 == iota((256, 128), 1) % 16, 1.0, 0.0).astype(BF16)
    high, low = split(value)
    both = jnp.concatenate([high, low], axis=1).astype(BF16)
    return jnp.dot(both, alike, preferred_element_type=F32)


def strip(i):
    return pl.ds(pl.multiple_of(i * 8, 8), 8)


def kernel(
    rhs_hbm, diag_hbm, inv_hbm, slot_hbm, slots_hbm, phi_hbm, psi_hbm, sk_hbm, wk_hbm, mix_hbm, weights_hbm, spread_hbm,
    base_hbm, resid_hbm, mine_out,
    ext, gm, d9, x, x2, u, first, res, py, inv, phi, psi, sk, wk, mix, weights, spread, slots,
    colsend, colrecv, corners, hcolsend, hcolrecv, hcorners, hrows,
    rows, st, drow, dst, qst, qpack, dpack, cz, cw, dbuf, qbuf, yw0, yw1, onehot, block, diag_modes, slot,
    load_sem, msend, mrecv, asend, arecv, store_sem,
):
    s = lax.axis_index("stream")
    w = lax.axis_index("wall")
    me = s * NW + w
    ya, xl = s % 4, s // 4
    xh, za, core = w // 16, (w // 2) % 8, w % 2
    xa = xh * 2 + xl
    up, down = (s + NS - 1) % NS, (s + 1) % NS
    left, right = (w + NW - 1) % NW, (w + 1) % NW

    def stream_mates(act):
        for d in (2, 3, 1, 0):
            for flip in (1, 0):
                if d or flip:
                    act(((xl if flip == 0 else 1 - xl) * 4 + (ya + d) % 4, w))

    def wall_mates(act):
        for d in (4, 5, 3, 6, 2, 7, 1, 0):
            for flip in (1, 0):
                for other in (1, 0):
                    if d or flip or other:
                        x_part = (xh if flip == 0 else 1 - xh) * 16
                        act((s, x_part + ((za + d) % 8) * 2 + (core if other == 0 else 1 - core)))

    def column_mates(act):
        for d in (4, 5, 3, 6, 2, 7, 1, 0):
            for other in (1, 0):
                if d or other:
                    act((s, xh * 16 + ((za + d) % 8) * 2 + (core if other == 0 else 1 - core)))

    def across(act):
        act((s, (1 - xh) * 16 + za * 2 + core))

    barrier = pltpu.get_barrier_semaphore()

    def greet(to):
        pl.semaphore_signal(barrier, inc=1, device_id=to, device_id_type=MESH)

    column_mates(greet)
    stream_mates(greet)
    across(greet)
    for to in [(up, left), (up, right), (down, left), (down, right), (s, left), (s, right)]:
        greet(to)

    own = ext.at[:, pl.ds(8, CX), pl.ds(0, CY)]
    loads = [
        pltpu.make_async_copy(src, dst, load_sem.at[i])
        for i, (src, dst) in enumerate(
            [
                (rhs_hbm, own.at[0]),
                (phi_hbm.at[pl.ds(0, 3 * CX)], phi.at[pl.ds(0, 3 * CX)]),
                (psi_hbm, psi),
                (diag_hbm, own.at[1]),
                (phi_hbm.at[pl.ds(3 * CX, 3 * CX)], phi.at[pl.ds(3 * CX, 3 * CX)]),
                (slot_hbm, slot),
                (slots_hbm, slots),
                (inv_hbm, inv),
                (sk_hbm, sk),
                (wk_hbm, wk),
                (mix_hbm, mix),
                (weights_hbm, weights),
                (spread_hbm, spread),
            ]
        )
    ]
    for load in loads:
        load.start()

    lane = iota((8, 128), 1)
    sub = iota((8, 128), 0)
    lane16 = iota((16, 128), 1)
    lane1 = iota((1, 128), 1)

    def mode_sums(load, count):
        def body(step, sums):
            sums = list(sums)
            for i in range(4):
                f = load(step * 4 + i)
                sums[0] = sums[0] + f
                for m in range(count - 1):
                    t = phi[pl.ds(pl.multiple_of(m * CX + (step * 4 + i) * 8, 8), 8), :]
                    sums[m + 1] = sums[m + 1] + f * jnp.concatenate([t] * 6, axis=1)
            return tuple(sums)

        return lax.fori_loop(0, CX // 32, body, (jnp.zeros((8, CY), F32),) * count)

    def fold(value):
        total = value[:, 0:128]
        for t in range(1, 6):
            total = total + value[:, 128 * t : 128 * t + 128]
        return total

    def mode_parts(sums, count):
        return [fold(v if n == 0 else v * psi[n : n + 1, :]) for v in sums for n in range(count)]

    def gathered(parts, period):
        totals = lane_totals(jnp.concatenate(parts, axis=0))
        shape = totals.shape
        keep = iota(shape, 0) // 8 == iota(shape, 1) % period
        return jnp.sum(jnp.where(keep, totals, 0.0), axis=0, keepdims=True)

    def pack(ref):
        to_left = jnp.zeros((16, 128), F32)
        to_right = jnp.zeros((16, 128), F32)
        for k in range(16):
            a = jnp.where(lane16 < 8, ref[8 + 16 * k : 24 + 16 * k, 0:128], 0.0)
            b = jnp.where(lane16 >= 120, ref[8 + 16 * k : 24 + 16 * k, CY - 128 : CY], 0.0)
            to_left = to_left + (pltpu.roll(a, 8 * k, 1) if k else a)
            shift = (8 * k + 8) % 128
            to_right = to_right + (pltpu.roll(b, shift, 1) if shift else b)
        return to_left, to_right

    def unpack(from_right, from_left, k):
        a = pltpu.roll(from_right, 128 - 8 * k, 1) if k else from_right
        shift = (120 - 8 * k) % 128
        b = pltpu.roll(from_left, shift, 1) if shift else from_left
        return jnp.where(lane16 < 8, a, jnp.where(lane16 >= 120, b, 0.0))

    def corner(from_right, from_left):
        return jnp.where(lane < 8, from_right, jnp.where(lane >= 120, from_left, 0.0))

    def to_neighbours(which, pairs):
        targets = [(up, w), (down, w), (s, left), (s, right), (up, left), (up, right), (down, left), (down, right)]
        return [
            pltpu.make_async_remote_copy(
                src_ref=src, dst_ref=dst, send_sem=msend.at[which, i], recv_sem=mrecv.at[which, i],
                device_id=to, device_id_type=MESH,
            )
            for i, ((src, dst), to) in enumerate(zip(pairs, targets, strict=True))
        ]

    def sender(index, src, dst):
        def act(to):
            pltpu.make_async_remote_copy(
                src_ref=src, dst_ref=dst, send_sem=asend.at[index], recv_sem=arecv.at[index],
                device_id=to, device_id_type=MESH,
            ).start()

        return act

    def send(index, mates, src, dst):
        mates(sender(index, src, dst))
        pltpu.make_async_copy(src, dst, arecv.at[index]).start()

    def send_row(which):
        send(2 * which, stream_mates, rows.at[which, pl.ds(0, 1)], st.at[which, pl.ds(s, 1)])

    def forward_row(which, mates, dst):
        wait_all(2 * which, st.at[which])
        total = jnp.sum(st[which], axis=0, keepdims=True)
        rows[3 + which] = jnp.broadcast_to(total, (8, 128))
        send(2 * which + 1, mates, rows.at[3 + which, pl.ds(0, 1)], dst)

    def side_by_side(buf, per, width, used, r):
        total = jnp.zeros((1, 128), F32)
        for a in range(per * r, min(per * r + per, NS)):
            value = jnp.broadcast_to(jnp.where(lane1 < used, buf[a], 0.0), (8, 128))
            total = total + (pltpu.roll(value, width * (a % per), 1) if a % per else value)[0:1]
        return total

    def taken_apart(buf, per, width):
        parts = []
        for a in range(NS):
            value = buf[a // per]
            parts.append(pltpu.roll(value, 128 - width * (a % per), 1) if a % per else value)
        return jnp.concatenate(parts, axis=0)

    def wait_all(index, buf):
        pltpu.make_async_copy(buf, buf, arecv.at[index]).wait()

    def wait_sent(index, part):
        pltpu.make_async_copy(part, part, asend.at[index]).wait()

    def partial_values(c, tiled):
        at = iota((32, DEVICES), 0) + 32 * s
        pick = jnp.where(slots[...] == at, 1.0, 0.0)
        high, low = split(c)
        pick2 = jnp.concatenate([pick, pick], axis=1).astype(BF16)
        both = jnp.concatenate([high, low], axis=0).astype(BF16)
        ordered = jnp.dot(pick2, both, preferred_element_type=F32)
        if not tiled:
            ordered = tile16(ordered)
        keep = iota((32, 128), 1) // 16 == iota((32, 128), 0) % 8
        ordered = jnp.where(keep, ordered, 0.0)
        total = jnp.zeros((128, 128), F32)
        for q in range(4):
            row = jnp.sum(ordered[8 * q : 8 * q + 8], axis=0, keepdims=True)
            total = total + inv[:, 128 * q : 128 * q + 128] * row
        sums = lane_totals(total)
        return jnp.sum(jnp.where(iota((128, 128), 0) == iota((128, 128), 1), sums, 0.0), axis=0, keepdims=True)

    def coefficients(which, a, b, place):
        mine = slot[a * NW + b]
        row = (yw1 if which else yw0)[pl.ds(lax.shift_right_logical(mine, 3), 1), :]
        shift = lax.bitwise_and(16 * place + 128 - 16 * lax.bitwise_and(mine, 7), 127)
        rolled = pltpu.roll(jnp.broadcast_to(row, (8, 128)), shift, 1)
        return jnp.where(lane // 16 == place, rolled, 0.0)

    tail_lane = iota((8, 128), 1)

    def tail_valid(depth):
        inner = jnp.logical_and(tail_lane < depth, w < NW - 1)
        outer = jnp.logical_and(tail_lane >= 128 - depth, w > 0)
        return jnp.logical_or(inner, outer)

    def masked(value, valid):
        return jnp.concatenate([value[:, 0:CY], jnp.where(valid, value[:, CY:], 0.0)], axis=1)

    wide_sub = iota((8, COLS), 0)

    def hsum(v):
        return v + pltpu.roll(v, 1, 1) + pltpu.roll(v, COLS - 1, 1)

    def vsum(before, here, after):
        above = pltpu.roll(jnp.where(wide_sub == 7, before, here), 1, 0)
        below = pltpu.roll(jnp.where(wide_sub == 0, after, here), 7, 0)
        return here + above + below

    def rows_at(i):
        return slice(8 * i, 8 * i + 8)

    def stencil_strips(load, use):
        zero = jnp.zeros((8, COLS), F32)
        value = load(0)
        before, now = zero, hsum(value)
        for i in range(STRIPS):
            following = load(i + 1) if i + 1 < STRIPS else None
            after = zero if following is None else hsum(following)
            use(i, value, vsum(before, now, after))
            before, now, value = now, after, following

    def inside(i, value, valid):
        value = masked(value, valid)
        if i == 0:
            return jnp.where(wide_sub >= 4, value, 0.0)
        if i == STRIPS - 1:
            return jnp.where(wide_sub < 4, value, 0.0)
        return value

    def chebyshev(g):
        valid = tail_valid(4)
        old, new = x, x2
        for k, (a, b) in enumerate(sweep_factors()):

            def load(i, k=k, old=old):
                return g[rows_at(i), :] * (1.0 / (3.0 * MIDDLE)) if k == 0 else old[rows_at(i), :]

            def use(i, value, total, k=k, a=a, b=b, new=new):
                e = g[rows_at(i), :] - d9[rows_at(i), :] * value + total
                step = a * (value if k == 0 else u[rows_at(i), :]) + (b / 3.0) * e
                step = inside(i, step, valid)
                if k < DEG - 1:
                    u[rows_at(i), :] = step
                new[rows_at(i), :] = value + step

            stencil_strips(load, use)
            old, new = new, old

    for load in loads[:3]:
        load.wait()
    sums = mode_sums(lambda i: ext[0, strip(i + 1), 0:CY], 4)
    first_residual = gathered(mode_parts(sums, 4), 16) * SCALE
    rows[0] = jnp.broadcast_to(jnp.where(lane1 // 16 == s, first_residual, 0.0), (8, 128))
    loads[3].wait()
    for f in range(2):
        a, b = pack(ext.at[f])
        colsend[0, 16 * f : 16 * f + 16] = a
        colsend[1, 16 * f : 16 * f + 16] = b

    pl.semaphore_wait(barrier, 7 + 15 + 1 + 6)
    top, bottom = pl.ds(8, 8), pl.ds(CX, 8)
    west, east, body_lanes = pl.ds(0, 128), pl.ds(CY - 128, 128), pl.ds(0, CY)
    margins = to_neighbours(
        0,
        [
            (ext.at[:, top, body_lanes], ext.at[:, pl.ds(ROWS - 8, 8), body_lanes]),
            (ext.at[:, bottom, body_lanes], ext.at[:, pl.ds(0, 8), body_lanes]),
            (colsend.at[0], colrecv.at[0]),
            (colsend.at[1], colrecv.at[1]),
            (ext.at[:, top, west], corners.at[3]),
            (ext.at[:, top, east], corners.at[2]),
            (ext.at[:, bottom, west], corners.at[1]),
            (ext.at[:, bottom, east], corners.at[0]),
        ],
    )
    send_row(0)
    for copy in margins:
        copy.start()
    loads[4].wait()
    sums = mode_sums(lambda i: ext[1, strip(i + 1), 0:CY], 7)
    drow[0] = gathered(mode_parts(sums, 7), 128)
    send(6, stream_mates, drow, dst.at[pl.ds(s, 1)])
    for load in loads[5:]:
        load.wait()
    at = iota((128, DEVICES), 0)
    group_of = lax.shift_right_logical(slots[...], 3)
    onehot[...] = jnp.where(jnp.logical_and(group_of == at % 32, at < 64), 1.0, 0.0).T
    block[...] = jnp.where(lax.bitwise_and(slots[...], 7) == at // 16, 1.0, 0.0).T
    forward_row(0, column_mates, cz.at[pl.ds(w % 16, 1)])
    for copy in margins:
        copy.wait_recv()

    valid4 = tail_valid(4)
    for f in range(2):
        from_right = colrecv[0, 16 * f : 16 * f + 16]
        from_left = colrecv[1, 16 * f : 16 * f + 16]
        for k in range(16):
            ext[f, 8 + 16 * k : 24 + 16 * k, CY:COLS] = unpack(from_right, from_left, k)
        ext[f, 0:8, CY:COLS] = corner(corners[1, f], corners[0, f])
        ext[f, ROWS - 8 : ROWS, CY:COLS] = corner(corners[3, f], corners[2, f])

    def prepare(i, carry):
        gm[strip(i), :] = masked(ext[0, strip(i), :], valid4)
        d9[strip(i), :] = ext[1, strip(i), :] * 3.0 + 9.0
        return carry

    lax.fori_loop(0, STRIPS, prepare, 0, unroll=True)
    gm[0:8, :] = jnp.where(wide_sub >= 4, gm[0:8, :], 0.0)
    gm[ROWS - 8 : ROWS, :] = jnp.where(wide_sub < 4, gm[ROWS - 8 : ROWS, :], 0.0)
    chebyshev(gm)

    wait_all(1, cz)
    send(10, across, cz, cw.at[pl.ds(pl.multiple_of(xh * 16, 16), 16)])

    u_sums = mode_sums(lambda i: x[strip(i + 1), 0:CY], 4)
    w_sums = mode_sums(lambda i: x[strip(i + 1), 0:CY] * d9[strip(i + 1), 0:CY], 4)
    parts = mode_parts(u_sums, 4) + mode_parts(w_sums, 4)
    for edge, here in ((x[8:16, 0:CY], sub == 0), (x[CX : CX + 8, 0:CY], sub == 7)):
        parts += [jnp.where(here, p, 0.0) for p in mode_parts([edge], 4)]
    parts += [jnp.where(lane == 0, v[:, 0:128], 0.0) for v in u_sums]
    parts += [jnp.where(lane == 127, v[:, CY - 128 : CY], 0.0) for v in u_sums]
    for edge, at_row in ((x[8:16, :], 0), (x[CX : CX + 8, :], 7)):
        for tile, at_lane in ((edge[:, 0:128], 0), (edge[:, CY - 128 : CY], 127)):
            parts.append(jnp.where(jnp.logical_and(sub == at_row, lane == at_lane), tile, 0.0))
    totals = lane_totals(jnp.concatenate(parts, axis=0)) * weights[...]
    moments = jnp.sum(totals, axis=0, keepdims=True)
    moments = moments + jnp.where(lane1 < 16, first_residual, 0.0)
    qpack[3] = moments
    send(8, stream_mates, qpack.at[pl.ds(3, 1)], qst.at[pl.ds(s, 1)])

    wait_all(10, cw)
    spread_rows = jnp.concatenate([cw[...]] * NS, axis=0)
    own_lanes = iota((DEVICES, 128), 1) // 16 == iota((DEVICES, 128), 0) // NW
    rows[1] = jnp.broadcast_to(partial_values(jnp.where(own_lanes, spread_rows, 0.0), False), (8, 128))
    send_row(1)
    wait_all(6, dst)
    for r in range(4):
        dpack[r] = side_by_side(dst, 2, 64, 49, r)
    send(7, wall_mates, dpack, dbuf.at[:, pl.ds(w, 1), :])

    a, b = pack(x)
    hcolsend[0] = a
    hcolsend[1] = b
    halos = to_neighbours(
        1,
        [
            (x.at[top, body_lanes], hrows.at[1]),
            (x.at[bottom, body_lanes], hrows.at[0]),
            (hcolsend.at[0], hcolrecv.at[0]),
            (hcolsend.at[1], hcolrecv.at[1]),
            (x.at[top, west], hcorners.at[3]),
            (x.at[top, east], hcorners.at[2]),
            (x.at[bottom, west], hcorners.at[1]),
            (x.at[bottom, east], hcorners.at[0]),
        ],
    )
    for copy in halos:
        copy.start()

    wait_all(8, qst)
    for r in range(3):
        qpack[r] = side_by_side(qst, 3, 40, 36, r)
    send(9, wall_mates, qpack.at[pl.ds(0, 3)], qbuf.at[:, pl.ds(w, 1), :])
    forward_row(1, wall_mates, yw0.at[pl.ds(w, 1)])

    for copy in halos:
        copy.wait_recv()
    valid8 = tail_valid(8)

    def place(i, carry):
        first[strip(i), 0:CY] = x[strip(i), 0:CY]
        return carry

    lax.fori_loop(1, STRIPS - 1, place, 0, unroll=True)
    first[0:8, 0:CY] = hrows[0]
    first[ROWS - 8 : ROWS, 0:CY] = hrows[1]
    for k in range(16):
        edge = unpack(hcolrecv[0], hcolrecv[1], k)
        first[8 + 16 * k : 16 + 16 * k, CY:COLS] = jnp.where(valid8, edge[0:8], 0.0)
        first[16 + 16 * k : 24 + 16 * k, CY:COLS] = jnp.where(valid8, edge[8:16], 0.0)
    first[0:8, CY:COLS] = jnp.where(valid8, corner(hcorners[1], hcorners[0]), 0.0)
    first[ROWS - 8 : ROWS, CY:COLS] = jnp.where(valid8, corner(hcorners[3], hcorners[2]), 0.0)

    wait_all(7, dbuf)
    diag = jnp.where(iota((DEVICES, 128), 1) < 64, taken_apart(dbuf, 2, 64), 0.0)
    high, low = split(diag)
    both = jnp.concatenate([high, low], axis=1).astype(BF16)
    diag_modes[...] = jnp.dot(both, spread[...], preferred_element_type=F32) * (-SCALE)
    wait_all(9, qbuf)
    known = taken_apart(qbuf, 3, 40)
    wait_all(3, yw0)

    high, low = split(yw0[...])
    both = jnp.concatenate([high, low, jnp.zeros((64, 128), F32)], axis=0).astype(BF16)
    values = jnp.dot(onehot[...].astype(BF16), both, preferred_element_type=F32) * block[...]
    values = tile16(values)
    lanes = iota((DEVICES, 128), 1)
    near = jnp.where(lanes < 36, known, jnp.where(lanes < 52, values, 0.0))
    near = jnp.where(lanes >= 16, near, 0.0)
    mixed = jnp.where(lanes < 16, known, near)
    mixed = mixed + pltpu.roll(jnp.concatenate([near[-NW:], near[:-NW]], axis=0), 36, 1)
    mixed = mixed + pltpu.roll(jnp.concatenate([near[NW:], near[:NW]], axis=0), 72, 1)
    high, low = split(mixed)
    both = jnp.concatenate([high, low, high], axis=1).astype(BF16)
    sides = jnp.dot(both, mix[...], preferred_element_type=F32)
    wall_row = iota((DEVICES, 128), 0) % NW
    second_residual = sides[:, 0:128]
    second_residual = second_residual + jnp.where(wall_row > 0, pltpu.roll(sides[:, 128:256], 1, 0), 0.0)
    second_residual = second_residual + jnp.where(
        wall_row < NW - 1, pltpu.roll(sides[:, 256:384], DEVICES - 1, 0), 0.0
    )
    products = [part for h in range(2) for part in split(values * diag_modes[:, 128 * h : 128 * h + 128])]
    both = jnp.concatenate(products, axis=1).astype(BF16)
    at = iota((512, 128), 0)
    summed = jnp.where(8 * (at // 256) + (at % 128) // 16 == iota((512, 128), 1) % 16, 1.0, 0.0)
    second_residual = second_residual + jnp.dot(both, summed.astype(BF16), preferred_element_type=F32)
    rows[2] = jnp.broadcast_to(partial_values(second_residual, True), (8, 128))
    send_row(2)

    groups = []
    for a in (up, s, down):
        group = coefficients(0, a, w, 1)
        group = group + jnp.where(w > 0, coefficients(0, a, left, 0), 0.0)
        group = group + jnp.where(w < NW - 1, coefficients(0, a, right, 2), 0.0)
        groups.append(jnp.where((lane % 16) // 4 == sub, group, 0.0))
    py[...] = prolonged(groups, sk[...], wk[...])
    forward_row(2, wall_mates, yw1.at[pl.ds(w, 1)])

    def first_at(i):
        value = first[rows_at(i), :] + py[rows_at(i), :] * (1.0 / 3.0)
        first[rows_at(i), :] = value
        return value

    def residual(i, value, total):
        res[rows_at(i), :] = inside(i, gm[rows_at(i), :] - d9[rows_at(i), :] * value + total, valid4)

    stencil_strips(first_at, residual)

    resid_copy = pltpu.make_async_copy(res.at[pl.ds(8, CX), pl.ds(0, CY)], resid_hbm, store_sem.at[0])
    resid_copy.start()
    for copy in halos:
        copy.wait_send()
    chebyshev(res)

    def add_local(i, carry):
        first[strip(i), 0:CY] = (first[strip(i), 0:CY] + x[strip(i), 0:CY]) * 3.0
        return carry

    lax.fori_loop(1, STRIPS - 1, add_local, 0, unroll=True)
    base_copy = pltpu.make_async_copy(first.at[pl.ds(8, CX), pl.ds(0, CY)], base_hbm, store_sem.at[1])
    base_copy.start()
    wait_all(5, yw1)
    own_row = (lane % 16) // 4 == sub
    mine_out[...] = jnp.where(own_row, coefficients(1, s, w, 1), 0.0)
    for which, part in enumerate((cz.at[pl.ds(0, 15)], yw0.at[pl.ds(0, NW - 1)], yw1.at[pl.ds(0, NW - 1)])):
        wait_sent(2 * which, st.at[which, pl.ds(0, NS - 1)])
        wait_sent(2 * which + 1, part)
    wait_sent(10, cz)
    wait_sent(6, dst.at[pl.ds(0, NS - 1)])
    wait_sent(7, dbuf.at[:, pl.ds(0, NW - 1), :])
    wait_sent(8, qst.at[pl.ds(0, NS - 1)])
    wait_sent(9, qbuf.at[:, pl.ds(0, NW - 1), :])
    for copy in margins:
        copy.wait_send()
    resid_copy.wait()
    base_copy.wait()


PIECES = 4


def finish(
    base_hbm, resid_hbm, mine_hbm, stream_hbm, wall_hbm, out_hbm, resid_out,
    base, resid, mine, stream_table, wall_table, small_sem, load_sem, store_sem,
):
    small = [
        pltpu.make_async_copy(src, dst, small_sem.at[i])
        for i, (src, dst) in enumerate([(mine_hbm, mine), (wall_hbm, wall_table), (stream_hbm, stream_table)])
    ]
    for copy in small:
        copy.start()
    parts = [pl.ds(i * (CX // PIECES), CX // PIECES) for i in range(PIECES)]
    loads, stores = [], []
    for k, (src, here, dst) in enumerate(((resid_hbm, resid, resid_out), (base_hbm, base, out_hbm))):
        loads.append([pltpu.make_async_copy(src.at[p], here.at[p], load_sem.at[k, i]) for i, p in enumerate(parts)])
        stores.append([pltpu.make_async_copy(here.at[p], dst.at[p], store_sem.at[k, i]) for i, p in enumerate(parts)])
    for copy in loads[0] + loads[1]:
        copy.start()
    for copy in small:
        copy.wait()
    none = jnp.zeros((8, 128), F32)
    coarse = prolonged([none, mine[...], none], stream_table[...], wall_table[...])
    for i in range(PIECES):
        loads[0][i].wait()
        stores[0][i].start()
    for i in range(PIECES):
        rows = slice(i * (CX // PIECES), (i + 1) * (CX // PIECES))
        loads[1][i].wait()
        base[rows, :] = base[rows, :] + coarse[rows, :]
        stores[1][i].start()
    for copy in stores[0] + stores[1]:
        copy.wait()


def local(right_side, diagonal, coarse_inverse, owner_slot):
    phi_lanes, psi_rows, stream_k, own_k, wall_k = tables()
    mix_k, moment_weights, spread_k = coarse_tables()
    field = jax.ShapeDtypeStruct((CX, CY), F32)
    anywhere = pl.BlockSpec(memory_space=pl.ANY)
    in_vmem = pl.BlockSpec(memory_space=pltpu.VMEM)
    vmem = pltpu.VMEM
    dma = pltpu.SemaphoreType.DMA
    work = vmem((ROWS, COLS), F32)
    base, resid, mine = pl.pallas_call(
        kernel,
        out_shape=(field, field, jax.ShapeDtypeStruct((8, 128), F32)),
        in_specs=[anywhere] * 12,
        out_specs=(anywhere, anywhere, in_vmem),
        scratch_shapes=[
            vmem((2, ROWS, COLS), F32), work, work, work, work, work, work, work, work,
            vmem((128, 512), F32), vmem((6 * CX, 128), F32), vmem((8, CY), F32),
            vmem((ROWS, 128), BF16), vmem((256, COLS), BF16),
            vmem((384, 384), BF16), vmem((416, 128), F32), vmem((256, 256), BF16), vmem((1, DEVICES), jnp.int32),
            vmem((2, 32, 128), F32), vmem((2, 32, 128), F32), vmem((4, 2, 8, 128), F32),
            vmem((2, 16, 128), F32), vmem((2, 16, 128), F32), vmem((4, 8, 128), F32), vmem((2, 8, CY), F32),
            vmem((6, 8, 128), F32), vmem((3, NS, 128), F32), vmem((1, 1, 128), F32), vmem((NS, 1, 128), F32),
            vmem((NS, 1, 128), F32), vmem((4, 1, 128), F32), vmem((4, 1, 128), F32), vmem((16, 128), F32), vmem((NW, 128), F32), vmem((4, NW, 128), F32),
            vmem((3, NW, 128), F32), vmem((NW, 128), F32), vmem((NW, 128), F32),
            vmem((DEVICES, 128), F32), vmem((DEVICES, 128), F32), vmem((DEVICES, 256), F32),
            pltpu.SMEM((DEVICES,), jnp.int32),
            dma((13,)), dma((2, 8)), dma((2, 8)), dma((11,)), dma((11,)), dma((2,)),
        ],
        compiler_params=pltpu.CompilerParams(
            collective_id=0, has_side_effects=True, vmem_limit_bytes=60 * 1024 * 1024
        ),
        cost_estimate=pl.CostEstimate(flops=100_000_000, bytes_accessed=4_000_000, transcendentals=0),
    )(
        right_side, diagonal, coarse_inverse, owner_slot, owner_slot.reshape(1, DEVICES),
        phi_lanes, psi_rows, stream_k, wall_k, mix_k, moment_weights, spread_k,
    )
    return pl.pallas_call(
        finish,
        out_shape=(field, field),
        in_specs=[anywhere] * 5,
        out_specs=(anywhere, anywhere),
        scratch_shapes=[
            vmem((CX, CY), F32), vmem((CX, CY), F32), vmem((8, 128), F32), vmem((CX, 128), BF16), vmem((256, CY), BF16),
            dma((3,)), dma((2, PIECES)), dma((2, PIECES)),
        ],
        compiler_params=pltpu.CompilerParams(vmem_limit_bytes=60 * 1024 * 1024),
        cost_estimate=pl.CostEstimate(flops=50_000_000, bytes_accessed=3_000_000, transcendentals=0),
    )(base, resid, mine, own_k, np.ascontiguousarray(wall_k[:, :CY]))


def solution(mesh):
    placed = (P("stream", "wall"), P("stream", "wall"), P("wall", "stream"), P())
    return jax.shard_map(
        local,
        mesh=mesh,
        in_specs=placed,
        out_specs=(P("stream", "wall"), P("stream", "wall")),
        check_vma=False,
    )
```

```python
import math

import jax
import jax.numpy as jnp
import numpy as np
from jax import lax
from jax.experimental import pallas as pl
from jax.experimental.pallas import tpu as pltpu
from jax.sharding import PartitionSpec as P

MESH = pl.DeviceIdType.MESH
NS, NW = 8, 32
DEVICES = NS * NW
CX, CY = 256, 768
DEG = 4
ROWS, COLS = CX + 16, CY + 128
STRIPS = ROWS // 8
MIDDLE = (5.0 + 0.05) / 2.0
SPREAD = (5.0 - 0.05) / 2.0
SCALE = 1.0 / math.sqrt(CX * CY)
F32, BF16 = jnp.float32, jnp.bfloat16


def sweep_factors():
    quotient = MIDDLE / SPREAD
    factor = 1.0 / quotient
    pairs = []
    for _ in range(DEG):
        following = 1.0 / (2.0 * quotient - factor)
        pairs.append((following * factor, 2.0 * following / SPREAD))
        factor = following
    return pairs


def halves(table):
    high = table.astype(BF16)
    return high, (table - high.astype(np.float32)).astype(BF16)


def tables():
    phi = np.cos(np.pi * (np.arange(CX) + 0.5)[None, :] * np.arange(7)[:, None] / CX)
    psi = np.cos(np.pi * (np.arange(CY) + 0.5)[None, :] * np.arange(7)[:, None] / CY)
    phi_lanes = np.repeat(phi[1:].reshape(6 * CX, 1), 128, axis=1).astype(np.float32)
    psi_rows = np.concatenate([psi, psi[:1]]).astype(np.float32)
    stream = np.zeros((ROWS, 32), np.float32)
    stream[0:8, 0:4] = phi[:4, CX - 8 :].T
    stream[8 : 8 + CX, 8:12] = phi[:4].T
    stream[8 + CX :, 16:20] = phi[:4, :8].T
    high, low = halves(stream)
    stream_k = np.concatenate([high, high, low, np.zeros_like(high)], axis=1)
    own_k = stream_k[8 : 8 + CX]
    wall = np.zeros((64, COLS), np.float32)
    for m in range(4):
        wall[4 * m : 4 * m + 4, COLS - 64 :] = psi[:4, CY - 64 :]
        wall[16 + 4 * m : 20 + 4 * m, :CY] = psi[:4]
        wall[32 + 4 * m : 36 + 4 * m, CY : CY + 64] = psi[:4, :64]
    high, low = halves(wall)
    wall_k = np.concatenate([high, high, low, np.zeros_like(high)], axis=0)
    return phi_lanes, psi_rows, stream_k, own_k, wall_k


EDGES = 20


def coarse_tables():
    phi = np.cos(np.pi * (np.arange(CX) + 0.5)[None, :] * np.arange(4)[:, None] / CX)
    psi = np.cos(np.pi * (np.arange(CY) + 0.5)[None, :] * np.arange(4)[:, None] / CY)
    lam = 1.0 + 2.0 * np.cos(np.pi * np.arange(4) / CX)
    mu = 1.0 + 2.0 * np.cos(np.pi * np.arange(4) / CY)
    p0, p1, q0, q1 = phi[:, 0], phi[:, -1], psi[:, 0], psi[:, -1]
    nx, ny = (phi**2).sum(1), (psi**2).sum(1)
    near = {(a, b): np.zeros((EDGES, 4, 4)) for a in (-1, 0, 1) for b in (-1, 0, 1)}
    from_modes = np.zeros((4, 4, EDGES))
    corner = {(0, 0): 16, (0, 1): 17, (1, 0): 18, (1, 1): 19}
    ps, qs = (p0, p1), (q0, q1)
    for n in range(4):
        for side in (0, 1):
            row = 4 * side + n
            near[0, 0][row, :, n] -= mu[n] * ps[side]
            near[1 if side == 0 else -1, 0][row, :, n] += mu[n] * ps[1 - side]
            from_modes[:, n, row] += ps[side] * ny[n]
    for m in range(4):
        for side in (0, 1):
            row = 8 + 4 * side + m
            near[0, 0][row, m, :] -= lam[m] * qs[side]
            near[0, 1 if side == 0 else -1][row, m, :] += lam[m] * qs[1 - side]
            from_modes[m, :, row] += qs[side] * nx[m]
    for (i, j), row in corner.items():
        a, b = (1 if i == 0 else -1), (1 if j == 0 else -1)
        near[0, 0][row] += np.outer(ps[i], qs[j])
        near[a, 0][row] -= np.outer(ps[1 - i], qs[j])
        near[0, b][row] -= np.outer(ps[i], qs[1 - j])
        near[a, b][row] += np.outer(ps[1 - i], qs[1 - j])
        from_modes[:, :, row] += np.outer(ps[i], qs[j])
    near = {key: value.reshape(EDGES, 16) * (SCALE / 3.0) for key, value in near.items()}
    from_modes = from_modes.reshape(16, EDGES)
    smooth = np.outer(lam, mu).reshape(16) / 3.0
    norm = np.outer(nx, ny).reshape(16)
    mix = np.zeros((3, 128, 16))
    mix[0, 0:16] = np.eye(16)
    for side, b in enumerate((0, -1, 1)):
        for place, a in enumerate((0, -1, 1)):
            start = 16 + 36 * place
            values = from_modes @ near[a, b]
            if a == 0 and b == 0:
                values = values - np.diag(SCALE * (3.0 - smooth) * norm)
            mix[side, start : start + 20] = near[a, b]
            for k in range(16):
                mix[side, start + 20 + k] = values[(36 + k) % 16]
    wide = np.concatenate([np.tile(mix[i], (1, 8)) for i in range(3)], axis=1).astype(np.float32)
    high, low = halves(wide)
    mix_k = np.concatenate([high, high, low], axis=0)
    weights = np.zeros((52, 128), np.float32)
    for k in range(16):
        weights[k, k] = 3.0 * SCALE * smooth[k]
        weights[16 + k, k] = -SCALE
    for e in range(EDGES):
        weights[32 + e, 16 + e] = 3.0
    spread = np.zeros((128, 256), np.float32)
    for k in range(16):
        for j in range(16):
            m, n, mm, nn = k // 4, k % 4, j // 4, j % 4
            for p in (m + mm, abs(m - mm)):
                for q in (n + nn, abs(n - nn)):
                    spread[7 * p + q, 16 * k + j] += 0.25
    return mix_k, np.repeat(weights, 8, axis=0), np.concatenate([spread, spread]).astype(BF16)


def iota(shape, dim):
    return lax.broadcasted_iota(jnp.int32, shape, dim)


def split(value):
    high = value.astype(BF16).astype(F32)
    return high, value - high


def lane_totals(value):
    high, low = split(value)
    both = jnp.concatenate([high, low], axis=1).astype(BF16)
    return jnp.dot(both, jnp.ones((256, 128), BF16), preferred_element_type=F32)


def prolonged(groups, stream_table, wall_table):
    stacked = jnp.concatenate(groups + [jnp.zeros((8, 128), F32)], axis=0)
    high, low = split(stacked)
    operand = jnp.concatenate([high + pltpu.roll(low, 64, 1), high], axis=1).astype(BF16)
    mixed = jnp.dot(operand, wall_table, preferred_element_type=F32)
    high, low = split(mixed)
    operand = jnp.concatenate([high, low, high, jnp.zeros_like(high)], axis=0).astype(BF16)
    return jnp.dot(stream_table, operand, preferred_element_type=F32)


def tile16(value):
    alike = jnp.where(iota((256, 128), 0) % 16 == iota((256, 128), 1) % 16, 1.0, 0.0).astype(BF16)
    high, low = split(value)
    both = jnp.concatenate([high, low], axis=1).astype(BF16)
    return jnp.dot(both, alike, preferred_element_type=F32)


def strip(i):
    return pl.ds(pl.multiple_of(i * 8, 8), 8)


def kernel(
    rhs_hbm, diag_hbm, inv_hbm, slot_hbm, slots_hbm, phi_hbm, psi_hbm, sk_hbm, wk_hbm, mix_hbm, weights_hbm, spread_hbm,
    base_hbm, resid_hbm, mine_out,
    ext, gm, d9, x, x2, u, first, res, py, inv, phi, psi, sk, wk, mix, weights, spread, slots,
    colsend, colrecv, corners, hcolsend, hcolrecv, hcorners, hrows,
    rows, st, drow, dst, qst, qpack, dpack, cw, dbuf, qbuf, yw0, yw1, all2, onehot, block, diag_modes, slot,
    load_sem, msend, mrecv, asend, arecv, store_sem,
):
    s = lax.axis_index("stream")
    w = lax.axis_index("wall")
    me = s * NW + w
    ya, xl = s % 4, s // 4
    xh, za, core = w // 16, (w // 2) % 8, w % 2
    xa = xh * 2 + xl
    up, down = (s + NS - 1) % NS, (s + 1) % NS
    left, right = (w + NW - 1) % NW, (w + 1) % NW

    def around(k, n):
        return n // 2 + (k % 2) * ((k + 1) // 2) - (1 - k % 2) * (k // 2)

    def everyone(act):
        xa = xh * 2 + xl
        ys = [(ya + d) % 4 for d in (2, 3, 1, 0)]

        def some(k, count):
            z = (za + around(k // 4, 8)) % 8
            xx = (xa + around(k % 4, 4)) % 4
            base_s = (xx % 2) * 4
            base_w = (xx // 2) * 16 + z * 2
            for j in range(count):
                act((base_s + ys[j // 2], base_w + ((1 - core) if j % 2 == 0 else core)))

        def body(k, carry):
            some(k, 8)
            return carry

        lax.fori_loop(0, 31, body, 0)
        some(jnp.int32(31), 7)

    def stream_mates(act):
        for d in (2, 3, 1, 0):
            for flip in (1, 0):
                if d or flip:
                    act(((xl if flip == 0 else 1 - xl) * 4 + (ya + d) % 4, w))

    def wall_mates(act):
        for d in (4, 5, 3, 6, 2, 7, 1, 0):
            for flip in (1, 0):
                for other in (1, 0):
                    if d or flip or other:
                        x_part = (xh if flip == 0 else 1 - xh) * 16
                        act((s, x_part + ((za + d) % 8) * 2 + (core if other == 0 else 1 - core)))

    barrier = pltpu.get_barrier_semaphore()

    def greet(to):
        pl.semaphore_signal(barrier, inc=1, device_id=to, device_id_type=MESH)

    wall_mates(greet)
    stream_mates(greet)
    for to in [(up, left), (up, right), (down, left), (down, right)]:
        greet(to)

    own = ext.at[:, pl.ds(8, CX), pl.ds(0, CY)]
    loads = [
        pltpu.make_async_copy(src, dst, load_sem.at[i])
        for i, (src, dst) in enumerate(
            [
                (rhs_hbm, own.at[0]),
                (phi_hbm.at[pl.ds(0, 3 * CX)], phi.at[pl.ds(0, 3 * CX)]),
                (psi_hbm, psi),
                (diag_hbm, own.at[1]),
                (phi_hbm.at[pl.ds(3 * CX, 3 * CX)], phi.at[pl.ds(3 * CX, 3 * CX)]),
                (slot_hbm, slot),
                (slots_hbm, slots),
                (inv_hbm, inv),
                (sk_hbm, sk),
                (wk_hbm, wk),
                (mix_hbm, mix),
                (weights_hbm, weights),
                (spread_hbm, spread),
            ]
        )
    ]
    for load in loads:
        load.start()

    lane = iota((8, 128), 1)
    sub = iota((8, 128), 0)
    lane16 = iota((16, 128), 1)
    lane1 = iota((1, 128), 1)

    def mode_sums(load, count):
        def body(step, sums):
            sums = list(sums)
            for i in range(4):
                f = load(step * 4 + i)
                sums[0] = sums[0] + f
                for m in range(count - 1):
                    t = phi[pl.ds(pl.multiple_of(m * CX + (step * 4 + i) * 8, 8), 8), :]
                    sums[m + 1] = sums[m + 1] + f * jnp.concatenate([t] * 6, axis=1)
            return tuple(sums)

        return lax.fori_loop(0, CX // 32, body, (jnp.zeros((8, CY), F32),) * count)

    def fold(value):
        total = value[:, 0:128]
        for t in range(1, 6):
            total = total + value[:, 128 * t : 128 * t + 128]
        return total

    def mode_parts(sums, count):
        return [fold(v if n == 0 else v * psi[n : n + 1, :]) for v in sums for n in range(count)]

    def gathered(parts, period):
        totals = lane_totals(jnp.concatenate(parts, axis=0))
        shape = totals.shape
        keep = iota(shape, 0) // 8 == iota(shape, 1) % period
        return jnp.sum(jnp.where(keep, totals, 0.0), axis=0, keepdims=True)

    def pack(ref):
        to_left = jnp.zeros((16, 128), F32)
        to_right = jnp.zeros((16, 128), F32)
        for k in range(16):
            a = jnp.where(lane16 < 8, ref[8 + 16 * k : 24 + 16 * k, 0:128], 0.0)
            b = jnp.where(lane16 >= 120, ref[8 + 16 * k : 24 + 16 * k, CY - 128 : CY], 0.0)
            to_left = to_left + (pltpu.roll(a, 8 * k, 1) if k else a)
            shift = (8 * k + 8) % 128
            to_right = to_right + (pltpu.roll(b, shift, 1) if shift else b)
        return to_left, to_right

    def unpack(from_right, from_left, k):
        a = pltpu.roll(from_right, 128 - 8 * k, 1) if k else from_right
        shift = (120 - 8 * k) % 128
        b = pltpu.roll(from_left, shift, 1) if shift else from_left
        return jnp.where(lane16 < 8, a, jnp.where(lane16 >= 120, b, 0.0))

    def corner(from_right, from_left):
        return jnp.where(lane < 8, from_right, jnp.where(lane >= 120, from_left, 0.0))

    def to_neighbours(which, pairs):
        targets = [(up, w), (down, w), (s, left), (s, right), (up, left), (up, right), (down, left), (down, right)]
        return [
            pltpu.make_async_remote_copy(
                src_ref=src, dst_ref=dst, send_sem=msend.at[which, i], recv_sem=mrecv.at[which, i],
                device_id=to, device_id_type=MESH,
            )
            for i, ((src, dst), to) in enumerate(zip(pairs, targets, strict=True))
        ]

    def sender(index, src, dst):
        def act(to):
            pltpu.make_async_remote_copy(
                src_ref=src, dst_ref=dst, send_sem=asend.at[index], recv_sem=arecv.at[index],
                device_id=to, device_id_type=MESH,
            ).start()

        return act

    def send(index, mates, src, dst):
        mates(sender(index, src, dst))
        pltpu.make_async_copy(src, dst, arecv.at[index]).start()

    def send_direct(which, buf):
        send(2 * which, everyone, rows.at[which, pl.ds(0, 1)], buf.at[pl.ds(s * NW + w, 1)])

    def sum_direct(which, buf, total_ref):
        wait_all(2 * which, buf)
        total = buf[0:NW]
        for a in range(1, NS):
            total = total + buf[NW * a : NW * a + NW]
        total_ref[...] = total

    def send_row(which):
        send(2 * which, stream_mates, rows.at[which, pl.ds(0, 1)], st.at[which, pl.ds(s, 1)])

    def forward_row(which, mates, dst):
        wait_all(2 * which, st.at[which])
        total = jnp.sum(st[which], axis=0, keepdims=True)
        rows[3 + which] = jnp.broadcast_to(total, (8, 128))
        send(2 * which + 1, mates, rows.at[3 + which, pl.ds(0, 1)], dst)

    def side_by_side(buf, per, width, used, r):
        total = jnp.zeros((1, 128), F32)
        for a in range(per * r, min(per * r + per, NS)):
            value = jnp.broadcast_to(jnp.where(lane1 < used, buf[a], 0.0), (8, 128))
            total = total + (pltpu.roll(value, width * (a % per), 1) if a % per else value)[0:1]
        return total

    def taken_apart(buf, per, width):
        parts = []
        for a in range(NS):
            value = buf[a // per]
            parts.append(pltpu.roll(value, 128 - width * (a % per), 1) if a % per else value)
        return jnp.concatenate(parts, axis=0)

    def wait_all(index, buf):
        pltpu.make_async_copy(buf, buf, arecv.at[index]).wait()

    def wait_sent(index, part):
        pltpu.make_async_copy(part, part, asend.at[index]).wait()

    def partial_values(c, tiled):
        at = iota((32, DEVICES), 0) + 32 * s
        pick = jnp.where(slots[...] == at, 1.0, 0.0)
        high, low = split(c)
        pick2 = jnp.concatenate([pick, pick], axis=1).astype(BF16)
        both = jnp.concatenate([high, low], axis=0).astype(BF16)
        ordered = jnp.dot(pick2, both, preferred_element_type=F32)
        if not tiled:
            ordered = tile16(ordered)
        keep = iota((32, 128), 1) // 16 == iota((32, 128), 0) % 8
        ordered = jnp.where(keep, ordered, 0.0)
        total = jnp.zeros((128, 128), F32)
        for q in range(4):
            row = jnp.sum(ordered[8 * q : 8 * q + 8], axis=0, keepdims=True)
            total = total + inv[:, 128 * q : 128 * q + 128] * row
        sums = lane_totals(total)
        return jnp.sum(jnp.where(iota((128, 128), 0) == iota((128, 128), 1), sums, 0.0), axis=0, keepdims=True)

    def coefficients(which, a, b, place):
        mine = slot[a * NW + b]
        row = (yw1 if which else yw0)[pl.ds(lax.shift_right_logical(mine, 3), 1), :]
        shift = lax.bitwise_and(16 * place + 128 - 16 * lax.bitwise_and(mine, 7), 127)
        rolled = pltpu.roll(jnp.broadcast_to(row, (8, 128)), shift, 1)
        return jnp.where(lane // 16 == place, rolled, 0.0)

    tail_lane = iota((8, 128), 1)

    def tail_valid(depth):
        inner = jnp.logical_and(tail_lane < depth, w < NW - 1)
        outer = jnp.logical_and(tail_lane >= 128 - depth, w > 0)
        return jnp.logical_or(inner, outer)

    def masked(value, valid):
        return jnp.concatenate([value[:, 0:CY], jnp.where(valid, value[:, CY:], 0.0)], axis=1)

    wide_sub = iota((8, COLS), 0)

    def hsum(v):
        return v + pltpu.roll(v, 1, 1) + pltpu.roll(v, COLS - 1, 1)

    def vsum(before, here, after):
        above = pltpu.roll(jnp.where(wide_sub == 7, before, here), 1, 0)
        below = pltpu.roll(jnp.where(wide_sub == 0, after, here), 7, 0)
        return here + above + below

    def rows_at(i):
        return slice(8 * i, 8 * i + 8)

    def stencil_strips(load, use):
        zero = jnp.zeros((8, COLS), F32)
        value = load(0)
        before, now = zero, hsum(value)
        for i in range(STRIPS):
            following = load(i + 1) if i + 1 < STRIPS else None
            after = zero if following is None else hsum(following)
            use(i, value, vsum(before, now, after))
            before, now, value = now, after, following

    def inside(i, value, valid):
        value = masked(value, valid)
        if i == 0:
            return jnp.where(wide_sub >= 4, value, 0.0)
        if i == STRIPS - 1:
            return jnp.where(wide_sub < 4, value, 0.0)
        return value

    def chebyshev(g):
        valid = tail_valid(4)
        old, new = x, x2
        for k, (a, b) in enumerate(sweep_factors()):

            def load(i, k=k, old=old):
                return g[rows_at(i), :] * (1.0 / (3.0 * MIDDLE)) if k == 0 else old[rows_at(i), :]

            def use(i, value, total, k=k, a=a, b=b, new=new):
                e = g[rows_at(i), :] - d9[rows_at(i), :] * value + total
                step = a * (value if k == 0 else u[rows_at(i), :]) + (b / 3.0) * e
                step = inside(i, step, valid)
                if k < DEG - 1:
                    u[rows_at(i), :] = step
                new[rows_at(i), :] = value + step

            stencil_strips(load, use)
            old, new = new, old

    for load in loads[:3]:
        load.wait()
    sums = mode_sums(lambda i: ext[0, strip(i + 1), 0:CY], 4)
    first_residual = gathered(mode_parts(sums, 4), 16) * SCALE
    rows[0] = jnp.broadcast_to(jnp.where(lane1 // 16 == s, first_residual, 0.0), (8, 128))
    loads[3].wait()
    for f in range(2):
        a, b = pack(ext.at[f])
        colsend[0, 16 * f : 16 * f + 16] = a
        colsend[1, 16 * f : 16 * f + 16] = b

    pl.semaphore_wait(barrier, 7 + 31 + 4)
    top, bottom = pl.ds(8, 8), pl.ds(CX, 8)
    west, east, body_lanes = pl.ds(0, 128), pl.ds(CY - 128, 128), pl.ds(0, CY)
    margins = to_neighbours(
        0,
        [
            (ext.at[:, top, body_lanes], ext.at[:, pl.ds(ROWS - 8, 8), body_lanes]),
            (ext.at[:, bottom, body_lanes], ext.at[:, pl.ds(0, 8), body_lanes]),
            (colsend.at[0], colrecv.at[0]),
            (colsend.at[1], colrecv.at[1]),
            (ext.at[:, top, west], corners.at[3]),
            (ext.at[:, top, east], corners.at[2]),
            (ext.at[:, bottom, west], corners.at[1]),
            (ext.at[:, bottom, east], corners.at[0]),
        ],
    )
    send_row(0)
    for copy in margins:
        copy.start()
    loads[4].wait()
    sums = mode_sums(lambda i: ext[1, strip(i + 1), 0:CY], 7)
    drow[0] = gathered(mode_parts(sums, 7), 128)
    send(6, stream_mates, drow, dst.at[pl.ds(s, 1)])
    for load in loads[5:]:
        load.wait()
    at = iota((128, DEVICES), 0)
    group_of = lax.shift_right_logical(slots[...], 3)
    onehot[...] = jnp.where(jnp.logical_and(group_of == at % 32, at < 64), 1.0, 0.0).T
    block[...] = jnp.where(lax.bitwise_and(slots[...], 7) == at // 16, 1.0, 0.0).T

    def own_part(i, carry):
        gm[strip(i), 0:CY] = ext[0, strip(i), 0:CY]
        d9[strip(i), 0:CY] = ext[1, strip(i), 0:CY] * 3.0 + 9.0
        return carry

    lax.fori_loop(1, STRIPS - 1, own_part, 0, unroll=True)
    forward_row(0, wall_mates, cw.at[pl.ds(w, 1)])
    for copy in margins:
        copy.wait_recv()

    valid4 = tail_valid(4)
    two_strips = jnp.concatenate([valid4, valid4], axis=0)
    for k in range(16):
        here = slice(8 + 16 * k, 24 + 16 * k)
        gm[here, CY:COLS] = jnp.where(two_strips, unpack(colrecv[0, 0:16], colrecv[1, 0:16], k), 0.0)
        d9[here, CY:COLS] = unpack(colrecv[0, 16:32], colrecv[1, 16:32], k) * 3.0 + 9.0
    for i, keep, right_at in ((0, sub >= 4, 1), (STRIPS - 1, sub < 4, 3)):
        here = rows_at(i)
        wide_keep = wide_sub[:, 0:CY] >= 4 if i == 0 else wide_sub[:, 0:CY] < 4
        gm[here, 0:CY] = jnp.where(wide_keep, ext[0, here, 0:CY], 0.0)
        d9[here, 0:CY] = ext[1, here, 0:CY] * 3.0 + 9.0
        tail = corner(corners[right_at, 0], corners[right_at - 1, 0])
        gm[here, CY:COLS] = jnp.where(jnp.logical_and(valid4, keep), tail, 0.0)
        d9[here, CY:COLS] = corner(corners[right_at, 1], corners[right_at - 1, 1]) * 3.0 + 9.0
    chebyshev(gm)

    def moment_body(step, sums):
        sums = list(sums)
        for k in range(2):
            i = step * 2 + k
            value = x[strip(i + 1), 0:CY]
            weighted = value * d9[strip(i + 1), 0:CY]
            sums[0], sums[4] = sums[0] + value, sums[4] + weighted
            for m in range(1, 4):
                t = phi[pl.ds(pl.multiple_of((m - 1) * CX + i * 8, 8), 8), :]
                t = jnp.concatenate([t] * 6, axis=1)
                sums[m], sums[4 + m] = sums[m] + value * t, sums[4 + m] + weighted * t
        return tuple(sums)

    sums = lax.fori_loop(0, CX // 16, moment_body, (jnp.zeros((8, CY), F32),) * 8)
    u_sums, w_sums = sums[:4], sums[4:]
    parts = mode_parts(u_sums, 4) + mode_parts(w_sums, 4)
    for edge, here in ((x[8:16, 0:CY], sub == 0), (x[CX : CX + 8, 0:CY], sub == 7)):
        parts += [jnp.where(here, p, 0.0) for p in mode_parts([edge], 4)]
    parts += [jnp.where(lane == 0, v[:, 0:128], 0.0) for v in u_sums]
    parts += [jnp.where(lane == 127, v[:, CY - 128 : CY], 0.0) for v in u_sums]
    for edge, at_row in ((x[8:16, :], 0), (x[CX : CX + 8, :], 7)):
        for tile, at_lane in ((edge[:, 0:128], 0), (edge[:, CY - 128 : CY], 127)):
            parts.append(jnp.where(jnp.logical_and(sub == at_row, lane == at_lane), tile, 0.0))
    totals = lane_totals(jnp.concatenate(parts, axis=0)) * weights[...]
    moments = jnp.sum(totals, axis=0, keepdims=True)
    moments = moments + jnp.where(lane1 < 16, first_residual, 0.0)
    qpack[3] = moments
    send(8, stream_mates, qpack.at[pl.ds(3, 1)], qst.at[pl.ds(s, 1)])

    wait_all(1, cw)
    spread_rows = jnp.concatenate([cw[...]] * NS, axis=0)
    own_lanes = iota((DEVICES, 128), 1) // 16 == iota((DEVICES, 128), 0) // NW
    rows[1] = jnp.broadcast_to(partial_values(jnp.where(own_lanes, spread_rows, 0.0), False), (8, 128))
    send_row(1)
    wait_all(6, dst)
    for r in range(4):
        dpack[r] = side_by_side(dst, 2, 64, 49, r)
    send(7, wall_mates, dpack, dbuf.at[:, pl.ds(w, 1), :])

    a, b = pack(x)
    hcolsend[0] = a
    hcolsend[1] = b
    halos = to_neighbours(
        1,
        [
            (x.at[top, body_lanes], hrows.at[1]),
            (x.at[bottom, body_lanes], hrows.at[0]),
            (hcolsend.at[0], hcolrecv.at[0]),
            (hcolsend.at[1], hcolrecv.at[1]),
            (x.at[top, west], hcorners.at[3]),
            (x.at[top, east], hcorners.at[2]),
            (x.at[bottom, west], hcorners.at[1]),
            (x.at[bottom, east], hcorners.at[0]),
        ],
    )
    for copy in halos:
        copy.start()

    wait_all(8, qst)
    for r in range(3):
        qpack[r] = side_by_side(qst, 3, 40, 36, r)
    send(9, wall_mates, qpack.at[pl.ds(0, 3)], qbuf.at[:, pl.ds(w, 1), :])
    forward_row(1, wall_mates, yw0.at[pl.ds(w, 1)])

    for copy in halos:
        copy.wait_recv()
    valid8 = tail_valid(8)

    def place(i, carry):
        first[strip(i), 0:CY] = x[strip(i), 0:CY]
        return carry

    lax.fori_loop(1, STRIPS - 1, place, 0, unroll=True)
    first[0:8, 0:CY] = hrows[0]
    first[ROWS - 8 : ROWS, 0:CY] = hrows[1]
    for k in range(16):
        edge = unpack(hcolrecv[0], hcolrecv[1], k)
        first[8 + 16 * k : 16 + 16 * k, CY:COLS] = jnp.where(valid8, edge[0:8], 0.0)
        first[16 + 16 * k : 24 + 16 * k, CY:COLS] = jnp.where(valid8, edge[8:16], 0.0)
    first[0:8, CY:COLS] = jnp.where(valid8, corner(hcorners[1], hcorners[0]), 0.0)
    first[ROWS - 8 : ROWS, CY:COLS] = jnp.where(valid8, corner(hcorners[3], hcorners[2]), 0.0)

    wait_all(7, dbuf)
    diag = jnp.where(iota((DEVICES, 128), 1) < 64, taken_apart(dbuf, 2, 64), 0.0)
    high, low = split(diag)
    both = jnp.concatenate([high, low], axis=1).astype(BF16)
    diag_modes[...] = jnp.dot(both, spread[...], preferred_element_type=F32) * (-SCALE)
    wait_all(9, qbuf)
    known = taken_apart(qbuf, 3, 40)
    wait_all(3, yw0)

    high, low = split(yw0[...])
    both = jnp.concatenate([high, low, jnp.zeros((64, 128), F32)], axis=0).astype(BF16)
    values = jnp.dot(onehot[...].astype(BF16), both, preferred_element_type=F32) * block[...]
    values = tile16(values)
    lanes = iota((DEVICES, 128), 1)
    near = jnp.where(lanes < 36, known, jnp.where(lanes < 52, values, 0.0))
    near = jnp.where(lanes >= 16, near, 0.0)
    mixed = jnp.where(lanes < 16, known, near)
    mixed = mixed + pltpu.roll(jnp.concatenate([near[-NW:], near[:-NW]], axis=0), 36, 1)
    mixed = mixed + pltpu.roll(jnp.concatenate([near[NW:], near[:NW]], axis=0), 72, 1)
    high, low = split(mixed)
    both = jnp.concatenate([high, low, high], axis=1).astype(BF16)
    sides = jnp.dot(both, mix[...], preferred_element_type=F32)
    wall_row = iota((DEVICES, 128), 0) % NW
    second_residual = sides[:, 0:128]
    second_residual = second_residual + jnp.where(wall_row > 0, pltpu.roll(sides[:, 128:256], 1, 0), 0.0)
    second_residual = second_residual + jnp.where(
        wall_row < NW - 1, pltpu.roll(sides[:, 256:384], DEVICES - 1, 0), 0.0
    )
    products = [part for h in range(2) for part in split(values * diag_modes[:, 128 * h : 128 * h + 128])]
    both = jnp.concatenate(products, axis=1).astype(BF16)
    at = iota((512, 128), 0)
    summed = jnp.where(8 * (at // 256) + (at % 128) // 16 == iota((512, 128), 1) % 16, 1.0, 0.0)
    second_residual = second_residual + jnp.dot(both, summed.astype(BF16), preferred_element_type=F32)
    rows[2] = jnp.broadcast_to(partial_values(second_residual, True), (8, 128))
    send_direct(2, all2)

    groups = []
    for a in (up, s, down):
        group = coefficients(0, a, w, 1)
        group = group + jnp.where(w > 0, coefficients(0, a, left, 0), 0.0)
        group = group + jnp.where(w < NW - 1, coefficients(0, a, right, 2), 0.0)
        groups.append(jnp.where((lane % 16) // 4 == sub, group, 0.0))
    py[...] = prolonged(groups, sk[...], wk[...])

    def first_at(i):
        value = first[rows_at(i), :] + py[rows_at(i), :] * (1.0 / 3.0)
        first[rows_at(i), :] = value
        return value

    def residual(i, value, total):
        res[rows_at(i), :] = inside(i, gm[rows_at(i), :] - d9[rows_at(i), :] * value + total, valid4)

    stencil_strips(first_at, residual)

    resid_copy = pltpu.make_async_copy(res.at[pl.ds(8, CX), pl.ds(0, CY)], resid_hbm, store_sem.at[0])
    resid_copy.start()
    for copy in halos:
        copy.wait_send()
    chebyshev(res)

    def add_local(i, carry):
        first[strip(i), 0:CY] = (first[strip(i), 0:CY] + x[strip(i), 0:CY]) * 3.0
        return carry

    lax.fori_loop(1, STRIPS - 1, add_local, 0, unroll=True)
    base_copy = pltpu.make_async_copy(first.at[pl.ds(8, CX), pl.ds(0, CY)], base_hbm, store_sem.at[1])
    base_copy.start()
    sum_direct(2, all2, yw1)
    own_row = (lane % 16) // 4 == sub
    mine_out[...] = jnp.where(own_row, coefficients(1, s, w, 1), 0.0)
    for which, part in enumerate((cw.at[pl.ds(0, NW - 1)], yw0.at[pl.ds(0, NW - 1)], None)):
        if part is None:
            wait_sent(2 * which, all2.at[pl.ds(0, DEVICES - 1)])
        else:
            wait_sent(2 * which, st.at[which, pl.ds(0, NS - 1)])
            wait_sent(2 * which + 1, part)
    wait_sent(6, dst.at[pl.ds(0, NS - 1)])
    wait_sent(7, dbuf.at[:, pl.ds(0, NW - 1), :])
    wait_sent(8, qst.at[pl.ds(0, NS - 1)])
    wait_sent(9, qbuf.at[:, pl.ds(0, NW - 1), :])
    for copy in margins:
        copy.wait_send()
    resid_copy.wait()
    base_copy.wait()


PIECES = 2


def finish(
    base_hbm, resid_hbm, mine_hbm, stream_hbm, wall_hbm, out_hbm, resid_out,
    base, resid, mine, stream_table, wall_table, small_sem, load_sem, store_sem,
):
    small = [
        pltpu.make_async_copy(src, dst, small_sem.at[i])
        for i, (src, dst) in enumerate([(mine_hbm, mine), (wall_hbm, wall_table), (stream_hbm, stream_table)])
    ]
    for copy in small:
        copy.start()
    parts = [pl.ds(i * (CX // PIECES), CX // PIECES) for i in range(PIECES)]
    loads, stores = [], []
    for k, (src, here, dst) in enumerate(((resid_hbm, resid, resid_out), (base_hbm, base, out_hbm))):
        loads.append([pltpu.make_async_copy(src.at[p], here.at[p], load_sem.at[k, i]) for i, p in enumerate(parts)])
        stores.append([pltpu.make_async_copy(here.at[p], dst.at[p], store_sem.at[k, i]) for i, p in enumerate(parts)])
    for copy in loads[0] + loads[1]:
        copy.start()
    for copy in small:
        copy.wait()
    none = jnp.zeros((8, 128), F32)
    coarse = prolonged([none, mine[...], none], stream_table[...], wall_table[...])
    for i in range(PIECES):
        loads[0][i].wait()
        stores[0][i].start()
    for i in range(PIECES):
        rows = slice(i * (CX // PIECES), (i + 1) * (CX // PIECES))
        loads[1][i].wait()
        base[rows, :] = base[rows, :] + coarse[rows, :]
        stores[1][i].start()
    for copy in stores[0] + stores[1]:
        copy.wait()


def local(right_side, diagonal, coarse_inverse, owner_slot):
    phi_lanes, psi_rows, stream_k, own_k, wall_k = tables()
    mix_k, moment_weights, spread_k = coarse_tables()
    field = jax.ShapeDtypeStruct((CX, CY), F32)
    anywhere = pl.BlockSpec(memory_space=pl.ANY)
    in_vmem = pl.BlockSpec(memory_space=pltpu.VMEM)
    vmem = pltpu.VMEM
    dma = pltpu.SemaphoreType.DMA
    work = vmem((ROWS, COLS), F32)
    base, resid, mine = pl.pallas_call(
        kernel,
        out_shape=(field, field, jax.ShapeDtypeStruct((8, 128), F32)),
        in_specs=[anywhere] * 12,
        out_specs=(anywhere, anywhere, in_vmem),
        scratch_shapes=[
            vmem((2, ROWS, COLS), F32), work, work, work, work, work, work, work, work,
            vmem((128, 512), F32), vmem((6 * CX, 128), F32), vmem((8, CY), F32),
            vmem((ROWS, 128), BF16), vmem((256, COLS), BF16),
            vmem((384, 384), BF16), vmem((416, 128), F32), vmem((256, 256), BF16), vmem((1, DEVICES), jnp.int32),
            vmem((2, 32, 128), F32), vmem((2, 32, 128), F32), vmem((4, 2, 8, 128), F32),
            vmem((2, 16, 128), F32), vmem((2, 16, 128), F32), vmem((4, 8, 128), F32), vmem((2, 8, CY), F32),
            vmem((6, 8, 128), F32), vmem((3, NS, 128), F32), vmem((1, 1, 128), F32), vmem((NS, 1, 128), F32),
            vmem((NS, 1, 128), F32), vmem((4, 1, 128), F32), vmem((4, 1, 128), F32), vmem((NW, 128), F32), vmem((4, NW, 128), F32),
            vmem((3, NW, 128), F32), vmem((NW, 128), F32), vmem((NW, 128), F32),
            vmem((DEVICES, 128), F32),
            vmem((DEVICES, 128), F32), vmem((DEVICES, 128), F32), vmem((DEVICES, 256), F32),
            pltpu.SMEM((DEVICES,), jnp.int32),
            dma((13,)), dma((2, 8)), dma((2, 8)), dma((11,)), dma((11,)), dma((2,)),
        ],
        compiler_params=pltpu.CompilerParams(
            collective_id=0, has_side_effects=True, vmem_limit_bytes=60 * 1024 * 1024
        ),
        cost_estimate=pl.CostEstimate(flops=100_000_000, bytes_accessed=4_000_000, transcendentals=0),
    )(
        right_side, diagonal, coarse_inverse, owner_slot, owner_slot.reshape(1, DEVICES),
        phi_lanes, psi_rows, stream_k, wall_k, mix_k, moment_weights, spread_k,
    )
    return pl.pallas_call(
        finish,
        out_shape=(field, field),
        in_specs=[anywhere] * 5,
        out_specs=(anywhere, anywhere),
        scratch_shapes=[
            vmem((CX, CY), F32), vmem((CX, CY), F32), vmem((8, 128), F32), vmem((CX, 128), BF16), vmem((256, CY), BF16),
            dma((3,)), dma((2, PIECES)), dma((2, PIECES)),
        ],
        compiler_params=pltpu.CompilerParams(vmem_limit_bytes=60 * 1024 * 1024),
        cost_estimate=pl.CostEstimate(flops=50_000_000, bytes_accessed=3_000_000, transcendentals=0),
    )(base, resid, mine, own_k, np.ascontiguousarray(wall_k[:, :CY]))


def solution(mesh):
    placed = (P("stream", "wall"), P("stream", "wall"), P("wall", "stream"), P())
    return jax.shard_map(
        local,
        mesh=mesh,
        in_specs=placed,
        out_specs=(P("stream", "wall"), P("stream", "wall")),
        check_vma=False,
    )
```

```python
import math

import jax
import jax.numpy as jnp
import numpy as np
from jax import lax
from jax.experimental import pallas as pl
from jax.experimental.pallas import tpu as pltpu
from jax.sharding import PartitionSpec as P

MESH = pl.DeviceIdType.MESH
NS, NW = 8, 32
DEVICES = NS * NW
CX, CY = 256, 768
DEG = 4
ROWS, COLS = CX + 16, CY + 128
STRIPS = ROWS // 8
MIDDLE = (5.0 + 0.05) / 2.0
SPREAD = (5.0 - 0.05) / 2.0
SCALE = 1.0 / math.sqrt(CX * CY)
F32, BF16 = jnp.float32, jnp.bfloat16


def sweep_factors():
    quotient = MIDDLE / SPREAD
    factor = 1.0 / quotient
    pairs = []
    for _ in range(DEG):
        following = 1.0 / (2.0 * quotient - factor)
        pairs.append((following * factor, 2.0 * following / SPREAD))
        factor = following
    return pairs


def halves(table):
    high = table.astype(BF16)
    return high, (table - high.astype(np.float32)).astype(BF16)


def tables():
    phi = np.cos(np.pi * (np.arange(CX) + 0.5)[None, :] * np.arange(7)[:, None] / CX)
    psi = np.cos(np.pi * (np.arange(CY) + 0.5)[None, :] * np.arange(7)[:, None] / CY)
    phi_lanes = np.repeat(phi[1:].reshape(6 * CX, 1), 128, axis=1).astype(np.float32)
    psi_rows = np.concatenate([psi, psi[:1]]).astype(np.float32)
    stream = np.zeros((ROWS, 32), np.float32)
    stream[0:8, 0:4] = phi[:4, CX - 8 :].T
    stream[8 : 8 + CX, 8:12] = phi[:4].T
    stream[8 + CX :, 16:20] = phi[:4, :8].T
    high, low = halves(stream)
    stream_k = np.concatenate([high, high, low, np.zeros_like(high)], axis=1)
    own_k = stream_k[8 : 8 + CX]
    wall = np.zeros((64, COLS), np.float32)
    for m in range(4):
        wall[4 * m : 4 * m + 4, COLS - 64 :] = psi[:4, CY - 64 :]
        wall[16 + 4 * m : 20 + 4 * m, :CY] = psi[:4]
        wall[32 + 4 * m : 36 + 4 * m, CY : CY + 64] = psi[:4, :64]
    high, low = halves(wall)
    wall_k = np.concatenate([high, high, low, np.zeros_like(high)], axis=0)
    return phi_lanes, psi_rows, stream_k, own_k, wall_k


EDGES = 20


def coarse_tables():
    phi = np.cos(np.pi * (np.arange(CX) + 0.5)[None, :] * np.arange(4)[:, None] / CX)
    psi = np.cos(np.pi * (np.arange(CY) + 0.5)[None, :] * np.arange(4)[:, None] / CY)
    lam = 1.0 + 2.0 * np.cos(np.pi * np.arange(4) / CX)
    mu = 1.0 + 2.0 * np.cos(np.pi * np.arange(4) / CY)
    p0, p1, q0, q1 = phi[:, 0], phi[:, -1], psi[:, 0], psi[:, -1]
    nx, ny = (phi**2).sum(1), (psi**2).sum(1)
    near = {(a, b): np.zeros((EDGES, 4, 4)) for a in (-1, 0, 1) for b in (-1, 0, 1)}
    from_modes = np.zeros((4, 4, EDGES))
    corner = {(0, 0): 16, (0, 1): 17, (1, 0): 18, (1, 1): 19}
    ps, qs = (p0, p1), (q0, q1)
    for n in range(4):
        for side in (0, 1):
            row = 4 * side + n
            near[0, 0][row, :, n] -= mu[n] * ps[side]
            near[1 if side == 0 else -1, 0][row, :, n] += mu[n] * ps[1 - side]
            from_modes[:, n, row] += ps[side] * ny[n]
    for m in range(4):
        for side in (0, 1):
            row = 8 + 4 * side + m
            near[0, 0][row, m, :] -= lam[m] * qs[side]
            near[0, 1 if side == 0 else -1][row, m, :] += lam[m] * qs[1 - side]
            from_modes[m, :, row] += qs[side] * nx[m]
    for (i, j), row in corner.items():
        a, b = (1 if i == 0 else -1), (1 if j == 0 else -1)
        near[0, 0][row] += np.outer(ps[i], qs[j])
        near[a, 0][row] -= np.outer(ps[1 - i], qs[j])
        near[0, b][row] -= np.outer(ps[i], qs[1 - j])
        near[a, b][row] += np.outer(ps[1 - i], qs[1 - j])
        from_modes[:, :, row] += np.outer(ps[i], qs[j])
    near = {key: value.reshape(EDGES, 16) * (SCALE / 3.0) for key, value in near.items()}
    from_modes = from_modes.reshape(16, EDGES)
    smooth = np.outer(lam, mu).reshape(16) / 3.0
    norm = np.outer(nx, ny).reshape(16)
    mix = np.zeros((3, 128, 16))
    mix[0, 0:16] = np.eye(16)
    for side, b in enumerate((0, -1, 1)):
        for place, a in enumerate((0, -1, 1)):
            start = 16 + 36 * place
            values = from_modes @ near[a, b]
            if a == 0 and b == 0:
                values = values - np.diag(SCALE * (3.0 - smooth) * norm)
            mix[side, start : start + 20] = near[a, b]
            for k in range(16):
                mix[side, start + 20 + k] = values[(36 + k) % 16]
    wide = np.concatenate([np.tile(mix[i], (1, 8)) for i in range(3)], axis=1).astype(np.float32)
    high, low = halves(wide)
    mix_k = np.concatenate([high, high, low], axis=0)
    weights = np.zeros((52, 128), np.float32)
    for k in range(16):
        weights[k, k] = 3.0 * SCALE * smooth[k]
        weights[16 + k, k] = -SCALE
    for e in range(EDGES):
        weights[32 + e, 16 + e] = 3.0
    spread = np.zeros((128, 256), np.float32)
    for k in range(16):
        for j in range(16):
            m, n, mm, nn = k // 4, k % 4, j // 4, j % 4
            for p in (m + mm, abs(m - mm)):
                for q in (n + nn, abs(n - nn)):
                    spread[7 * p + q, 16 * k + j] += 0.25
    return mix_k, np.repeat(weights, 8, axis=0), np.concatenate([spread, spread]).astype(BF16)


def iota(shape, dim):
    return lax.broadcasted_iota(jnp.int32, shape, dim)


def split(value):
    high = value.astype(BF16).astype(F32)
    return high, value - high


def lane_totals(value):
    high, low = split(value)
    both = jnp.concatenate([high, low], axis=1).astype(BF16)
    return jnp.dot(both, jnp.ones((256, 128), BF16), preferred_element_type=F32)


def prolonged(groups, stream_table, wall_table):
    stacked = jnp.concatenate(groups + [jnp.zeros((8, 128), F32)], axis=0)
    high, low = split(stacked)
    operand = jnp.concatenate([high + pltpu.roll(low, 64, 1), high], axis=1).astype(BF16)
    mixed = jnp.dot(operand, wall_table, preferred_element_type=F32)
    high, low = split(mixed)
    operand = jnp.concatenate([high, low, high, jnp.zeros_like(high)], axis=0).astype(BF16)
    return jnp.dot(stream_table, operand, preferred_element_type=F32)


def tile16(value):
    alike = jnp.where(iota((256, 128), 0) % 16 == iota((256, 128), 1) % 16, 1.0, 0.0).astype(BF16)
    high, low = split(value)
    both = jnp.concatenate([high, low], axis=1).astype(BF16)
    return jnp.dot(both, alike, preferred_element_type=F32)


def strip(i):
    return pl.ds(pl.multiple_of(i * 8, 8), 8)


def kernel(
    rhs_hbm, diag_hbm, inv_hbm, slot_hbm, slots_hbm, phi_hbm, psi_hbm, sk_hbm, wk_hbm, mix_hbm, weights_hbm, spread_hbm,
    base_hbm, resid_hbm, mine_out,
    ext, gm, d9, x, x2, u, first, res, py, inv, phi, psi, sk, wk, mix, weights, spread, slots,
    colsend, colrecv, corners, hcolsend, hcolrecv, hcorners, hrows,
    rows, st, drow, dst, qst, qpack, dpack, cw, dbuf, qbuf, yw0, yw1, all2, onehot, block, diag_modes, slot,
    load_sem, msend, mrecv, asend, arecv, store_sem,
):
    s = lax.axis_index("stream")
    w = lax.axis_index("wall")
    me = s * NW + w
    ya, xl = s % 4, s // 4
    xh, za, core = w // 16, (w // 2) % 8, w % 2
    xa = xh * 2 + xl
    up, down = (s + NS - 1) % NS, (s + 1) % NS
    left, right = (w + NW - 1) % NW, (w + 1) % NW

    def around(k, n):
        return n // 2 + (k % 2) * ((k + 1) // 2) - (1 - k % 2) * (k // 2)

    def everyone(act):
        xa = xh * 2 + xl
        ys = [(ya + d) % 4 for d in (2, 3, 1, 0)]

        def some(k, count):
            z = (za + around(k // 4, 8)) % 8
            xx = (xa + around(k % 4, 4)) % 4
            base_s = (xx % 2) * 4
            base_w = (xx // 2) * 16 + z * 2
            for j in range(count):
                act((base_s + ys[j // 2], base_w + ((1 - core) if j % 2 == 0 else core)))

        def body(k, carry):
            some(k, 8)
            return carry

        lax.fori_loop(0, 31, body, 0)
        some(jnp.int32(31), 7)

    def stream_mates(act):
        for d in (2, 3, 1, 0):
            for flip in (1, 0):
                if d or flip:
                    act(((xl if flip == 0 else 1 - xl) * 4 + (ya + d) % 4, w))

    def wall_mates(act):
        for d in (4, 5, 3, 6, 2, 7, 1, 0):
            for flip in (1, 0):
                for other in (1, 0):
                    if d or flip or other:
                        x_part = (xh if flip == 0 else 1 - xh) * 16
                        act((s, x_part + ((za + d) % 8) * 2 + (core if other == 0 else 1 - core)))

    barrier = pltpu.get_barrier_semaphore()

    def greet(to):
        pl.semaphore_signal(barrier, inc=1, device_id=to, device_id_type=MESH)

    wall_mates(greet)
    stream_mates(greet)
    for to in [(up, left), (up, right), (down, left), (down, right)]:
        greet(to)

    own = ext.at[:, pl.ds(8, CX), pl.ds(0, CY)]
    loads = [
        pltpu.make_async_copy(src, dst, load_sem.at[i])
        for i, (src, dst) in enumerate(
            [
                (rhs_hbm, own.at[0]),
                (phi_hbm.at[pl.ds(0, 3 * CX)], phi.at[pl.ds(0, 3 * CX)]),
                (psi_hbm, psi),
                (diag_hbm, own.at[1]),
                (phi_hbm.at[pl.ds(3 * CX, 3 * CX)], phi.at[pl.ds(3 * CX, 3 * CX)]),
                (slot_hbm, slot),
                (slots_hbm, slots),
                (inv_hbm, inv),
                (sk_hbm, sk),
                (wk_hbm, wk),
                (mix_hbm, mix),
                (weights_hbm, weights),
                (spread_hbm, spread),
            ]
        )
    ]
    for load in loads:
        load.start()

    lane = iota((8, 128), 1)
    sub = iota((8, 128), 0)
    lane16 = iota((16, 128), 1)
    lane1 = iota((1, 128), 1)

    def mode_sums(load, count):
        def body(step, sums):
            sums = list(sums)
            for i in range(4):
                f = load(step * 4 + i)
                sums[0] = sums[0] + f
                for m in range(count - 1):
                    t = phi[pl.ds(pl.multiple_of(m * CX + (step * 4 + i) * 8, 8), 8), :]
                    sums[m + 1] = sums[m + 1] + f * jnp.concatenate([t] * 6, axis=1)
            return tuple(sums)

        return lax.fori_loop(0, CX // 32, body, (jnp.zeros((8, CY), F32),) * count)

    def fold(value):
        total = value[:, 0:128]
        for t in range(1, 6):
            total = total + value[:, 128 * t : 128 * t + 128]
        return total

    def mode_parts(sums, count):
        return [fold(v if n == 0 else v * psi[n : n + 1, :]) for v in sums for n in range(count)]

    def gathered(parts, period):
        totals = lane_totals(jnp.concatenate(parts, axis=0))
        shape = totals.shape
        keep = iota(shape, 0) // 8 == iota(shape, 1) % period
        return jnp.sum(jnp.where(keep, totals, 0.0), axis=0, keepdims=True)

    def pack(ref):
        to_left = jnp.zeros((16, 128), F32)
        to_right = jnp.zeros((16, 128), F32)
        for k in range(16):
            a = jnp.where(lane16 < 8, ref[8 + 16 * k : 24 + 16 * k, 0:128], 0.0)
            b = jnp.where(lane16 >= 120, ref[8 + 16 * k : 24 + 16 * k, CY - 128 : CY], 0.0)
            to_left = to_left + (pltpu.roll(a, 8 * k, 1) if k else a)
            shift = (8 * k + 8) % 128
            to_right = to_right + (pltpu.roll(b, shift, 1) if shift else b)
        return to_left, to_right

    def unpack(from_right, from_left, k):
        a = pltpu.roll(from_right, 128 - 8 * k, 1) if k else from_right
        shift = (120 - 8 * k) % 128
        b = pltpu.roll(from_left, shift, 1) if shift else from_left
        return jnp.where(lane16 < 8, a, jnp.where(lane16 >= 120, b, 0.0))

    def corner(from_right, from_left):
        return jnp.where(lane < 8, from_right, jnp.where(lane >= 120, from_left, 0.0))

    def to_neighbours(which, pairs):
        targets = [(up, w), (down, w), (s, left), (s, right), (up, left), (up, right), (down, left), (down, right)]
        return [
            pltpu.make_async_remote_copy(
                src_ref=src, dst_ref=dst, send_sem=msend.at[which, i], recv_sem=mrecv.at[which, i],
                device_id=to, device_id_type=MESH,
            )
            for i, ((src, dst), to) in enumerate(zip(pairs, targets, strict=True))
        ]

    def sender(index, src, dst):
        def act(to):
            pltpu.make_async_remote_copy(
                src_ref=src, dst_ref=dst, send_sem=asend.at[index], recv_sem=arecv.at[index],
                device_id=to, device_id_type=MESH,
            ).start()

        return act

    def send(index, mates, src, dst):
        mates(sender(index, src, dst))
        pltpu.make_async_copy(src, dst, arecv.at[index]).start()

    def send_direct(which, buf):
        send(2 * which, everyone, rows.at[which, pl.ds(0, 1)], buf.at[pl.ds(s * NW + w, 1)])

    def sum_direct(which, buf, total_ref):
        wait_all(2 * which, buf)
        total = buf[0:NW]
        for a in range(1, NS):
            total = total + buf[NW * a : NW * a + NW]
        total_ref[...] = total

    def send_row(which):
        send(2 * which, stream_mates, rows.at[which, pl.ds(0, 1)], st.at[which, pl.ds(s, 1)])

    def forward_row(which, mates, dst):
        wait_all(2 * which, st.at[which])
        total = jnp.sum(st[which], axis=0, keepdims=True)
        rows[3 + which] = jnp.broadcast_to(total, (8, 128))
        send(2 * which + 1, mates, rows.at[3 + which, pl.ds(0, 1)], dst)

    def side_by_side(buf, per, width, used, r):
        total = jnp.zeros((1, 128), F32)
        for a in range(per * r, min(per * r + per, NS)):
            value = jnp.broadcast_to(jnp.where(lane1 < used, buf[a], 0.0), (8, 128))
            total = total + (pltpu.roll(value, width * (a % per), 1) if a % per else value)[0:1]
        return total

    def taken_apart(buf, per, width):
        parts = []
        for a in range(NS):
            value = buf[a // per]
            parts.append(pltpu.roll(value, 128 - width * (a % per), 1) if a % per else value)
        return jnp.concatenate(parts, axis=0)

    def wait_all(index, buf):
        pltpu.make_async_copy(buf, buf, arecv.at[index]).wait()

    def wait_sent(index, part):
        pltpu.make_async_copy(part, part, asend.at[index]).wait()

    def partial_values(c, tiled):
        at = iota((32, DEVICES), 0) + 32 * s
        pick = jnp.where(slots[...] == at, 1.0, 0.0)
        high, low = split(c)
        pick2 = jnp.concatenate([pick, pick], axis=1).astype(BF16)
        both = jnp.concatenate([high, low], axis=0).astype(BF16)
        ordered = jnp.dot(pick2, both, preferred_element_type=F32)
        if not tiled:
            ordered = tile16(ordered)
        keep = iota((32, 128), 1) // 16 == iota((32, 128), 0) % 8
        ordered = jnp.where(keep, ordered, 0.0)
        total = jnp.zeros((128, 128), F32)
        for q in range(4):
            row = jnp.sum(ordered[8 * q : 8 * q + 8], axis=0, keepdims=True)
            total = total + inv[:, 128 * q : 128 * q + 128] * row
        sums = lane_totals(total)
        return jnp.sum(jnp.where(iota((128, 128), 0) == iota((128, 128), 1), sums, 0.0), axis=0, keepdims=True)

    def coefficients(which, a, b, place):
        mine = slot[a * NW + b]
        row = (yw1 if which else yw0)[pl.ds(lax.shift_right_logical(mine, 3), 1), :]
        shift = lax.bitwise_and(16 * place + 128 - 16 * lax.bitwise_and(mine, 7), 127)
        rolled = pltpu.roll(jnp.broadcast_to(row, (8, 128)), shift, 1)
        return jnp.where(lane // 16 == place, rolled, 0.0)

    tail_lane = iota((8, 128), 1)

    def tail_valid(depth):
        inner = jnp.logical_and(tail_lane < depth, w < NW - 1)
        outer = jnp.logical_and(tail_lane >= 128 - depth, w > 0)
        return jnp.logical_or(inner, outer)

    def masked(value, valid):
        return jnp.concatenate([value[:, 0:CY], jnp.where(valid, value[:, CY:], 0.0)], axis=1)

    wide_sub = iota((8, COLS), 0)

    def hsum(v):
        return v + pltpu.roll(v, 1, 1) + pltpu.roll(v, COLS - 1, 1)

    def vsum(before, here, after):
        above = pltpu.roll(jnp.where(wide_sub == 7, before, here), 1, 0)
        below = pltpu.roll(jnp.where(wide_sub == 0, after, here), 7, 0)
        return here + above + below

    def rows_at(i):
        return slice(8 * i, 8 * i + 8)

    def stencil_strips(load, use):
        zero = jnp.zeros((8, COLS), F32)
        value = load(0)
        before, now = zero, hsum(value)
        for i in range(STRIPS):
            following = load(i + 1) if i + 1 < STRIPS else None
            after = zero if following is None else hsum(following)
            use(i, value, vsum(before, now, after))
            before, now, value = now, after, following

    def inside(i, value, valid):
        value = masked(value, valid)
        if i == 0:
            return jnp.where(wide_sub >= 4, value, 0.0)
        if i == STRIPS - 1:
            return jnp.where(wide_sub < 4, value, 0.0)
        return value

    def chebyshev(g, take=None):
        valid = tail_valid(4)
        old, new = x, x2
        for k, (a, b) in enumerate(sweep_factors()):

            def load(i, k=k, old=old):
                return g[rows_at(i), :] * (1.0 / (3.0 * MIDDLE)) if k == 0 else old[rows_at(i), :]

            last = k == DEG - 1 and take is not None

            def use(i, value, total, k=k, a=a, b=b, new=new, last=last):
                e = g[rows_at(i), :] - d9[rows_at(i), :] * value + total
                step = a * (value if k == 0 else u[rows_at(i), :]) + (b / 3.0) * e
                step = inside(i, step, valid)
                if k < DEG - 1:
                    u[rows_at(i), :] = step
                if last:
                    take(i, value + step)
                else:
                    new[rows_at(i), :] = value + step

            stencil_strips(load, use)
            old, new = new, old

    for load in loads[:3]:
        load.wait()
    sums = mode_sums(lambda i: ext[0, strip(i + 1), 0:CY], 4)
    first_residual = gathered(mode_parts(sums, 4), 16) * SCALE
    rows[0] = jnp.broadcast_to(jnp.where(lane1 // 16 == s, first_residual, 0.0), (8, 128))
    loads[3].wait()
    for f in range(2):
        a, b = pack(ext.at[f])
        colsend[0, 16 * f : 16 * f + 16] = a
        colsend[1, 16 * f : 16 * f + 16] = b

    pl.semaphore_wait(barrier, 7 + 31 + 4)
    top, bottom = pl.ds(8, 8), pl.ds(CX, 8)
    west, east, body_lanes = pl.ds(0, 128), pl.ds(CY - 128, 128), pl.ds(0, CY)
    margins = to_neighbours(
        0,
        [
            (ext.at[:, top, body_lanes], ext.at[:, pl.ds(ROWS - 8, 8), body_lanes]),
            (ext.at[:, bottom, body_lanes], ext.at[:, pl.ds(0, 8), body_lanes]),
            (colsend.at[0], colrecv.at[0]),
            (colsend.at[1], colrecv.at[1]),
            (ext.at[:, top, west], corners.at[3]),
            (ext.at[:, top, east], corners.at[2]),
            (ext.at[:, bottom, west], corners.at[1]),
            (ext.at[:, bottom, east], corners.at[0]),
        ],
    )
    send_row(0)
    for copy in margins:
        copy.start()
    loads[4].wait()
    sums = mode_sums(lambda i: ext[1, strip(i + 1), 0:CY], 7)
    drow[0] = gathered(mode_parts(sums, 7), 128)
    send(6, stream_mates, drow, dst.at[pl.ds(s, 1)])
    for load in loads[5:]:
        load.wait()
    at = iota((128, DEVICES), 0)
    group_of = lax.shift_right_logical(slots[...], 3)
    onehot[...] = jnp.where(jnp.logical_and(group_of == at % 32, at < 64), 1.0, 0.0).T
    block[...] = jnp.where(lax.bitwise_and(slots[...], 7) == at // 16, 1.0, 0.0).T

    def own_part(i, carry):
        gm[strip(i), 0:CY] = ext[0, strip(i), 0:CY]
        d9[strip(i), 0:CY] = ext[1, strip(i), 0:CY] * 3.0 + 9.0
        return carry

    lax.fori_loop(1, STRIPS - 1, own_part, 0, unroll=True)
    forward_row(0, wall_mates, cw.at[pl.ds(w, 1)])
    for copy in margins:
        copy.wait_recv()

    valid4 = tail_valid(4)
    two_strips = jnp.concatenate([valid4, valid4], axis=0)
    for k in range(16):
        here = slice(8 + 16 * k, 24 + 16 * k)
        gm[here, CY:COLS] = jnp.where(two_strips, unpack(colrecv[0, 0:16], colrecv[1, 0:16], k), 0.0)
        d9[here, CY:COLS] = unpack(colrecv[0, 16:32], colrecv[1, 16:32], k) * 3.0 + 9.0
    for i, keep, right_at in ((0, sub >= 4, 1), (STRIPS - 1, sub < 4, 3)):
        here = rows_at(i)
        wide_keep = wide_sub[:, 0:CY] >= 4 if i == 0 else wide_sub[:, 0:CY] < 4
        gm[here, 0:CY] = jnp.where(wide_keep, ext[0, here, 0:CY], 0.0)
        d9[here, 0:CY] = ext[1, here, 0:CY] * 3.0 + 9.0
        tail = corner(corners[right_at, 0], corners[right_at - 1, 0])
        gm[here, CY:COLS] = jnp.where(jnp.logical_and(valid4, keep), tail, 0.0)
        d9[here, CY:COLS] = corner(corners[right_at, 1], corners[right_at - 1, 1]) * 3.0 + 9.0
    chebyshev(gm)

    def moment_body(step, sums):
        sums = list(sums)
        for k in range(2):
            i = step * 2 + k
            value = x[strip(i + 1), 0:CY]
            weighted = value * d9[strip(i + 1), 0:CY]
            sums[0], sums[4] = sums[0] + value, sums[4] + weighted
            for m in range(1, 4):
                t = phi[pl.ds(pl.multiple_of((m - 1) * CX + i * 8, 8), 8), :]
                t = jnp.concatenate([t] * 6, axis=1)
                sums[m], sums[4 + m] = sums[m] + value * t, sums[4 + m] + weighted * t
        return tuple(sums)

    sums = lax.fori_loop(0, CX // 16, moment_body, (jnp.zeros((8, CY), F32),) * 8)
    u_sums, w_sums = sums[:4], sums[4:]
    parts = mode_parts(u_sums, 4) + mode_parts(w_sums, 4)
    for edge, here in ((x[8:16, 0:CY], sub == 0), (x[CX : CX + 8, 0:CY], sub == 7)):
        parts += [jnp.where(here, p, 0.0) for p in mode_parts([edge], 4)]
    parts += [jnp.where(lane == 0, v[:, 0:128], 0.0) for v in u_sums]
    parts += [jnp.where(lane == 127, v[:, CY - 128 : CY], 0.0) for v in u_sums]
    for edge, at_row in ((x[8:16, :], 0), (x[CX : CX + 8, :], 7)):
        for tile, at_lane in ((edge[:, 0:128], 0), (edge[:, CY - 128 : CY], 127)):
            parts.append(jnp.where(jnp.logical_and(sub == at_row, lane == at_lane), tile, 0.0))
    totals = lane_totals(jnp.concatenate(parts, axis=0)) * weights[...]
    moments = jnp.sum(totals, axis=0, keepdims=True)
    moments = moments + jnp.where(lane1 < 16, first_residual, 0.0)
    qpack[3] = moments
    send(8, stream_mates, qpack.at[pl.ds(3, 1)], qst.at[pl.ds(s, 1)])

    wait_all(1, cw)
    spread_rows = jnp.concatenate([cw[...]] * NS, axis=0)
    own_lanes = iota((DEVICES, 128), 1) // 16 == iota((DEVICES, 128), 0) // NW
    rows[1] = jnp.broadcast_to(partial_values(jnp.where(own_lanes, spread_rows, 0.0), False), (8, 128))
    send_row(1)
    wait_all(6, dst)
    for r in range(4):
        dpack[r] = side_by_side(dst, 2, 64, 49, r)
    send(7, wall_mates, dpack, dbuf.at[:, pl.ds(w, 1), :])

    a, b = pack(x)
    hcolsend[0] = a
    hcolsend[1] = b
    halos = to_neighbours(
        1,
        [
            (x.at[top, body_lanes], hrows.at[1]),
            (x.at[bottom, body_lanes], hrows.at[0]),
            (hcolsend.at[0], hcolrecv.at[0]),
            (hcolsend.at[1], hcolrecv.at[1]),
            (x.at[top, west], hcorners.at[3]),
            (x.at[top, east], hcorners.at[2]),
            (x.at[bottom, west], hcorners.at[1]),
            (x.at[bottom, east], hcorners.at[0]),
        ],
    )
    for copy in halos:
        copy.start()

    wait_all(8, qst)
    for r in range(3):
        qpack[r] = side_by_side(qst, 3, 40, 36, r)
    send(9, wall_mates, qpack.at[pl.ds(0, 3)], qbuf.at[:, pl.ds(w, 1), :])
    forward_row(1, wall_mates, yw0.at[pl.ds(w, 1)])

    for copy in halos:
        copy.wait_recv()
    valid8 = tail_valid(8)

    def place(i, carry):
        first[strip(i), 0:CY] = x[strip(i), 0:CY]
        return carry

    lax.fori_loop(1, STRIPS - 1, place, 0, unroll=True)
    first[0:8, 0:CY] = hrows[0]
    first[ROWS - 8 : ROWS, 0:CY] = hrows[1]
    for k in range(16):
        edge = unpack(hcolrecv[0], hcolrecv[1], k)
        first[8 + 16 * k : 16 + 16 * k, CY:COLS] = jnp.where(valid8, edge[0:8], 0.0)
        first[16 + 16 * k : 24 + 16 * k, CY:COLS] = jnp.where(valid8, edge[8:16], 0.0)
    first[0:8, CY:COLS] = jnp.where(valid8, corner(hcorners[1], hcorners[0]), 0.0)
    first[ROWS - 8 : ROWS, CY:COLS] = jnp.where(valid8, corner(hcorners[3], hcorners[2]), 0.0)

    wait_all(7, dbuf)
    diag = jnp.where(iota((DEVICES, 128), 1) < 64, taken_apart(dbuf, 2, 64), 0.0)
    high, low = split(diag)
    both = jnp.concatenate([high, low], axis=1).astype(BF16)
    diag_modes[...] = jnp.dot(both, spread[...], preferred_element_type=F32) * (-SCALE)
    wait_all(9, qbuf)
    known = taken_apart(qbuf, 3, 40)
    wait_all(3, yw0)

    high, low = split(yw0[...])
    both = jnp.concatenate([high, low, jnp.zeros((64, 128), F32)], axis=0).astype(BF16)
    values = jnp.dot(onehot[...].astype(BF16), both, preferred_element_type=F32) * block[...]
    values = tile16(values)
    lanes = iota((DEVICES, 128), 1)
    near = jnp.where(lanes < 36, known, jnp.where(lanes < 52, values, 0.0))
    near = jnp.where(lanes >= 16, near, 0.0)
    mixed = jnp.where(lanes < 16, known, near)
    mixed = mixed + pltpu.roll(jnp.concatenate([near[-NW:], near[:-NW]], axis=0), 36, 1)
    mixed = mixed + pltpu.roll(jnp.concatenate([near[NW:], near[:NW]], axis=0), 72, 1)
    high, low = split(mixed)
    both = jnp.concatenate([high, low, high], axis=1).astype(BF16)
    sides = jnp.dot(both, mix[...], preferred_element_type=F32)
    wall_row = iota((DEVICES, 128), 0) % NW
    second_residual = sides[:, 0:128]
    second_residual = second_residual + jnp.where(wall_row > 0, pltpu.roll(sides[:, 128:256], 1, 0), 0.0)
    second_residual = second_residual + jnp.where(
        wall_row < NW - 1, pltpu.roll(sides[:, 256:384], DEVICES - 1, 0), 0.0
    )
    products = [part for h in range(2) for part in split(values * diag_modes[:, 128 * h : 128 * h + 128])]
    both = jnp.concatenate(products, axis=1).astype(BF16)
    at = iota((512, 128), 0)
    summed = jnp.where(8 * (at // 256) + (at % 128) // 16 == iota((512, 128), 1) % 16, 1.0, 0.0)
    second_residual = second_residual + jnp.dot(both, summed.astype(BF16), preferred_element_type=F32)
    rows[2] = jnp.broadcast_to(partial_values(second_residual, True), (8, 128))
    send_direct(2, all2)

    groups = []
    for a in (up, s, down):
        group = coefficients(0, a, w, 1)
        group = group + jnp.where(w > 0, coefficients(0, a, left, 0), 0.0)
        group = group + jnp.where(w < NW - 1, coefficients(0, a, right, 2), 0.0)
        groups.append(jnp.where((lane % 16) // 4 == sub, group, 0.0))
    py[...] = prolonged(groups, sk[...], wk[...])

    def first_at(i):
        value = first[rows_at(i), :] + py[rows_at(i), :] * (1.0 / 3.0)
        first[rows_at(i), :] = value
        return value

    def residual(i, value, total):
        res[rows_at(i), :] = inside(i, gm[rows_at(i), :] - d9[rows_at(i), :] * value + total, valid4)

    stencil_strips(first_at, residual)

    resid_copy = pltpu.make_async_copy(res.at[pl.ds(8, CX), pl.ds(0, CY)], resid_hbm, store_sem.at[0])
    resid_copy.start()
    for copy in halos:
        copy.wait_send()
    quarter = CX // 4
    base_copies = [
        pltpu.make_async_copy(
            first.at[pl.ds(8 + quarter * p, quarter), pl.ds(0, CY)],
            base_hbm.at[pl.ds(quarter * p, quarter)],
            store_sem.at[1 + p],
        )
        for p in range(4)
    ]

    def add_local(i, value):
        if 1 <= i <= CX // 8:
            first[rows_at(i), 0:CY] = (first[rows_at(i), 0:CY] + value[:, 0:CY]) * 3.0
            if i % (quarter // 8) == 0:
                base_copies[i // (quarter // 8) - 1].start()

    chebyshev(res, add_local)
    sum_direct(2, all2, yw1)
    own_row = (lane % 16) // 4 == sub
    mine_out[...] = jnp.where(own_row, coefficients(1, s, w, 1), 0.0)
    for which, part in enumerate((cw.at[pl.ds(0, NW - 1)], yw0.at[pl.ds(0, NW - 1)], None)):
        if part is None:
            wait_sent(2 * which, all2.at[pl.ds(0, DEVICES - 1)])
        else:
            wait_sent(2 * which, st.at[which, pl.ds(0, NS - 1)])
            wait_sent(2 * which + 1, part)
    wait_sent(6, dst.at[pl.ds(0, NS - 1)])
    wait_sent(7, dbuf.at[:, pl.ds(0, NW - 1), :])
    wait_sent(8, qst.at[pl.ds(0, NS - 1)])
    wait_sent(9, qbuf.at[:, pl.ds(0, NW - 1), :])
    for copy in margins:
        copy.wait_send()
    resid_copy.wait()
    for copy in base_copies:
        copy.wait()


PIECES = 2


def finish(
    base_hbm, resid_hbm, mine_hbm, stream_hbm, wall_hbm, out_hbm, resid_out,
    base, resid, mine, stream_table, wall_table, small_sem, load_sem, store_sem,
):
    small = [
        pltpu.make_async_copy(src, dst, small_sem.at[i])
        for i, (src, dst) in enumerate([(mine_hbm, mine), (wall_hbm, wall_table), (stream_hbm, stream_table)])
    ]
    for copy in small:
        copy.start()
    parts = [pl.ds(i * (CX // PIECES), CX // PIECES) for i in range(PIECES)]
    loads, stores = [], []
    for k, (src, here, dst) in enumerate(((resid_hbm, resid, resid_out), (base_hbm, base, out_hbm))):
        loads.append([pltpu.make_async_copy(src.at[p], here.at[p], load_sem.at[k, i]) for i, p in enumerate(parts)])
        stores.append([pltpu.make_async_copy(here.at[p], dst.at[p], store_sem.at[k, i]) for i, p in enumerate(parts)])
    for copy in loads[0] + loads[1]:
        copy.start()
    for copy in small:
        copy.wait()
    none = jnp.zeros((8, 128), F32)
    coarse = prolonged([none, mine[...], none], stream_table[...], wall_table[...])
    for i in range(PIECES):
        loads[0][i].wait()
        stores[0][i].start()
    for i in range(PIECES):
        rows = slice(i * (CX // PIECES), (i + 1) * (CX // PIECES))
        loads[1][i].wait()
        base[rows, :] = base[rows, :] + coarse[rows, :]
        stores[1][i].start()
    for copy in stores[0] + stores[1]:
        copy.wait()


def local(right_side, diagonal, coarse_inverse, owner_slot):
    phi_lanes, psi_rows, stream_k, own_k, wall_k = tables()
    mix_k, moment_weights, spread_k = coarse_tables()
    field = jax.ShapeDtypeStruct((CX, CY), F32)
    anywhere = pl.BlockSpec(memory_space=pl.ANY)
    in_vmem = pl.BlockSpec(memory_space=pltpu.VMEM)
    vmem = pltpu.VMEM
    dma = pltpu.SemaphoreType.DMA
    work = vmem((ROWS, COLS), F32)
    base, resid, mine = pl.pallas_call(
        kernel,
        out_shape=(field, field, jax.ShapeDtypeStruct((8, 128), F32)),
        in_specs=[anywhere] * 12,
        out_specs=(anywhere, anywhere, in_vmem),
        scratch_shapes=[
            vmem((2, ROWS, COLS), F32), work, work, work, work, work, work, work, work,
            vmem((128, 512), F32), vmem((6 * CX, 128), F32), vmem((8, CY), F32),
            vmem((ROWS, 128), BF16), vmem((256, COLS), BF16),
            vmem((384, 384), BF16), vmem((416, 128), F32), vmem((256, 256), BF16), vmem((1, DEVICES), jnp.int32),
            vmem((2, 32, 128), F32), vmem((2, 32, 128), F32), vmem((4, 2, 8, 128), F32),
            vmem((2, 16, 128), F32), vmem((2, 16, 128), F32), vmem((4, 8, 128), F32), vmem((2, 8, CY), F32),
            vmem((6, 8, 128), F32), vmem((3, NS, 128), F32), vmem((1, 1, 128), F32), vmem((NS, 1, 128), F32),
            vmem((NS, 1, 128), F32), vmem((4, 1, 128), F32), vmem((4, 1, 128), F32), vmem((NW, 128), F32), vmem((4, NW, 128), F32),
            vmem((3, NW, 128), F32), vmem((NW, 128), F32), vmem((NW, 128), F32),
            vmem((DEVICES, 128), F32),
            vmem((DEVICES, 128), F32), vmem((DEVICES, 128), F32), vmem((DEVICES, 256), F32),
            pltpu.SMEM((DEVICES,), jnp.int32),
            dma((13,)), dma((2, 8)), dma((2, 8)), dma((11,)), dma((11,)), dma((5,)),
        ],
        compiler_params=pltpu.CompilerParams(
            collective_id=0, has_side_effects=True, vmem_limit_bytes=60 * 1024 * 1024
        ),
        cost_estimate=pl.CostEstimate(flops=100_000_000, bytes_accessed=4_000_000, transcendentals=0),
    )(
        right_side, diagonal, coarse_inverse, owner_slot, owner_slot.reshape(1, DEVICES),
        phi_lanes, psi_rows, stream_k, wall_k, mix_k, moment_weights, spread_k,
    )
    return pl.pallas_call(
        finish,
        out_shape=(field, field),
        in_specs=[anywhere] * 5,
        out_specs=(anywhere, anywhere),
        scratch_shapes=[
            vmem((CX, CY), F32), vmem((CX, CY), F32), vmem((8, 128), F32), vmem((CX, 128), BF16), vmem((256, CY), BF16),
            dma((3,)), dma((2, PIECES)), dma((2, PIECES)),
        ],
        compiler_params=pltpu.CompilerParams(vmem_limit_bytes=60 * 1024 * 1024),
        cost_estimate=pl.CostEstimate(flops=50_000_000, bytes_accessed=3_000_000, transcendentals=0),
    )(base, resid, mine, own_k, np.ascontiguousarray(wall_k[:, :CY]))


def solution(mesh):
    placed = (P("stream", "wall"), P("stream", "wall"), P("wall", "stream"), P())
    return jax.shard_map(
        local,
        mesh=mesh,
        in_specs=placed,
        out_specs=(P("stream", "wall"), P("stream", "wall")),
        check_vma=False,
    )
```

```python
import math

import jax
import jax.numpy as jnp
import numpy as np
from jax import lax
from jax.experimental import pallas as pl
from jax.experimental.pallas import tpu as pltpu
from jax.sharding import PartitionSpec as P

MESH = pl.DeviceIdType.MESH
NS, NW = 8, 32
DEVICES = NS * NW
CX, CY = 256, 768
DEG = 4
ROWS, COLS = CX + 16, CY + 128
STRIPS = ROWS // 8
MIDDLE = (5.0 + 0.05) / 2.0
SPREAD = (5.0 - 0.05) / 2.0
SCALE = 1.0 / math.sqrt(CX * CY)
F32, BF16 = jnp.float32, jnp.bfloat16


def sweep_factors():
    quotient = MIDDLE / SPREAD
    factor = 1.0 / quotient
    pairs = []
    for _ in range(DEG):
        following = 1.0 / (2.0 * quotient - factor)
        pairs.append((following * factor, 2.0 * following / SPREAD))
        factor = following
    return pairs


def halves(table):
    high = table.astype(BF16)
    return high, (table - high.astype(np.float32)).astype(BF16)


def tables():
    phi = np.cos(np.pi * (np.arange(CX) + 0.5)[None, :] * np.arange(7)[:, None] / CX)
    psi = np.cos(np.pi * (np.arange(CY) + 0.5)[None, :] * np.arange(7)[:, None] / CY)
    phi_lanes = np.repeat(phi[1:].reshape(6 * CX, 1), 128, axis=1).astype(np.float32)
    psi_rows = np.concatenate([psi, psi[:1]]).astype(np.float32)
    stream = np.zeros((ROWS, 32), np.float32)
    stream[0:8, 0:4] = phi[:4, CX - 8 :].T
    stream[8 : 8 + CX, 8:12] = phi[:4].T
    stream[8 + CX :, 16:20] = phi[:4, :8].T
    high, low = halves(stream)
    stream_k = np.concatenate([high, high, low, np.zeros_like(high)], axis=1)
    own_k = stream_k[8 : 8 + CX]
    wall = np.zeros((64, COLS), np.float32)
    for m in range(4):
        wall[4 * m : 4 * m + 4, COLS - 64 :] = psi[:4, CY - 64 :]
        wall[16 + 4 * m : 20 + 4 * m, :CY] = psi[:4]
        wall[32 + 4 * m : 36 + 4 * m, CY : CY + 64] = psi[:4, :64]
    high, low = halves(wall)
    wall_k = np.concatenate([high, high, low, np.zeros_like(high)], axis=0)
    return phi_lanes, psi_rows, stream_k, own_k, wall_k


EDGES = 20


def coarse_tables():
    phi = np.cos(np.pi * (np.arange(CX) + 0.5)[None, :] * np.arange(4)[:, None] / CX)
    psi = np.cos(np.pi * (np.arange(CY) + 0.5)[None, :] * np.arange(4)[:, None] / CY)
    lam = 1.0 + 2.0 * np.cos(np.pi * np.arange(4) / CX)
    mu = 1.0 + 2.0 * np.cos(np.pi * np.arange(4) / CY)
    p0, p1, q0, q1 = phi[:, 0], phi[:, -1], psi[:, 0], psi[:, -1]
    nx, ny = (phi**2).sum(1), (psi**2).sum(1)
    near = {(a, b): np.zeros((EDGES, 4, 4)) for a in (-1, 0, 1) for b in (-1, 0, 1)}
    from_modes = np.zeros((4, 4, EDGES))
    corner = {(0, 0): 16, (0, 1): 17, (1, 0): 18, (1, 1): 19}
    ps, qs = (p0, p1), (q0, q1)
    for n in range(4):
        for side in (0, 1):
            row = 4 * side + n
            near[0, 0][row, :, n] -= mu[n] * ps[side]
            near[1 if side == 0 else -1, 0][row, :, n] += mu[n] * ps[1 - side]
            from_modes[:, n, row] += ps[side] * ny[n]
    for m in range(4):
        for side in (0, 1):
            row = 8 + 4 * side + m
            near[0, 0][row, m, :] -= lam[m] * qs[side]
            near[0, 1 if side == 0 else -1][row, m, :] += lam[m] * qs[1 - side]
            from_modes[m, :, row] += qs[side] * nx[m]
    for (i, j), row in corner.items():
        a, b = (1 if i == 0 else -1), (1 if j == 0 else -1)
        near[0, 0][row] += np.outer(ps[i], qs[j])
        near[a, 0][row] -= np.outer(ps[1 - i], qs[j])
        near[0, b][row] -= np.outer(ps[i], qs[1 - j])
        near[a, b][row] += np.outer(ps[1 - i], qs[1 - j])
        from_modes[:, :, row] += np.outer(ps[i], qs[j])
    near = {key: value.reshape(EDGES, 16) * (SCALE / 3.0) for key, value in near.items()}
    from_modes = from_modes.reshape(16, EDGES)
    smooth = np.outer(lam, mu).reshape(16) / 3.0
    norm = np.outer(nx, ny).reshape(16)
    mix = np.zeros((3, 128, 16))
    mix[0, 0:16] = np.eye(16)
    for side, b in enumerate((0, -1, 1)):
        for place, a in enumerate((0, -1, 1)):
            start = 16 + 36 * place
            values = from_modes @ near[a, b]
            if a == 0 and b == 0:
                values = values - np.diag(SCALE * (3.0 - smooth) * norm)
            mix[side, start : start + 20] = near[a, b]
            for k in range(16):
                mix[side, start + 20 + k] = values[(36 + k) % 16]
    wide = np.concatenate([np.tile(mix[i], (1, 8)) for i in range(3)], axis=1).astype(np.float32)
    high, low = halves(wide)
    mix_k = np.concatenate([high, high, low], axis=0)
    weights = np.zeros((52, 128), np.float32)
    for k in range(16):
        weights[k, k] = 3.0 * SCALE * smooth[k]
        weights[16 + k, k] = -SCALE
    for e in range(EDGES):
        weights[32 + e, 16 + e] = 3.0
    spread = np.zeros((128, 256), np.float32)
    for k in range(16):
        for j in range(16):
            m, n, mm, nn = k // 4, k % 4, j // 4, j % 4
            for p in (m + mm, abs(m - mm)):
                for q in (n + nn, abs(n - nn)):
                    spread[7 * p + q, 16 * k + j] += 0.25
    return mix_k, np.repeat(weights, 8, axis=0), np.concatenate([spread, spread]).astype(BF16)


def iota(shape, dim):
    return lax.broadcasted_iota(jnp.int32, shape, dim)


def split(value):
    high = value.astype(BF16).astype(F32)
    return high, value - high


def lane_totals(value):
    high, low = split(value)
    both = jnp.concatenate([high, low], axis=1).astype(BF16)
    return jnp.dot(both, jnp.ones((256, 128), BF16), preferred_element_type=F32)


def prolonged(groups, stream_table, wall_table):
    stacked = jnp.concatenate(groups + [jnp.zeros((8, 128), F32)], axis=0)
    high, low = split(stacked)
    operand = jnp.concatenate([high + pltpu.roll(low, 64, 1), high], axis=1).astype(BF16)
    mixed = jnp.dot(operand, wall_table, preferred_element_type=F32)
    high, low = split(mixed)
    operand = jnp.concatenate([high, low, high, jnp.zeros_like(high)], axis=0).astype(BF16)
    return jnp.dot(stream_table, operand, preferred_element_type=F32)


def tile16(value):
    alike = jnp.where(iota((256, 128), 0) % 16 == iota((256, 128), 1) % 16, 1.0, 0.0).astype(BF16)
    high, low = split(value)
    both = jnp.concatenate([high, low], axis=1).astype(BF16)
    return jnp.dot(both, alike, preferred_element_type=F32)


def strip(i):
    return pl.ds(pl.multiple_of(i * 8, 8), 8)


def kernel(
    rhs_hbm, diag_hbm, inv_hbm, slot_hbm, slots_hbm, phi_hbm, psi_hbm, sk_hbm, wk_hbm, mix_hbm, weights_hbm, spread_hbm,
    base_hbm, resid_hbm, mine_out,
    ext, gm, d9, x, x2, u, first, res, py, inv, phi, psi, sk, wk, mix, weights, spread, slots,
    colsend, colrecv, corners, hcolsend, hcolrecv, hcorners, hrows,
    rows, st, drow, dst, qst, qpack, dpack, cw, dbuf, qbuf, yw0, yw1, all2, onehot, block, diag_modes, slot,
    load_sem, msend, mrecv, asend, arecv, store_sem,
):
    s = lax.axis_index("stream")
    w = lax.axis_index("wall")
    me = s * NW + w
    ya, xl = s % 4, s // 4
    xh, za, core = w // 16, (w // 2) % 8, w % 2
    xa = xh * 2 + xl
    up, down = (s + NS - 1) % NS, (s + 1) % NS
    left, right = (w + NW - 1) % NW, (w + 1) % NW

    def around(k, n):
        return n // 2 + (k % 2) * ((k + 1) // 2) - (1 - k % 2) * (k // 2)

    def everyone(act):
        xa = xh * 2 + xl
        ys = [(ya + d) % 4 for d in (2, 3, 1, 0)]

        def some(k, count):
            z = (za + around(k // 4, 8)) % 8
            xx = (xa + around(k % 4, 4)) % 4
            base_s = (xx % 2) * 4
            base_w = (xx // 2) * 16 + z * 2
            for j in range(count):
                act((base_s + ys[j // 2], base_w + ((1 - core) if j % 2 == 0 else core)))

        def body(k, carry):
            some(k, 8)
            return carry

        lax.fori_loop(0, 31, body, 0)
        some(jnp.int32(31), 7)

    def stream_mates(act):
        for d in (2, 3, 1, 0):
            for flip in (1, 0):
                if d or flip:
                    act(((xl if flip == 0 else 1 - xl) * 4 + (ya + d) % 4, w))

    def wall_mates(act):
        for d in (4, 5, 3, 6, 2, 7, 1, 0):
            for flip in (1, 0):
                for other in (1, 0):
                    if d or flip or other:
                        x_part = (xh if flip == 0 else 1 - xh) * 16
                        act((s, x_part + ((za + d) % 8) * 2 + (core if other == 0 else 1 - core)))

    barrier = pltpu.get_barrier_semaphore()

    def greet(to):
        pl.semaphore_signal(barrier, inc=1, device_id=to, device_id_type=MESH)

    wall_mates(greet)
    stream_mates(greet)
    for to in [(up, left), (up, right), (down, left), (down, right)]:
        greet(to)

    own = ext.at[:, pl.ds(8, CX), pl.ds(0, CY)]
    loads = [
        pltpu.make_async_copy(src, dst, load_sem.at[i])
        for i, (src, dst) in enumerate(
            [
                (rhs_hbm, own.at[0]),
                (phi_hbm.at[pl.ds(0, 3 * CX)], phi.at[pl.ds(0, 3 * CX)]),
                (psi_hbm, psi),
                (diag_hbm, own.at[1]),
                (phi_hbm.at[pl.ds(3 * CX, 3 * CX)], phi.at[pl.ds(3 * CX, 3 * CX)]),
                (slot_hbm, slot),
                (slots_hbm, slots),
                (inv_hbm, inv),
                (sk_hbm, sk),
                (wk_hbm, wk),
                (mix_hbm, mix),
                (weights_hbm, weights),
                (spread_hbm, spread),
            ]
        )
    ]
    for load in loads:
        load.start()

    lane = iota((8, 128), 1)
    sub = iota((8, 128), 0)
    lane16 = iota((16, 128), 1)
    lane1 = iota((1, 128), 1)

    def mode_sums(load, count):
        def body(step, sums):
            sums = list(sums)
            for i in range(4):
                f = load(step * 4 + i)
                sums[0] = sums[0] + f
                for m in range(count - 1):
                    t = phi[pl.ds(pl.multiple_of(m * CX + (step * 4 + i) * 8, 8), 8), :]
                    sums[m + 1] = sums[m + 1] + f * jnp.concatenate([t] * 6, axis=1)
            return tuple(sums)

        return lax.fori_loop(0, CX // 32, body, (jnp.zeros((8, CY), F32),) * count)

    def fold(value):
        total = value[:, 0:128]
        for t in range(1, 6):
            total = total + value[:, 128 * t : 128 * t + 128]
        return total

    def mode_parts(sums, count):
        return [fold(v if n == 0 else v * psi[n : n + 1, :]) for v in sums for n in range(count)]

    def gathered(parts, period):
        totals = lane_totals(jnp.concatenate(parts, axis=0))
        shape = totals.shape
        keep = iota(shape, 0) // 8 == iota(shape, 1) % period
        return jnp.sum(jnp.where(keep, totals, 0.0), axis=0, keepdims=True)

    def pack(ref):
        to_left = jnp.zeros((16, 128), F32)
        to_right = jnp.zeros((16, 128), F32)
        for k in range(16):
            a = jnp.where(lane16 < 8, ref[8 + 16 * k : 24 + 16 * k, 0:128], 0.0)
            b = jnp.where(lane16 >= 120, ref[8 + 16 * k : 24 + 16 * k, CY - 128 : CY], 0.0)
            to_left = to_left + (pltpu.roll(a, 8 * k, 1) if k else a)
            shift = (8 * k + 8) % 128
            to_right = to_right + (pltpu.roll(b, shift, 1) if shift else b)
        return to_left, to_right

    def unpack(from_right, from_left, k):
        a = pltpu.roll(from_right, 128 - 8 * k, 1) if k else from_right
        shift = (120 - 8 * k) % 128
        b = pltpu.roll(from_left, shift, 1) if shift else from_left
        return jnp.where(lane16 < 8, a, jnp.where(lane16 >= 120, b, 0.0))

    def corner(from_right, from_left):
        return jnp.where(lane < 8, from_right, jnp.where(lane >= 120, from_left, 0.0))

    def to_neighbours(which, pairs):
        targets = [(up, w), (down, w), (s, left), (s, right), (up, left), (up, right), (down, left), (down, right)]
        return [
            pltpu.make_async_remote_copy(
                src_ref=src, dst_ref=dst, send_sem=msend.at[which, i], recv_sem=mrecv.at[which, i],
                device_id=to, device_id_type=MESH,
            )
            for i, ((src, dst), to) in enumerate(zip(pairs, targets, strict=True))
        ]

    def sender(index, src, dst):
        def act(to):
            pltpu.make_async_remote_copy(
                src_ref=src, dst_ref=dst, send_sem=asend.at[index], recv_sem=arecv.at[index],
                device_id=to, device_id_type=MESH,
            ).start()

        return act

    def send(index, mates, src, dst):
        mates(sender(index, src, dst))
        pltpu.make_async_copy(src, dst, arecv.at[index]).start()

    def send_direct(which, buf):
        send(2 * which, everyone, rows.at[which, pl.ds(0, 1)], buf.at[pl.ds(s * NW + w, 1)])

    def sum_direct(which, buf, total_ref):
        wait_all(2 * which, buf)
        total = buf[0:NW]
        for a in range(1, NS):
            total = total + buf[NW * a : NW * a + NW]
        total_ref[...] = total

    def send_row(which):
        send(2 * which, stream_mates, rows.at[which, pl.ds(0, 1)], st.at[which, pl.ds(s, 1)])

    def forward_row(which, mates, dst):
        wait_all(2 * which, st.at[which])
        total = jnp.sum(st[which], axis=0, keepdims=True)
        rows[3 + which] = jnp.broadcast_to(total, (8, 128))
        send(2 * which + 1, mates, rows.at[3 + which, pl.ds(0, 1)], dst)

    def side_by_side(buf, per, width, used, r):
        total = jnp.zeros((1, 128), F32)
        for a in range(per * r, min(per * r + per, NS)):
            value = jnp.broadcast_to(jnp.where(lane1 < used, buf[a], 0.0), (8, 128))
            total = total + (pltpu.roll(value, width * (a % per), 1) if a % per else value)[0:1]
        return total

    def taken_apart(buf, per, width):
        parts = []
        for a in range(NS):
            value = buf[a // per]
            parts.append(pltpu.roll(value, 128 - width * (a % per), 1) if a % per else value)
        return jnp.concatenate(parts, axis=0)

    def wait_all(index, buf):
        pltpu.make_async_copy(buf, buf, arecv.at[index]).wait()

    def wait_sent(index, part):
        pltpu.make_async_copy(part, part, asend.at[index]).wait()

    def partial_values(c, tiled):
        at = iota((32, DEVICES), 0) + 32 * s
        pick = jnp.where(slots[...] == at, 1.0, 0.0)
        high, low = split(c)
        pick2 = jnp.concatenate([pick, pick], axis=1).astype(BF16)
        both = jnp.concatenate([high, low], axis=0).astype(BF16)
        ordered = jnp.dot(pick2, both, preferred_element_type=F32)
        if not tiled:
            ordered = tile16(ordered)
        keep = iota((32, 128), 1) // 16 == iota((32, 128), 0) % 8
        ordered = jnp.where(keep, ordered, 0.0)
        total = jnp.zeros((128, 128), F32)
        for q in range(4):
            row = jnp.sum(ordered[8 * q : 8 * q + 8], axis=0, keepdims=True)
            total = total + inv[:, 128 * q : 128 * q + 128] * row
        sums = lane_totals(total)
        return jnp.sum(jnp.where(iota((128, 128), 0) == iota((128, 128), 1), sums, 0.0), axis=0, keepdims=True)

    def coefficients(which, a, b, place):
        mine = slot[a * NW + b]
        row = (yw1 if which else yw0)[pl.ds(lax.shift_right_logical(mine, 3), 1), :]
        shift = lax.bitwise_and(16 * place + 128 - 16 * lax.bitwise_and(mine, 7), 127)
        rolled = pltpu.roll(jnp.broadcast_to(row, (8, 128)), shift, 1)
        return jnp.where(lane // 16 == place, rolled, 0.0)

    tail_lane = iota((8, 128), 1)

    def tail_valid(depth):
        inner = jnp.logical_and(tail_lane < depth, w < NW - 1)
        outer = jnp.logical_and(tail_lane >= 128 - depth, w > 0)
        return jnp.logical_or(inner, outer)

    def masked(value, valid):
        return jnp.concatenate([value[:, 0:CY], jnp.where(valid, value[:, CY:], 0.0)], axis=1)

    wide_sub = iota((8, COLS), 0)

    def hsum(v):
        return v + pltpu.roll(v, 1, 1) + pltpu.roll(v, COLS - 1, 1)

    def vsum(before, here, after):
        above = pltpu.roll(jnp.where(wide_sub == 7, before, here), 1, 0)
        below = pltpu.roll(jnp.where(wide_sub == 0, after, here), 7, 0)
        return here + above + below

    def rows_at(i):
        return slice(8 * i, 8 * i + 8)

    def stencil_strips(load, use):
        zero = jnp.zeros((8, COLS), F32)
        value = load(0)
        before, now = zero, hsum(value)
        for i in range(STRIPS):
            following = load(i + 1) if i + 1 < STRIPS else None
            after = zero if following is None else hsum(following)
            use(i, value, vsum(before, now, after))
            before, now, value = now, after, following

    def inside(i, value, valid):
        value = masked(value, valid)
        if i == 0:
            return jnp.where(wide_sub >= 4, value, 0.0)
        if i == STRIPS - 1:
            return jnp.where(wide_sub < 4, value, 0.0)
        return value

    def chebyshev(g):
        valid = tail_valid(4)
        old, new = x, x2
        for k, (a, b) in enumerate(sweep_factors()):

            def load(i, k=k, old=old):
                return g[rows_at(i), :] * (1.0 / (3.0 * MIDDLE)) if k == 0 else old[rows_at(i), :]

            def use(i, value, total, k=k, a=a, b=b, new=new):
                e = g[rows_at(i), :] - d9[rows_at(i), :] * value + total
                step = a * (value if k == 0 else u[rows_at(i), :]) + (b / 3.0) * e
                step = inside(i, step, valid)
                if k < DEG - 1:
                    u[rows_at(i), :] = step
                new[rows_at(i), :] = value + step

            stencil_strips(load, use)
            old, new = new, old

    for load in loads[:3]:
        load.wait()
    sums = mode_sums(lambda i: ext[0, strip(i + 1), 0:CY], 4)
    first_residual = gathered(mode_parts(sums, 4), 16) * SCALE
    rows[0] = jnp.broadcast_to(jnp.where(lane1 // 16 == s, first_residual, 0.0), (8, 128))
    loads[3].wait()
    for f in range(2):
        a, b = pack(ext.at[f])
        colsend[0, 16 * f : 16 * f + 16] = a
        colsend[1, 16 * f : 16 * f + 16] = b

    pl.semaphore_wait(barrier, 7 + 31 + 4)
    top, bottom = pl.ds(8, 8), pl.ds(CX, 8)
    west, east, body_lanes = pl.ds(0, 128), pl.ds(CY - 128, 128), pl.ds(0, CY)
    margins = to_neighbours(
        0,
        [
            (ext.at[:, top, body_lanes], ext.at[:, pl.ds(ROWS - 8, 8), body_lanes]),
            (ext.at[:, bottom, body_lanes], ext.at[:, pl.ds(0, 8), body_lanes]),
            (colsend.at[0], colrecv.at[0]),
            (colsend.at[1], colrecv.at[1]),
            (ext.at[:, top, west], corners.at[3]),
            (ext.at[:, top, east], corners.at[2]),
            (ext.at[:, bottom, west], corners.at[1]),
            (ext.at[:, bottom, east], corners.at[0]),
        ],
    )
    send_row(0)
    for copy in margins:
        copy.start()
    loads[4].wait()
    sums = mode_sums(lambda i: ext[1, strip(i + 1), 0:CY], 7)
    drow[0] = gathered(mode_parts(sums, 7), 128)
    send(6, stream_mates, drow, dst.at[pl.ds(s, 1)])
    for load in loads[5:]:
        load.wait()
    at = iota((128, DEVICES), 0)
    group_of = lax.shift_right_logical(slots[...], 3)
    onehot[...] = jnp.where(jnp.logical_and(group_of == at % 32, at < 64), 1.0, 0.0).T
    block[...] = jnp.where(lax.bitwise_and(slots[...], 7) == at // 16, 1.0, 0.0).T

    def own_part(i, carry):
        gm[strip(i), 0:CY] = ext[0, strip(i), 0:CY]
        d9[strip(i), 0:CY] = ext[1, strip(i), 0:CY] * 3.0 + 9.0
        return carry

    lax.fori_loop(1, STRIPS - 1, own_part, 0, unroll=True)
    forward_row(0, wall_mates, cw.at[pl.ds(w, 1)])
    for copy in margins:
        copy.wait_recv()

    valid4 = tail_valid(4)
    two_strips = jnp.concatenate([valid4, valid4], axis=0)
    for k in range(16):
        here = slice(8 + 16 * k, 24 + 16 * k)
        gm[here, CY:COLS] = jnp.where(two_strips, unpack(colrecv[0, 0:16], colrecv[1, 0:16], k), 0.0)
        d9[here, CY:COLS] = unpack(colrecv[0, 16:32], colrecv[1, 16:32], k) * 3.0 + 9.0
    for i, keep, right_at in ((0, sub >= 4, 1), (STRIPS - 1, sub < 4, 3)):
        here = rows_at(i)
        wide_keep = wide_sub[:, 0:CY] >= 4 if i == 0 else wide_sub[:, 0:CY] < 4
        gm[here, 0:CY] = jnp.where(wide_keep, ext[0, here, 0:CY], 0.0)
        d9[here, 0:CY] = ext[1, here, 0:CY] * 3.0 + 9.0
        tail = corner(corners[right_at, 0], corners[right_at - 1, 0])
        gm[here, CY:COLS] = jnp.where(jnp.logical_and(valid4, keep), tail, 0.0)
        d9[here, CY:COLS] = corner(corners[right_at, 1], corners[right_at - 1, 1]) * 3.0 + 9.0
    chebyshev(gm)

    def moment_body(step, sums):
        sums = list(sums)
        for k in range(2):
            i = step * 2 + k
            value = x[strip(i + 1), 0:CY]
            weighted = value * d9[strip(i + 1), 0:CY]
            sums[0], sums[4] = sums[0] + value, sums[4] + weighted
            for m in range(1, 4):
                t = phi[pl.ds(pl.multiple_of((m - 1) * CX + i * 8, 8), 8), :]
                t = jnp.concatenate([t] * 6, axis=1)
                sums[m], sums[4 + m] = sums[m] + value * t, sums[4 + m] + weighted * t
        return tuple(sums)

    sums = lax.fori_loop(0, CX // 16, moment_body, (jnp.zeros((8, CY), F32),) * 8)
    u_sums, w_sums = sums[:4], sums[4:]
    parts = mode_parts(u_sums, 4) + mode_parts(w_sums, 4)
    for edge, here in ((x[8:16, 0:CY], sub == 0), (x[CX : CX + 8, 0:CY], sub == 7)):
        parts += [jnp.where(here, p, 0.0) for p in mode_parts([edge], 4)]
    parts += [jnp.where(lane == 0, v[:, 0:128], 0.0) for v in u_sums]
    parts += [jnp.where(lane == 127, v[:, CY - 128 : CY], 0.0) for v in u_sums]
    for edge, at_row in ((x[8:16, :], 0), (x[CX : CX + 8, :], 7)):
        for tile, at_lane in ((edge[:, 0:128], 0), (edge[:, CY - 128 : CY], 127)):
            parts.append(jnp.where(jnp.logical_and(sub == at_row, lane == at_lane), tile, 0.0))
    totals = lane_totals(jnp.concatenate(parts, axis=0)) * weights[...]
    moments = jnp.sum(totals, axis=0, keepdims=True)
    moments = moments + jnp.where(lane1 < 16, first_residual, 0.0)
    qpack[3] = moments
    send(8, stream_mates, qpack.at[pl.ds(3, 1)], qst.at[pl.ds(s, 1)])

    wait_all(1, cw)
    spread_rows = jnp.concatenate([cw[...]] * NS, axis=0)
    own_lanes = iota((DEVICES, 128), 1) // 16 == iota((DEVICES, 128), 0) // NW
    rows[1] = jnp.broadcast_to(partial_values(jnp.where(own_lanes, spread_rows, 0.0), False), (8, 128))
    send_row(1)
    wait_all(6, dst)
    for r in range(4):
        dpack[r] = side_by_side(dst, 2, 64, 49, r)
    send(7, wall_mates, dpack, dbuf.at[:, pl.ds(w, 1), :])

    a, b = pack(x)
    hcolsend[0] = a
    hcolsend[1] = b
    halos = to_neighbours(
        1,
        [
            (x.at[top, body_lanes], hrows.at[1]),
            (x.at[bottom, body_lanes], hrows.at[0]),
            (hcolsend.at[0], hcolrecv.at[0]),
            (hcolsend.at[1], hcolrecv.at[1]),
            (x.at[top, west], hcorners.at[3]),
            (x.at[top, east], hcorners.at[2]),
            (x.at[bottom, west], hcorners.at[1]),
            (x.at[bottom, east], hcorners.at[0]),
        ],
    )
    for copy in halos:
        copy.start()

    wait_all(8, qst)
    for r in range(3):
        qpack[r] = side_by_side(qst, 3, 40, 36, r)
    send(9, wall_mates, qpack.at[pl.ds(0, 3)], qbuf.at[:, pl.ds(w, 1), :])
    forward_row(1, wall_mates, yw0.at[pl.ds(w, 1)])

    for copy in halos:
        copy.wait_recv()
    valid8 = tail_valid(8)

    def place(i, carry):
        first[strip(i), 0:CY] = x[strip(i), 0:CY]
        return carry

    lax.fori_loop(1, STRIPS - 1, place, 0, unroll=True)
    first[0:8, 0:CY] = hrows[0]
    first[ROWS - 8 : ROWS, 0:CY] = hrows[1]
    for k in range(16):
        edge = unpack(hcolrecv[0], hcolrecv[1], k)
        first[8 + 16 * k : 16 + 16 * k, CY:COLS] = jnp.where(valid8, edge[0:8], 0.0)
        first[16 + 16 * k : 24 + 16 * k, CY:COLS] = jnp.where(valid8, edge[8:16], 0.0)
    first[0:8, CY:COLS] = jnp.where(valid8, corner(hcorners[1], hcorners[0]), 0.0)
    first[ROWS - 8 : ROWS, CY:COLS] = jnp.where(valid8, corner(hcorners[3], hcorners[2]), 0.0)

    wait_all(7, dbuf)
    diag = jnp.where(iota((DEVICES, 128), 1) < 64, taken_apart(dbuf, 2, 64), 0.0)
    high, low = split(diag)
    both = jnp.concatenate([high, low], axis=1).astype(BF16)
    diag_modes[...] = jnp.dot(both, spread[...], preferred_element_type=F32) * (-SCALE)
    wait_all(3, yw0)

    high, low = split(yw0[...])
    both = jnp.concatenate([high, low, jnp.zeros((64, 128), F32)], axis=0).astype(BF16)
    values = jnp.dot(onehot[...].astype(BF16), both, preferred_element_type=F32) * block[...]
    values = tile16(values)
    products = [part for h in range(2) for part in split(values * diag_modes[:, 128 * h : 128 * h + 128])]
    both = jnp.concatenate(products, axis=1).astype(BF16)
    at = iota((512, 128), 0)
    summed = jnp.where(8 * (at // 256) + (at % 128) // 16 == iota((512, 128), 1) % 16, 1.0, 0.0)
    from_diagonal = jnp.dot(both, summed.astype(BF16), preferred_element_type=F32)
    wait_all(9, qbuf)
    known = taken_apart(qbuf, 3, 40)
    lanes = iota((DEVICES, 128), 1)
    near = jnp.where(lanes < 36, known, jnp.where(lanes < 52, values, 0.0))
    near = jnp.where(lanes >= 16, near, 0.0)
    mixed = jnp.where(lanes < 16, known, near)
    mixed = mixed + pltpu.roll(jnp.concatenate([near[-NW:], near[:-NW]], axis=0), 36, 1)
    mixed = mixed + pltpu.roll(jnp.concatenate([near[NW:], near[:NW]], axis=0), 72, 1)
    high, low = split(mixed)
    both = jnp.concatenate([high, low, high], axis=1).astype(BF16)
    sides = jnp.dot(both, mix[...], preferred_element_type=F32)
    wall_row = iota((DEVICES, 128), 0) % NW
    second_residual = from_diagonal + sides[:, 0:128]
    second_residual = second_residual + jnp.where(wall_row > 0, pltpu.roll(sides[:, 128:256], 1, 0), 0.0)
    second_residual = second_residual + jnp.where(
        wall_row < NW - 1, pltpu.roll(sides[:, 256:384], DEVICES - 1, 0), 0.0
    )
    rows[2] = jnp.broadcast_to(partial_values(second_residual, True), (8, 128))
    send_direct(2, all2)

    groups = []
    for a in (up, s, down):
        group = coefficients(0, a, w, 1)
        group = group + jnp.where(w > 0, coefficients(0, a, left, 0), 0.0)
        group = group + jnp.where(w < NW - 1, coefficients(0, a, right, 2), 0.0)
        groups.append(jnp.where((lane % 16) // 4 == sub, group, 0.0))
    py[...] = prolonged(groups, sk[...], wk[...])

    def first_at(i):
        value = first[rows_at(i), :] + py[rows_at(i), :] * (1.0 / 3.0)
        first[rows_at(i), :] = value
        return value

    def residual(i, value, total):
        res[rows_at(i), :] = inside(i, gm[rows_at(i), :] - d9[rows_at(i), :] * value + total, valid4)

    stencil_strips(first_at, residual)

    resid_copy = pltpu.make_async_copy(res.at[pl.ds(8, CX), pl.ds(0, CY)], resid_hbm, store_sem.at[0])
    resid_copy.start()
    for copy in halos:
        copy.wait_send()
    chebyshev(res)

    def add_local(i, carry):
        first[strip(i), 0:CY] = (first[strip(i), 0:CY] + x[strip(i), 0:CY]) * 3.0
        return carry

    lax.fori_loop(1, STRIPS - 1, add_local, 0, unroll=True)
    base_copy = pltpu.make_async_copy(first.at[pl.ds(8, CX), pl.ds(0, CY)], base_hbm, store_sem.at[1])
    base_copy.start()
    sum_direct(2, all2, yw1)
    own_row = (lane % 16) // 4 == sub
    mine_out[...] = jnp.where(own_row, coefficients(1, s, w, 1), 0.0)
    for which, part in enumerate((cw.at[pl.ds(0, NW - 1)], yw0.at[pl.ds(0, NW - 1)], None)):
        if part is None:
            wait_sent(2 * which, all2.at[pl.ds(0, DEVICES - 1)])
        else:
            wait_sent(2 * which, st.at[which, pl.ds(0, NS - 1)])
            wait_sent(2 * which + 1, part)
    wait_sent(6, dst.at[pl.ds(0, NS - 1)])
    wait_sent(7, dbuf.at[:, pl.ds(0, NW - 1), :])
    wait_sent(8, qst.at[pl.ds(0, NS - 1)])
    wait_sent(9, qbuf.at[:, pl.ds(0, NW - 1), :])
    for copy in margins:
        copy.wait_send()
    resid_copy.wait()
    base_copy.wait()


PIECES = 2


def finish(
    base_hbm, resid_hbm, mine_hbm, stream_hbm, wall_hbm, out_hbm, resid_out,
    base, resid, mine, stream_table, wall_table, small_sem, load_sem, store_sem,
):
    small = [
        pltpu.make_async_copy(src, dst, small_sem.at[i])
        for i, (src, dst) in enumerate([(mine_hbm, mine), (wall_hbm, wall_table), (stream_hbm, stream_table)])
    ]
    for copy in small:
        copy.start()
    parts = [pl.ds(i * (CX // PIECES), CX // PIECES) for i in range(PIECES)]
    loads, stores = [], []
    for k, (src, here, dst) in enumerate(((resid_hbm, resid, resid_out), (base_hbm, base, out_hbm))):
        loads.append([pltpu.make_async_copy(src.at[p], here.at[p], load_sem.at[k, i]) for i, p in enumerate(parts)])
        stores.append([pltpu.make_async_copy(here.at[p], dst.at[p], store_sem.at[k, i]) for i, p in enumerate(parts)])
    for copy in loads[0] + loads[1]:
        copy.start()
    for copy in small:
        copy.wait()
    none = jnp.zeros((8, 128), F32)
    coarse = prolonged([none, mine[...], none], stream_table[...], wall_table[...])
    for i in range(PIECES):
        loads[0][i].wait()
        stores[0][i].start()
    for i in range(PIECES):
        rows = slice(i * (CX // PIECES), (i + 1) * (CX // PIECES))
        loads[1][i].wait()
        base[rows, :] = base[rows, :] + coarse[rows, :]
        stores[1][i].start()
    for copy in stores[0] + stores[1]:
        copy.wait()


def local(right_side, diagonal, coarse_inverse, owner_slot):
    phi_lanes, psi_rows, stream_k, own_k, wall_k = tables()
    mix_k, moment_weights, spread_k = coarse_tables()
    field = jax.ShapeDtypeStruct((CX, CY), F32)
    anywhere = pl.BlockSpec(memory_space=pl.ANY)
    in_vmem = pl.BlockSpec(memory_space=pltpu.VMEM)
    vmem = pltpu.VMEM
    dma = pltpu.SemaphoreType.DMA
    work = vmem((ROWS, COLS), F32)
    base, resid, mine = pl.pallas_call(
        kernel,
        out_shape=(field, field, jax.ShapeDtypeStruct((8, 128), F32)),
        in_specs=[anywhere] * 12,
        out_specs=(anywhere, anywhere, in_vmem),
        scratch_shapes=[
            vmem((2, ROWS, COLS), F32), work, work, work, work, work, work, work, work,
            vmem((128, 512), F32), vmem((6 * CX, 128), F32), vmem((8, CY), F32),
            vmem((ROWS, 128), BF16), vmem((256, COLS), BF16),
            vmem((384, 384), BF16), vmem((416, 128), F32), vmem((256, 256), BF16), vmem((1, DEVICES), jnp.int32),
            vmem((2, 32, 128), F32), vmem((2, 32, 128), F32), vmem((4, 2, 8, 128), F32),
            vmem((2, 16, 128), F32), vmem((2, 16, 128), F32), vmem((4, 8, 128), F32), vmem((2, 8, CY), F32),
            vmem((6, 8, 128), F32), vmem((3, NS, 128), F32), vmem((1, 1, 128), F32), vmem((NS, 1, 128), F32),
            vmem((NS, 1, 128), F32), vmem((4, 1, 128), F32), vmem((4, 1, 128), F32), vmem((NW, 128), F32), vmem((4, NW, 128), F32),
            vmem((3, NW, 128), F32), vmem((NW, 128), F32), vmem((NW, 128), F32),
            vmem((DEVICES, 128), F32),
            vmem((DEVICES, 128), F32), vmem((DEVICES, 128), F32), vmem((DEVICES, 256), F32),
            pltpu.SMEM((DEVICES,), jnp.int32),
            dma((13,)), dma((2, 8)), dma((2, 8)), dma((11,)), dma((11,)), dma((2,)),
        ],
        compiler_params=pltpu.CompilerParams(
            collective_id=0, has_side_effects=True, vmem_limit_bytes=60 * 1024 * 1024
        ),
        cost_estimate=pl.CostEstimate(flops=100_000_000, bytes_accessed=4_000_000, transcendentals=0),
    )(
        right_side, diagonal, coarse_inverse, owner_slot, owner_slot.reshape(1, DEVICES),
        phi_lanes, psi_rows, stream_k, wall_k, mix_k, moment_weights, spread_k,
    )
    return pl.pallas_call(
        finish,
        out_shape=(field, field),
        in_specs=[anywhere] * 5,
        out_specs=(anywhere, anywhere),
        scratch_shapes=[
            vmem((CX, CY), F32), vmem((CX, CY), F32), vmem((8, 128), F32), vmem((CX, 128), BF16), vmem((256, CY), BF16),
            dma((3,)), dma((2, PIECES)), dma((2, PIECES)),
        ],
        compiler_params=pltpu.CompilerParams(vmem_limit_bytes=60 * 1024 * 1024),
        cost_estimate=pl.CostEstimate(flops=50_000_000, bytes_accessed=3_000_000, transcendentals=0),
    )(base, resid, mine, own_k, np.ascontiguousarray(wall_k[:, :CY]))


def solution(mesh):
    placed = (P("stream", "wall"), P("stream", "wall"), P("wall", "stream"), P())
    return jax.shard_map(
        local,
        mesh=mesh,
        in_specs=placed,
        out_specs=(P("stream", "wall"), P("stream", "wall")),
        check_vma=False,
    )
```
